32 devices in a mesh: seq: 4 (over x, core), head: 8 (over z, y).
Axes of the slice: x: 2, y: 2, z: 4, core: 2. Of those that a mesh axis runs over, the one named last changes fastest.
Arguments:
- query_heads: bfloat16 [512, 16, 128], P(('seq', 'head')), may hold values from -6 to 6
- key_heads: bfloat16 [512, 16, 128], P(('seq', 'head')), may hold values from -6 to 6
- value_heads: bfloat16 [512, 32, 128], P(('seq', 'head')), may hold values from -6 to 6
- gate_log: bfloat16 [512, 32], P(('seq', 'head')), may hold values from -1 to 0
- beta_rate: bfloat16 [512, 32], P(('seq', 'head')), may hold values from 0.0099487305 to 0.099609375
Outputs:
- head_output: bfloat16 [512, 4096], P(('seq', 'head'))
- block_states: float32 [4, 32, 128, 128], P('seq', 'head')
The draws below stay inside these ranges and needn't reach their ends.
All inputs are finite; a program needn't handle non-finite values.
Results may differ from the reference program's by a relative error of at most 0.001.
Values may be sent and summed in bfloat16 or wider, within the bound.
A program may use at most 64 MiB of HBM per device.

```python
import jax
import jax.numpy as jnp
from jax import lax

VALUE_HEAD_COUNT = 32
HK = 16
DK = 128
DV = 128
STRETCH = 64
SLAB = 128
PROMPT_TOKENS = 512
N_SEQ = 4


def draw_gate_log(key, part):
    random_subkeys = jax.random.split(key, 7)
    fast_share = 0.5
    fast_head = jax.random.uniform(random_subkeys[0], (VALUE_HEAD_COUNT,)) < fast_share
    fast_rate = jnp.exp(jax.random.uniform(random_subkeys[1], (VALUE_HEAD_COUNT,), minval=jnp.log(1.0 / 50.0), maxval=jnp.log(1.0 / 30.0)))
    slow_rate = jax.random.uniform(random_subkeys[2], (VALUE_HEAD_COUNT,), minval=0.2, maxval=0.8) / PROMPT_TOKENS
    base_rate = jnp.where(fast_head, fast_rate, slow_rate)
    slab_factor = jnp.exp(jax.random.uniform(random_subkeys[3], (PROMPT_TOKENS // SLAB, 1, VALUE_HEAD_COUNT), minval=-0.7, maxval=0.7))
    token_factor = jnp.exp(jax.random.uniform(random_subkeys[4], (PROMPT_TOKENS // SLAB, SLAB, VALUE_HEAD_COUNT), minval=-0.5, maxval=0.5))
    decay_factor = (base_rate * slab_factor * token_factor).reshape(PROMPT_TOKENS, VALUE_HEAD_COUNT)
    doubling_reached = jax.random.uniform(random_subkeys[5], (PROMPT_TOKENS, VALUE_HEAD_COUNT)) < 2.0 / PROMPT_TOKENS
    doubling_depth = jax.random.uniform(random_subkeys[6], (PROMPT_TOKENS, VALUE_HEAD_COUNT), minval=jnp.log(0.5), maxval=jnp.log(0.8))
    return (jnp.where(doubling_reached, doubling_depth, 0.0) - decay_factor).astype(jnp.bfloat16)


def shard_levels(key, shape, cuts, low, top_value):
    level = 1.0
    for position, parts in cuts:
        heights = jax.random.uniform(jax.random.fold_in(jax.random.fold_in(key, 6), position), (parts,), jnp.float32, low / len(cuts), top_value / len(cuts))
        level = level * jnp.repeat(jnp.exp(heights), shape[position] // parts).reshape((-1,) + (1,) * (len(shape) - 1 - position))
    return level


def normal_values(stream_key, shape, deviation, limit, cuts=(), kind=jnp.bfloat16):
    array = jax.random.normal(stream_key, shape, jnp.float32) * deviation
    if len(cuts) > 0:
        array = shard_levels(stream_key, shape, cuts, -0.22, 0.18) * array
    return jnp.clip(array, min=-limit, max=limit).astype(kind)


def setup_inputs(seed: int = 0) -> dict:
    key_of = jax.random.split(jax.random.key(seed), 6)
    query_heads = normal_values(key_of[0], (PROMPT_TOKENS, HK, DK), 1.0, 6.0, ((0, 32),))
    key_heads = normal_values(key_of[1], (PROMPT_TOKENS, HK, DK), 1.0, 6.0, ((0, 32),))
    value_heads = normal_values(key_of[2], (PROMPT_TOKENS, VALUE_HEAD_COUNT, DV), 1.0, 6.0, ((0, 32),))
    gate_log = draw_gate_log(jax.random.fold_in(key_of[5], 71), 0)
    beta_rate = jnp.clip(0.0099487305 + 0.089660645 * jax.random.uniform(key_of[4], (PROMPT_TOKENS, VALUE_HEAD_COUNT), jnp.float32) ** shard_levels(key_of[4], (PROMPT_TOKENS, VALUE_HEAD_COUNT), ((0, 32),), -0.2, 0.2), 0.0099487305, 0.099609375).astype(jnp.bfloat16)
    return {"query_heads": query_heads, "key_heads": key_heads, "value_heads": value_heads, "gate_log": gate_log, "beta_rate": beta_rate}


HIGHEST = lax.Precision.HIGHEST

def normalize(tensor):
    tensor = tensor.astype(jnp.float32)
    return tensor / jnp.sqrt(lax.optimization_barrier(jnp.sum(tensor * tensor, axis=-1, keepdims=True)) + 1e-06)

def stretch_parts(queries, keys_in, values, gate_vals, beta_vals):
    span_len = gate_vals.shape[-1]
    cumulative = jnp.cumsum(gate_vals, axis=-1)
    row_ids = lax.broadcasted_iota(jnp.int32, (span_len, span_len), 0)
    columns = lax.broadcasted_iota(jnp.int32, (span_len, span_len), 1)
    strict = row_ids > columns
    inclusive = row_ids >= columns
    differ = cumulative[..., :, None] - cumulative[..., None, :]
    key_key = jnp.einsum('...rd,...sd->...rs', keys_in, keys_in, precision=HIGHEST)
    query_key = jnp.einsum('...rd,...sd->...rs', queries, keys_in, precision=HIGHEST)
    lower_triangle = jnp.where(strict, beta_vals[..., :, None] * jnp.exp(jnp.where(strict, differ, 0.0)) * key_key, 0.0)
    scores = jnp.where(inclusive, jnp.exp(jnp.where(inclusive, differ, 0.0)) * query_key, 0.0)
    identity = jnp.eye(span_len, dtype=jnp.float32)
    right_side = jnp.concatenate([(beta_vals * jnp.exp(cumulative))[..., None] * keys_in, beta_vals[..., None] * values], axis=-1)
    solved = jax.scipy.linalg.solve_triangular(identity + lower_triangle, right_side, lower=True, unit_diagonal=True)
    key_width = keys_in.shape[-1]
    last_cum = cumulative[..., -1:]
    query_dec = jnp.exp(cumulative)[..., None] * queries
    key_dec = jnp.exp(last_cum - cumulative)[..., None] * keys_in
    return (solved[..., :key_width], solved[..., key_width:], scores, query_dec, key_dec, jnp.exp(last_cum[..., 0]))

def stretch_step(carried, pieces):
    query_part, key_segment, value_part, gate_part, beta_part = pieces
    grouping = value_part.shape[1] // query_part.shape[1]
    queries = jnp.swapaxes(jnp.repeat(normalize(query_part), grouping, axis=1), 0, 1)
    keys_in = jnp.swapaxes(jnp.repeat(normalize(key_segment), grouping, axis=1), 0, 1)
    values = jnp.swapaxes(value_part.astype(jnp.float32), 0, 1)
    gate_vals = jnp.swapaxes(gate_part.astype(jnp.float32), 0, 1)
    beta_vals = jnp.swapaxes(beta_part.astype(jnp.float32), 0, 1)
    write_keys, write_vals, scores, query_dec, key_dec, stretch_decay = stretch_parts(queries, keys_in, values, gate_vals, beta_vals)
    fresh_vals = write_vals - jnp.einsum('hcd,hde->hce', write_keys, carried, precision=HIGHEST)
    outputs = jnp.einsum('hcd,hde->hce', query_dec, carried, precision=HIGHEST) + jnp.einsum('hrs,hse->hre', scores, fresh_vals, precision=HIGHEST)
    carried = stretch_decay[:, None, None] * carried + jnp.einsum('hcd,hce->hde', key_dec, fresh_vals, precision=HIGHEST)
    return (carried, jnp.swapaxes(outputs, 0, 1).astype(jnp.bfloat16))

def reference(query_heads, key_heads, value_heads, gate_log, beta_rate):
    blocks = SLAB // STRETCH

    def arrange(tensor):
        return tensor.reshape((N_SEQ, blocks, STRETCH) + tensor.shape[1:])

    def slab_step(carried, pieces):
        carried, outputs = lax.scan(stretch_step, carried, pieces)
        return (carried, (carried, outputs))
    initial = jnp.zeros((VALUE_HEAD_COUNT, DK, DV), jnp.float32)
    last_state, (block_states, outputs) = lax.scan(slab_step, initial, (arrange(query_heads), arrange(key_heads), arrange(value_heads), arrange(gate_log), arrange(beta_rate)))
    return (outputs.reshape(PROMPT_TOKENS, VALUE_HEAD_COUNT * DV), block_states)
```

```python
import functools

import jax
import jax.numpy as jnp
from jax import lax
from jax.experimental import pallas as pl
from jax.experimental.pallas import tpu as pltpu
from jax.sharding import PartitionSpec as P

STRETCH = 64
MESH = pl.DeviceIdType.MESH


HIGHEST = lax.Precision.HIGHEST


def shifted(block, axis, distance):
    devices = range(lax.axis_size(axis))
    route = [(i - distance, i) for i in devices if i - distance in devices]
    return lax.ppermute(block, axis, route)


def normalize(tensor):
    tensor = tensor.astype(jnp.float32)
    return tensor / jnp.sqrt(jnp.sum(tensor * tensor, axis=-1, keepdims=True) + 1e-06)


def stretch_parts(queries, keys_in, values, gate_vals, beta_vals):
    span_len = gate_vals.shape[-1]
    cumulative = jnp.cumsum(gate_vals, axis=-1)
    row_ids = lax.broadcasted_iota(jnp.int32, (span_len, span_len), 0)
    columns = lax.broadcasted_iota(jnp.int32, (span_len, span_len), 1)
    strict = row_ids > columns
    inclusive = row_ids >= columns
    differ = cumulative[..., :, None] - cumulative[..., None, :]
    key_key = jnp.einsum("...rd,...sd->...rs", keys_in, keys_in, precision=HIGHEST)
    query_key = jnp.einsum("...rd,...sd->...rs", queries, keys_in, precision=HIGHEST)
    lower_triangle = jnp.where(
        strict, beta_vals[..., :, None] * jnp.exp(jnp.where(strict, differ, 0.0)) * key_key, 0.0
    )
    scores = jnp.where(inclusive, jnp.exp(jnp.where(inclusive, differ, 0.0)) * query_key, 0.0)
    identity = jnp.eye(span_len, dtype=jnp.float32)
    right_side = jnp.concatenate(
        [(beta_vals * jnp.exp(cumulative))[..., None] * keys_in, beta_vals[..., None] * values],
        axis=-1,
    )
    solved = jax.scipy.linalg.solve_triangular(
        identity + lower_triangle, right_side, lower=True, unit_diagonal=True
    )
    key_width = keys_in.shape[-1]
    last_cum = cumulative[..., -1:]
    query_dec = jnp.exp(cumulative)[..., None] * queries
    key_dec = jnp.exp(last_cum - cumulative)[..., None] * keys_in
    return (
        solved[..., :key_width],
        solved[..., key_width:],
        scores,
        query_dec,
        key_dec,
        jnp.exp(last_cum[..., 0]),
    )


def product(left_mat, right_mat):
    return jnp.einsum("...ij,...jk->...ik", left_mat, right_mat, precision=HIGHEST)


def compose(earlier, later):
    return (product(later[0], earlier[0]), product(later[0], earlier[1]) + later[1])


def slab_local(queries, keys_in, values, gate_vals, beta_vals):
    heads, length = gate_vals.shape
    blocks = length // STRETCH

    def split_rows(tensor):
        return tensor.reshape((heads, blocks, STRETCH) + tensor.shape[2:])

    write_keys, write_vals, scores, query_dec, key_dec, stretch_decay = stretch_parts(
        split_rows(queries),
        split_rows(keys_in),
        split_rows(values),
        split_rows(gate_vals),
        split_rows(beta_vals),
    )
    key_width = keys_in.shape[-1]
    identity = jnp.eye(key_width, dtype=jnp.float32)
    transit = stretch_decay[..., None, None] * identity - jnp.einsum(
        "hncd,hnce->hnde", key_dec, write_keys, precision=HIGHEST
    )
    inject = jnp.einsum("hncd,hnce->hnde", key_dec, write_vals, precision=HIGHEST)
    project = query_dec - jnp.einsum("hnrs,hnsd->hnrd", scores, write_keys, precision=HIGHEST)
    direct = jnp.einsum("hnrs,hnse->hnre", scores, write_vals, precision=HIGHEST)
    maps_all, states_all = lax.associative_scan(compose, (transit, inject), axis=1)
    reach_rest = product(project[:, 1:], maps_all[:, :-1])
    reach = jnp.concatenate([project[:, :1], reach_rest], axis=1).reshape(heads, length, key_width)
    out_rest = product(project[:, 1:], states_all[:, :-1]) + direct[:, 1:]
    local_out = jnp.concatenate([direct[:, :1], out_rest], axis=1).reshape(heads, length, -1)
    return (local_out, reach, maps_all[:, -1], states_all[:, -1])


def per_device(query_heads, key_heads, value_heads, gate_log, beta_rate):
    key_count = query_heads.shape[1]
    grouping = value_heads.shape[1] // key_count
    got_query, got_key, got_value, got_gate, got_beta = (
        lax.all_to_all(
            jnp.repeat(query_heads, grouping, axis=1),
            "head",
            split_axis=1,
            concat_axis=0,
            tiled=True,
        ),
        lax.all_to_all(
            jnp.repeat(key_heads, grouping, axis=1), "head", split_axis=1, concat_axis=0, tiled=True
        ),
        lax.all_to_all(value_heads, "head", split_axis=1, concat_axis=0, tiled=True),
        lax.all_to_all(gate_log, "head", split_axis=1, concat_axis=0, tiled=True),
        lax.all_to_all(beta_rate, "head", split_axis=1, concat_axis=0, tiled=True),
    )
    queries = jnp.swapaxes(normalize(got_query), 0, 1)
    keys_in = jnp.swapaxes(normalize(got_key), 0, 1)
    values = jnp.swapaxes(got_value.astype(jnp.float32), 0, 1)
    gate_vals = jnp.swapaxes(got_gate.astype(jnp.float32), 0, 1)
    beta_vals = jnp.swapaxes(got_beta.astype(jnp.float32), 0, 1)
    local_out, reach, slab_map, slab_state = slab_local(
        queries, keys_in, values, gate_vals, beta_vals
    )

    def advance(counter, carried):
        return shifted(product(slab_map, carried) + slab_state, "seq", 1)

    incoming = lax.fori_loop(0, lax.axis_size("seq") - 1, advance, jnp.zeros_like(slab_state))
    combined = local_out + product(reach, incoming)
    head_rows = jnp.swapaxes(combined, 0, 1).astype(jnp.bfloat16)
    flat_rows = head_rows.reshape(head_rows.shape[0], -1)
    head_output = lax.all_to_all(flat_rows, "head", split_axis=0, concat_axis=1, tiled=True)
    last_state = (product(slab_map, incoming) + slab_state)[None]
    return (head_output, last_state)


def split(matrix):
    high = matrix.astype(jnp.bfloat16)
    low = (matrix - high.astype(jnp.float32)).astype(jnp.bfloat16)
    return high, low


def dot(left, right):
    return jnp.dot(left, right, preferred_element_type=jnp.float32)


def wide(matrix):
    return jnp.concatenate(split(matrix), axis=1)


def tall(*matrices):
    row = jnp.concatenate([half for matrix in matrices for half in split(matrix)], axis=1)
    return jnp.concatenate([row, row], axis=0)


def fold(product):
    width = product.shape[1] // 2
    return product[:, :width] + product[:, width:]


def mul(left, right):
    return fold(dot(wide(left), tall(right)))


def fast_kernel(
    sizes,
    q_hbm,
    k_hbm,
    v_hbm,
    g_hbm,
    b_hbm,
    out_ref,
    states_ref,
    q_in,
    k_in,
    v_in,
    g_in,
    b_in,
    q_wide,
    k_wide,
    v_wide,
    send,
    gb_send,
    recv,
    gb_recv,
    out_buf,
    state_buf,
    load_sem,
    send_sem,
    recv_sem,
):
    ns, nh, tokens, heads, grouping = sizes
    key_heads = heads // grouping
    slab = nh * tokens
    width = 128
    s = lax.axis_index("seq")
    h = lax.axis_index("head")
    mine = h * ns + s

    loads = [
        pltpu.make_async_copy(source, target, load_sem.at[i])
        for i, (source, target) in enumerate(
            [(q_hbm, q_in), (k_hbm, k_in), (v_hbm, v_in), (g_hbm, g_in), (b_hbm, b_in)]
        )
    ]
    for load in loads:
        load.start()

    peers = []
    for ds in range(ns):
        for dh in range(nh):
            peers.append((lax.rem(s + ds, ns), lax.rem(h + dh, nh)))

    barrier = pltpu.get_barrier_semaphore()
    for ps, ph in peers[1:]:
        pl.semaphore_signal(barrier, inc=1, device_id=(ps, ph), device_id_type=MESH)

    for load in loads:
        load.wait()
    q_wide[...] = q_in[...].astype(jnp.float32).reshape(tokens * key_heads, width)
    k_wide[...] = k_in[...].astype(jnp.float32).reshape(tokens * key_heads, width)
    v_wide[...] = v_in[...].astype(jnp.float32).reshape(tokens * heads, width)
    for j in range(key_heads):
        queries = q_wide[pl.ds(j, tokens, stride=key_heads), :].astype(jnp.bfloat16)
        keys = k_wide[pl.ds(j, tokens, stride=key_heads), :].astype(jnp.bfloat16)
        for g in range(grouping):
            send[j * grouping + g, 0:tokens, :] = queries
            send[j * grouping + g, tokens : 2 * tokens, :] = keys
    for j in range(heads):
        values = v_wide[pl.ds(j, tokens, stride=heads), :].astype(jnp.bfloat16)
        send[j, 2 * tokens : 3 * tokens, :] = values
    both = jnp.concatenate([g_in[...], b_in[...]], axis=0).astype(jnp.float32)
    place_row = lax.broadcasted_iota(jnp.int32, (2 * tokens, width), 0)
    place_col = lax.broadcasted_iota(jnp.int32, (2 * tokens, width), 1)
    place = (place_row == place_col).astype(jnp.bfloat16)
    turned = dot(both.T.astype(jnp.bfloat16), place)
    for j in range(heads):
        gb_send[j, :, :] = turned[j : j + 1, :]

    pl.semaphore_wait(barrier, ns * nh - 1)

    for i, (ps, ph) in enumerate(peers):
        j = ph * ns + ps
        if i == 0:
            pltpu.make_async_copy(send.at[j], recv.at[s, h], recv_sem.at[0]).start()
            pltpu.make_async_copy(gb_send.at[j], gb_recv.at[s, h], recv_sem.at[1]).start()
        else:
            for source, target, n in ((gb_send, gb_recv, 1), (send, recv, 0)):
                pltpu.make_async_remote_copy(
                    src_ref=source.at[j],
                    dst_ref=target.at[s, h],
                    send_sem=send_sem.at[n],
                    recv_sem=recv_sem.at[n],
                    device_id=(ps, ph),
                    device_id_type=MESH,
                ).start()

    row_ids = lax.broadcasted_iota(jnp.int32, (slab, slab), 0)
    col_ids = lax.broadcasted_iota(jnp.int32, (slab, slab), 1)
    strict = row_ids > col_ids
    inclusive = row_ids >= col_ids
    eye = (row_ids == col_ids).astype(jnp.float32)
    lower_ones = inclusive.astype(jnp.bfloat16)
    all_ones = jnp.ones((slab, slab), jnp.bfloat16)
    token_at = row_ids % tokens
    expand = (
        lax.broadcasted_iota(jnp.int32, (slab, nh), 0) // tokens
        == lax.broadcasted_iota(jnp.int32, (slab, nh), 1)
    ).astype(jnp.bfloat16)

    pltpu.make_async_copy(gb_recv, gb_recv, recv_sem.at[1]).wait()
    cums, betas = [], []
    for n in range(ns):
        rates = dot(expand, gb_recv[n, :, 0, :].astype(jnp.bfloat16))
        gates = jnp.where(col_ids == token_at, rates, 0.0).astype(jnp.bfloat16)
        writes = jnp.where(col_ids == token_at + tokens, rates, 0.0).astype(jnp.bfloat16)
        gate_cols = dot(gates, all_ones).astype(jnp.bfloat16)
        cums.append(dot(lower_ones, gate_cols))
        betas.append(dot(writes, all_ones))

    pltpu.make_async_copy(recv, recv, recv_sem.at[0]).wait()

    parts = []
    for n in range(ns):
        queries = recv[n, :, 0:tokens, :].reshape(slab, width)
        keys = recv[n, :, tokens : 2 * tokens, :].reshape(slab, width)
        values = recv[n, :, 2 * tokens : 3 * tokens, :].reshape(slab, width)
        cum, beta = cums[n], betas[n]
        q32, k32 = queries.astype(jnp.float32), keys.astype(jnp.float32)
        q_norm = 1.0 / jnp.sqrt(jnp.sum(q32 * q32, axis=1, keepdims=True) + 1e-06)
        k_norm = 1.0 / jnp.sqrt(jnp.sum(k32 * k32, axis=1, keepdims=True) + 1e-06)
        columns = jnp.where(col_ids == 0, cum, jnp.where(col_ids == 1, k_norm, beta))
        rows = columns.T
        cum_row, k_norm_row, beta_row = rows[0:1, :], rows[1:2, :], rows[2:3, :]
        k_turned = k32.T.astype(jnp.bfloat16)
        decay = jnp.where(inclusive, jnp.exp(jnp.where(inclusive, cum - cum_row, 0.0)), 0.0)
        decay = decay * k_norm_row
        key_key = dot(keys, k_turned)
        query_key = dot(queries, k_turned)
        lower = jnp.where(strict, (beta * k_norm) * decay * key_key, 0.0)
        scores = q_norm * decay * query_key
        parts.append((queries, keys, values, cum, k_norm, q_norm, cum_row, k_norm_row, beta_row,
                      k_turned, lower, scores, q32))

    small = 32
    same = (row_ids // small) == (col_ids // small)
    lowers = [part[10] for part in parts]
    blocks = [jnp.where(same, lower, 0.0) for lower in lowers]
    inverses = [eye - block for block in blocks]
    powers = [mul(block, block) for block in blocks]
    reach = 2
    while reach < small:
        last = reach * 2 >= small
        for n in range(ns):
            right = tall(powers[n])
            if last:
                inverses[n] = inverses[n] + fold(dot(wide(inverses[n]), right))
            else:
                left = jnp.concatenate([wide(inverses[n]), wide(powers[n])], axis=0)
                both_products = fold(dot(left, right))
                inverses[n] = inverses[n] + both_products[:slab]
                powers[n] = both_products[slab:]
        reach *= 2
    size = small
    while size < slab:
        pair = ((row_ids // (2 * size)) == (col_ids // (2 * size))) & (
            (row_ids // size) != (col_ids // size)
        )
        inner = [mul(jnp.where(pair, lowers[n], 0.0), inverses[n]) for n in range(ns)]
        inverses = [inverses[n] - mul(inverses[n], inner[n]) for n in range(ns)]
        size *= 2

    maps = []
    for n in range(ns):
        (queries, keys, values, cum, k_norm, q_norm, cum_row, k_norm_row, beta_row,
         k_turned, lower, scores, q32) = parts[n]
        solve = inverses[n] * beta_row
        write_vals = dot(wide(solve), jnp.concatenate([values, values], axis=0))
        final = cum[slab - 1 : slab, :]
        key_decay = jnp.exp(final - cum) * k_norm
        if n == 0:
            inject = fold(dot(k_turned, wide(key_decay * write_vals)))
            direct = mul(scores, write_vals)
            maps.append((None, None, inject, direct, None))
            continue
        key_solve = solve * (jnp.exp(cum_row) * k_norm_row)
        write_keys = dot(wide(key_solve), jnp.concatenate([keys, keys], axis=0))
        scaled = jnp.concatenate([wide(key_decay * write_keys), wide(key_decay * write_vals)], axis=1)
        moved = dot(k_turned, scaled)
        read = dot(wide(scores), tall(write_keys, write_vals))
        project = (jnp.exp(cum) * q_norm) * q32 - fold(read[:, : 2 * width])
        maps.append((fold(moved[:, : 2 * width]), project, fold(moved[:, 2 * width :]),
                     fold(read[:, 2 * width :]), jnp.exp(final)))

    state = None
    for n in range(ns):
        erase, project, inject, direct, total_decay = maps[n]
        if n == 0:
            output, state = direct, inject
        else:
            right = tall(state)
            products = fold(dot(jnp.concatenate([wide(erase), wide(project)], axis=0), right))
            output = direct + products[slab:]
            state = total_decay * state + inject - products[:slab]
        out_buf[n * nh : (n + 1) * nh] = output.astype(jnp.bfloat16).reshape(nh, tokens, width)
        state_buf[n] = state

    columns = pl.ds(pl.multiple_of(mine * width, width), width)
    for i, (ps, ph) in enumerate(peers):
        block = out_buf.at[ps * nh + ph]
        target = out_ref.at[:, columns]
        if i == 0:
            pltpu.make_async_copy(block, target, recv_sem.at[2]).start()
            pltpu.make_async_copy(state_buf.at[s], states_ref.at[0, s], recv_sem.at[3]).start()
        else:
            pltpu.make_async_remote_copy(
                src_ref=block,
                dst_ref=target,
                send_sem=send_sem.at[2],
                recv_sem=recv_sem.at[2],
                device_id=(ps, ph),
                device_id_type=MESH,
            ).start()
        if i > 0 and i % nh == 0:
            pltpu.make_async_remote_copy(
                src_ref=state_buf.at[ps],
                dst_ref=states_ref.at[0, s],
                send_sem=send_sem.at[3],
                recv_sem=recv_sem.at[3],
                device_id=(ps, h),
                device_id_type=MESH,
            ).start()

    others = pl.ds(0, ns * nh - 1)
    pltpu.make_async_copy(send.at[others], send.at[others], send_sem.at[0]).wait()
    pltpu.make_async_copy(gb_send.at[others], gb_send.at[others], send_sem.at[1]).wait()
    pltpu.make_async_copy(out_buf.at[others], out_buf.at[others], send_sem.at[2]).wait()
    rest = state_buf.at[pl.ds(0, ns - 1)]
    pltpu.make_async_copy(rest, rest, send_sem.at[3]).wait()
    pltpu.make_async_copy(out_ref, out_ref, recv_sem.at[2]).wait()
    pltpu.make_async_copy(states_ref, states_ref, recv_sem.at[3]).wait()


def fast_device(query_heads, key_heads, value_heads, gate_log, beta_rate):
    ns, nh = lax.axis_size("seq"), lax.axis_size("head")
    tokens, heads, width = value_heads.shape
    key_count = key_heads.shape[1]
    sizes = (ns, nh, tokens, heads, heads // key_count)
    bf16, f32 = jnp.bfloat16, jnp.float32
    vmem = pl.BlockSpec(memory_space=pltpu.VMEM)
    return pl.pallas_call(
        functools.partial(fast_kernel, sizes),
        out_shape=(
            jax.ShapeDtypeStruct((tokens, heads * width), bf16),
            jax.ShapeDtypeStruct((1, ns, width, width), f32),
        ),
        in_specs=[pl.BlockSpec(memory_space=pl.ANY)] * 5,
        out_specs=(vmem, vmem),
        scratch_shapes=[
            pltpu.VMEM((tokens, key_count, width), bf16),
            pltpu.VMEM((tokens, key_count, width), bf16),
            pltpu.VMEM((tokens, heads, width), bf16),
            pltpu.VMEM((tokens, heads), bf16),
            pltpu.VMEM((tokens, heads), bf16),
            pltpu.VMEM((tokens * key_count, width), f32),
            pltpu.VMEM((tokens * key_count, width), f32),
            pltpu.VMEM((tokens * heads, width), f32),
            pltpu.VMEM((heads, 3 * tokens, width), bf16),
            pltpu.VMEM((heads, 1, width), f32),
            pltpu.VMEM((ns, nh, 3 * tokens, width), bf16),
            pltpu.VMEM((ns, nh, 1, width), f32),
            pltpu.VMEM((ns * nh, tokens, width), bf16),
            pltpu.VMEM((ns, width, width), f32),
            pltpu.SemaphoreType.DMA((5,)),
            pltpu.SemaphoreType.DMA((4,)),
            pltpu.SemaphoreType.DMA((4,)),
        ],
        compiler_params=pltpu.CompilerParams(
            collective_id=0, has_side_effects=True, vmem_limit_bytes=32 * 1024 * 1024
        ),
    )(query_heads, key_heads, value_heads, gate_log, beta_rate)


def choose_device(query_heads, key_heads, value_heads, gate_log, beta_rate):
    ns, nh = lax.axis_size("seq"), lax.axis_size("head")
    tokens, heads, width = value_heads.shape
    fits = ns * nh == heads and tokens == 16 and nh * tokens == 128
    fits = fits and width == 128 and key_heads.shape[2] == 128
    run = fast_device if fits else per_device
    return run(query_heads, key_heads, value_heads, gate_log, beta_rate)


def solution(mesh):
    return jax.shard_map(
        choose_device,
        mesh=mesh,
        in_specs=(
            P(("seq", "head"), None, None),
            P(("seq", "head"), None, None),
            P(("seq", "head"), None, None),
            P(("seq", "head"), None),
            P(("seq", "head"), None),
        ),
        out_specs=(P(("seq", "head"), None), P("seq", "head", None, None)),
        check_vma=False,
    )
```

```python
import functools

import jax
import jax.numpy as jnp
from jax import lax
from jax.experimental import pallas as pl
from jax.experimental.pallas import tpu as pltpu
from jax.sharding import PartitionSpec as P

STRETCH = 64
MESH = pl.DeviceIdType.MESH


HIGHEST = lax.Precision.HIGHEST


def shifted(block, axis, distance):
    devices = range(lax.axis_size(axis))
    route = [(i - distance, i) for i in devices if i - distance in devices]
    return lax.ppermute(block, axis, route)


def normalize(tensor):
    tensor = tensor.astype(jnp.float32)
    return tensor / jnp.sqrt(jnp.sum(tensor * tensor, axis=-1, keepdims=True) + 1e-06)


def stretch_parts(queries, keys_in, values, gate_vals, beta_vals):
    span_len = gate_vals.shape[-1]
    cumulative = jnp.cumsum(gate_vals, axis=-1)
    row_ids = lax.broadcasted_iota(jnp.int32, (span_len, span_len), 0)
    columns = lax.broadcasted_iota(jnp.int32, (span_len, span_len), 1)
    strict = row_ids > columns
    inclusive = row_ids >= columns
    differ = cumulative[..., :, None] - cumulative[..., None, :]
    key_key = jnp.einsum("...rd,...sd->...rs", keys_in, keys_in, precision=HIGHEST)
    query_key = jnp.einsum("...rd,...sd->...rs", queries, keys_in, precision=HIGHEST)
    lower_triangle = jnp.where(
        strict, beta_vals[..., :, None] * jnp.exp(jnp.where(strict, differ, 0.0)) * key_key, 0.0
    )
    scores = jnp.where(inclusive, jnp.exp(jnp.where(inclusive, differ, 0.0)) * query_key, 0.0)
    identity = jnp.eye(span_len, dtype=jnp.float32)
    right_side = jnp.concatenate(
        [(beta_vals * jnp.exp(cumulative))[..., None] * keys_in, beta_vals[..., None] * values],
        axis=-1,
    )
    solved = jax.scipy.linalg.solve_triangular(
        identity + lower_triangle, right_side, lower=True, unit_diagonal=True
    )
    key_width = keys_in.shape[-1]
    last_cum = cumulative[..., -1:]
    query_dec = jnp.exp(cumulative)[..., None] * queries
    key_dec = jnp.exp(last_cum - cumulative)[..., None] * keys_in
    return (
        solved[..., :key_width],
        solved[..., key_width:],
        scores,
        query_dec,
        key_dec,
        jnp.exp(last_cum[..., 0]),
    )


def product(left_mat, right_mat):
    return jnp.einsum("...ij,...jk->...ik", left_mat, right_mat, precision=HIGHEST)


def compose(earlier, later):
    return (product(later[0], earlier[0]), product(later[0], earlier[1]) + later[1])


def slab_local(queries, keys_in, values, gate_vals, beta_vals):
    heads, length = gate_vals.shape
    blocks = length // STRETCH

    def split_rows(tensor):
        return tensor.reshape((heads, blocks, STRETCH) + tensor.shape[2:])

    write_keys, write_vals, scores, query_dec, key_dec, stretch_decay = stretch_parts(
        split_rows(queries),
        split_rows(keys_in),
        split_rows(values),
        split_rows(gate_vals),
        split_rows(beta_vals),
    )
    key_width = keys_in.shape[-1]
    identity = jnp.eye(key_width, dtype=jnp.float32)
    transit = stretch_decay[..., None, None] * identity - jnp.einsum(
        "hncd,hnce->hnde", key_dec, write_keys, precision=HIGHEST
    )
    inject = jnp.einsum("hncd,hnce->hnde", key_dec, write_vals, precision=HIGHEST)
    project = query_dec - jnp.einsum("hnrs,hnsd->hnrd", scores, write_keys, precision=HIGHEST)
    direct = jnp.einsum("hnrs,hnse->hnre", scores, write_vals, precision=HIGHEST)
    maps_all, states_all = lax.associative_scan(compose, (transit, inject), axis=1)
    reach_rest = product(project[:, 1:], maps_all[:, :-1])
    reach = jnp.concatenate([project[:, :1], reach_rest], axis=1).reshape(heads, length, key_width)
    out_rest = product(project[:, 1:], states_all[:, :-1]) + direct[:, 1:]
    local_out = jnp.concatenate([direct[:, :1], out_rest], axis=1).reshape(heads, length, -1)
    return (local_out, reach, maps_all[:, -1], states_all[:, -1])


def per_device(query_heads, key_heads, value_heads, gate_log, beta_rate):
    key_count = query_heads.shape[1]
    grouping = value_heads.shape[1] // key_count
    got_query, got_key, got_value, got_gate, got_beta = (
        lax.all_to_all(
            jnp.repeat(query_heads, grouping, axis=1),
            "head",
            split_axis=1,
            concat_axis=0,
            tiled=True,
        ),
        lax.all_to_all(
            jnp.repeat(key_heads, grouping, axis=1), "head", split_axis=1, concat_axis=0, tiled=True
        ),
        lax.all_to_all(value_heads, "head", split_axis=1, concat_axis=0, tiled=True),
        lax.all_to_all(gate_log, "head", split_axis=1, concat_axis=0, tiled=True),
        lax.all_to_all(beta_rate, "head", split_axis=1, concat_axis=0, tiled=True),
    )
    queries = jnp.swapaxes(normalize(got_query), 0, 1)
    keys_in = jnp.swapaxes(normalize(got_key), 0, 1)
    values = jnp.swapaxes(got_value.astype(jnp.float32), 0, 1)
    gate_vals = jnp.swapaxes(got_gate.astype(jnp.float32), 0, 1)
    beta_vals = jnp.swapaxes(got_beta.astype(jnp.float32), 0, 1)
    local_out, reach, slab_map, slab_state = slab_local(
        queries, keys_in, values, gate_vals, beta_vals
    )

    def advance(counter, carried):
        return shifted(product(slab_map, carried) + slab_state, "seq", 1)

    incoming = lax.fori_loop(0, lax.axis_size("seq") - 1, advance, jnp.zeros_like(slab_state))
    combined = local_out + product(reach, incoming)
    head_rows = jnp.swapaxes(combined, 0, 1).astype(jnp.bfloat16)
    flat_rows = head_rows.reshape(head_rows.shape[0], -1)
    head_output = lax.all_to_all(flat_rows, "head", split_axis=0, concat_axis=1, tiled=True)
    last_state = (product(slab_map, incoming) + slab_state)[None]
    return (head_output, last_state)


def split(matrix):
    high = matrix.astype(jnp.bfloat16)
    low = (matrix - high.astype(jnp.float32)).astype(jnp.bfloat16)
    return high, low


def dot(left, right):
    return jnp.dot(left, right, preferred_element_type=jnp.float32)


def wide(matrix):
    return jnp.concatenate(split(matrix), axis=1)


def tall(*matrices):
    row = jnp.concatenate([half for matrix in matrices for half in split(matrix)], axis=1)
    return jnp.concatenate([row, row], axis=0)


def fold(product):
    width = product.shape[1] // 2
    return product[:, :width] + product[:, width:]


def mul(left, right):
    return fold(dot(wide(left), tall(right)))


def fast_kernel(
    sizes,
    q_hbm,
    k_hbm,
    v_hbm,
    g_hbm,
    b_hbm,
    out_ref,
    states_ref,
    q_in,
    k_in,
    v_in,
    g_in,
    b_in,
    q_wide,
    k_wide,
    v_wide,
    send,
    gb_send,
    recv,
    gb_recv,
    out_buf,
    state_buf,
    step_maps,
    step_terms,
    step_decay,
    load_sem,
    send_sem,
    recv_sem,
    gb_sem,
    back_sem,
):
    ns, nh, tokens, heads, grouping = sizes
    key_heads = heads // grouping
    slab = nh * tokens
    width = 128
    s = lax.axis_index("seq")
    h = lax.axis_index("head")
    mine = h * ns + s

    loads = [
        pltpu.make_async_copy(source, target, load_sem.at[i])
        for i, (source, target) in enumerate(
            [(q_hbm, q_in), (k_hbm, k_in), (v_hbm, v_in), (g_hbm, g_in), (b_hbm, b_in)]
        )
    ]
    for load in loads:
        load.start()

    peers = []
    for ds in range(ns):
        for dh in range(nh):
            peers.append((lax.rem(s + ds, ns), lax.rem(h + dh, nh)))

    barrier = pltpu.get_barrier_semaphore()
    for ps, ph in peers[1:]:
        pl.semaphore_signal(barrier, inc=1, device_id=(ps, ph), device_id_type=MESH)

    for load in loads:
        load.wait()
    q_wide[...] = q_in[...].astype(jnp.float32).reshape(tokens * key_heads, width)
    k_wide[...] = k_in[...].astype(jnp.float32).reshape(tokens * key_heads, width)
    v_wide[...] = v_in[...].astype(jnp.float32).reshape(tokens * heads, width)
    for j in range(key_heads):
        queries = q_wide[pl.ds(j, tokens, stride=key_heads), :].astype(jnp.bfloat16)
        keys = k_wide[pl.ds(j, tokens, stride=key_heads), :].astype(jnp.bfloat16)
        for g in range(grouping):
            send[j * grouping + g, 0:tokens, :] = queries
            send[j * grouping + g, tokens : 2 * tokens, :] = keys
    for j in range(heads):
        values = v_wide[pl.ds(j, tokens, stride=heads), :].astype(jnp.bfloat16)
        send[j, 2 * tokens : 3 * tokens, :] = values
    both = jnp.concatenate([g_in[...], b_in[...]], axis=0).astype(jnp.float32)
    place_row = lax.broadcasted_iota(jnp.int32, (2 * tokens, width), 0)
    place_col = lax.broadcasted_iota(jnp.int32, (2 * tokens, width), 1)
    place = (place_row == place_col).astype(jnp.bfloat16)
    turned = dot(both.T.astype(jnp.bfloat16), place)
    for j in range(heads):
        gb_send[j, :, :] = turned[j : j + 1, :]

    pl.semaphore_wait(barrier, ns * nh - 1)

    for i, (ps, ph) in enumerate(peers):
        j = ph * ns + ps
        if i == 0:
            pltpu.make_async_copy(send.at[j], recv.at[s, h], recv_sem.at[0]).start()
            pltpu.make_async_copy(gb_send.at[j], gb_recv.at[s, h], gb_sem.at[0]).start()
        else:
            for source, target, n, sem in ((gb_send, gb_recv, 1, gb_sem), (send, recv, 0, recv_sem)):
                pltpu.make_async_remote_copy(
                    src_ref=source.at[j],
                    dst_ref=target.at[s, h],
                    send_sem=send_sem.at[n],
                    recv_sem=sem.at[i // nh],
                    device_id=(ps, ph),
                    device_id_type=MESH,
                ).start()

    row_ids = lax.broadcasted_iota(jnp.int32, (slab, slab), 0)
    col_ids = lax.broadcasted_iota(jnp.int32, (slab, slab), 1)
    strict = row_ids > col_ids
    inclusive = row_ids >= col_ids
    eye = (row_ids == col_ids).astype(jnp.float32)
    lower_ones = inclusive.astype(jnp.bfloat16)
    all_ones = jnp.ones((slab, slab), jnp.bfloat16)
    token_at = row_ids % tokens
    expand = (
        lax.broadcasted_iota(jnp.int32, (slab, nh), 0) // tokens
        == lax.broadcasted_iota(jnp.int32, (slab, nh), 1)
    ).astype(jnp.bfloat16)

    for first in range(0, ns, 2):
        slabs = [lax.rem(s + ns - first - i, ns) for i in range(min(2, ns - first))]
        count = len(slabs)
        for i, at in enumerate(slabs):
            pltpu.make_async_copy(gb_recv.at[at], gb_recv.at[at], gb_sem.at[first + i]).wait()
        cums, betas = [], []
        for at in slabs:
            rates = dot(expand, gb_recv[at, :, 0, :].astype(jnp.bfloat16))
            gates = jnp.where(col_ids == token_at, rates, 0.0).astype(jnp.bfloat16)
            writes = jnp.where(col_ids == token_at + tokens, rates, 0.0).astype(jnp.bfloat16)
            gate_cols = dot(gates, all_ones).astype(jnp.bfloat16)
            cums.append(dot(lower_ones, gate_cols))
            betas.append(dot(writes, all_ones))

        for i, at in enumerate(slabs):
            pltpu.make_async_copy(recv.at[at], recv.at[at], recv_sem.at[first + i]).wait()

        parts = []
        for n in range(count):
            queries = recv[slabs[n], :, 0:tokens, :].reshape(slab, width)
            keys = recv[slabs[n], :, tokens : 2 * tokens, :].reshape(slab, width)
            values = recv[slabs[n], :, 2 * tokens : 3 * tokens, :].reshape(slab, width)
            cum, beta = cums[n], betas[n]
            q32, k32 = queries.astype(jnp.float32), keys.astype(jnp.float32)
            q_norm = 1.0 / jnp.sqrt(jnp.sum(q32 * q32, axis=1, keepdims=True) + 1e-06)
            k_norm = 1.0 / jnp.sqrt(jnp.sum(k32 * k32, axis=1, keepdims=True) + 1e-06)
            columns = jnp.where(col_ids == 0, cum, jnp.where(col_ids == 1, k_norm, beta))
            rows = columns.T
            cum_row, k_norm_row, beta_row = rows[0:1, :], rows[1:2, :], rows[2:3, :]
            k_turned = k32.T.astype(jnp.bfloat16)
            decay = jnp.where(inclusive, jnp.exp(jnp.where(inclusive, cum - cum_row, 0.0)), 0.0)
            decay = decay * k_norm_row
            key_key = dot(keys, k_turned)
            query_key = dot(queries, k_turned)
            lower = jnp.where(strict, (beta * k_norm) * decay * key_key, 0.0)
            scores = q_norm * decay * query_key
            parts.append((queries, keys, values, cum, k_norm, q_norm, cum_row, k_norm_row, beta_row,
                          k_turned, lower, scores, q32))

        small = 32
        same = (row_ids // small) == (col_ids // small)
        lowers = [part[10] for part in parts]
        blocks = [jnp.where(same, lower, 0.0) for lower in lowers]
        inverses = [eye - block for block in blocks]
        powers = [mul(block, block) for block in blocks]
        reach = 2
        while reach < small:
            last = reach * 2 >= small
            for n in range(count):
                right = tall(powers[n])
                if last:
                    inverses[n] = inverses[n] + fold(dot(wide(inverses[n]), right))
                else:
                    left = jnp.concatenate([wide(inverses[n]), wide(powers[n])], axis=0)
                    both_products = fold(dot(left, right))
                    inverses[n] = inverses[n] + both_products[:slab]
                    powers[n] = both_products[slab:]
            reach *= 2
        size = small
        while size < slab:
            pair = ((row_ids // (2 * size)) == (col_ids // (2 * size))) & (
                (row_ids // size) != (col_ids // size)
            )
            inner = [mul(jnp.where(pair, lowers[n], 0.0), inverses[n]) for n in range(count)]
            inverses = [inverses[n] - mul(inverses[n], inner[n]) for n in range(count)]
            size *= 2

        for n in range(count):
            (queries, keys, values, cum, k_norm, q_norm, cum_row, k_norm_row, beta_row,
             k_turned, lower, scores, q32) = parts[n]
            solve = inverses[n] * beta_row
            write_vals = dot(wide(solve), jnp.concatenate([values, values], axis=0))
            final = cum[slab - 1 : slab, :]
            key_decay = jnp.exp(final - cum) * k_norm
            key_solve = solve * (jnp.exp(cum_row) * k_norm_row)
            write_keys = dot(wide(key_solve), jnp.concatenate([keys, keys], axis=0))
            scaled = jnp.concatenate([wide(key_decay * write_keys), wide(key_decay * write_vals)], axis=1)
            moved = dot(k_turned, scaled)
            read = dot(wide(scores), tall(write_keys, write_vals))
            project = (jnp.exp(cum) * q_norm) * q32 - fold(read[:, : 2 * width])
            at = slabs[n]
            step_maps[at, :slab, :] = wide(fold(moved[:, : 2 * width]))
            step_maps[at, slab:, :] = wide(project)
            step_terms[at, :slab, :] = fold(moved[:, 2 * width :])
            step_terms[at, slab:, :] = fold(read[:, 2 * width :])
            step_decay[at, :, :] = jnp.exp(final)

    columns = pl.ds(pl.multiple_of(mine * width, width), width)
    state = None
    for n in range(ns):
        if n == 0:
            state, output = step_terms[n, :slab, :], step_terms[n, slab:, :]
        else:
            products = fold(dot(step_maps[n], tall(state)))
            output = step_terms[n, slab:, :] + products[slab:]
            state = step_decay[n] * state + step_terms[n, :slab, :] - products[:slab]
        out_buf[n * nh : (n + 1) * nh] = output.astype(jnp.bfloat16).reshape(nh, tokens, width)
        state_buf[n] = state

        @pl.when(s == n)
        def _():
            pltpu.make_async_copy(state_buf.at[n], states_ref.at[0, s], back_sem.at[1]).start()

        @pl.when(s != n)
        def _():
            pltpu.make_async_remote_copy(
                src_ref=state_buf.at[n],
                dst_ref=states_ref.at[0, s],
                send_sem=send_sem.at[3],
                recv_sem=back_sem.at[1],
                device_id=(n, h),
                device_id_type=MESH,
            ).start()

        def give(ph):
            pltpu.make_async_remote_copy(
                src_ref=out_buf.at[n * nh + ph],
                dst_ref=out_ref.at[:, columns],
                send_sem=send_sem.at[2],
                recv_sem=back_sem.at[0],
                device_id=(n, ph),
                device_id_type=MESH,
            ).start()

        for dh in range(1, nh):
            give(lax.rem(h + dh, nh))

        @pl.when(s == n)
        def _():
            pltpu.make_async_copy(
                out_buf.at[n * nh + h], out_ref.at[:, columns], back_sem.at[0]
            ).start()

        @pl.when(s != n)
        def _():
            give(h)

    others = pl.ds(0, ns * nh - 1)
    pltpu.make_async_copy(send.at[others], send.at[others], send_sem.at[0]).wait()
    pltpu.make_async_copy(gb_send.at[others], gb_send.at[others], send_sem.at[1]).wait()
    pltpu.make_async_copy(out_buf.at[others], out_buf.at[others], send_sem.at[2]).wait()
    rest = state_buf.at[pl.ds(0, ns - 1)]
    pltpu.make_async_copy(rest, rest, send_sem.at[3]).wait()
    pltpu.make_async_copy(out_ref, out_ref, back_sem.at[0]).wait()
    pltpu.make_async_copy(states_ref, states_ref, back_sem.at[1]).wait()


def fast_device(query_heads, key_heads, value_heads, gate_log, beta_rate):
    ns, nh = lax.axis_size("seq"), lax.axis_size("head")
    tokens, heads, width = value_heads.shape
    key_count = key_heads.shape[1]
    sizes = (ns, nh, tokens, heads, heads // key_count)
    bf16, f32 = jnp.bfloat16, jnp.float32
    anywhere = pl.BlockSpec(memory_space=pl.ANY)
    return pl.pallas_call(
        functools.partial(fast_kernel, sizes),
        out_shape=(
            jax.ShapeDtypeStruct((tokens, heads * width), bf16),
            jax.ShapeDtypeStruct((1, ns, width, width), f32),
        ),
        in_specs=[anywhere] * 5,
        out_specs=(anywhere, anywhere),
        scratch_shapes=[
            pltpu.VMEM((tokens, key_count, width), bf16),
            pltpu.VMEM((tokens, key_count, width), bf16),
            pltpu.VMEM((tokens, heads, width), bf16),
            pltpu.VMEM((tokens, heads), bf16),
            pltpu.VMEM((tokens, heads), bf16),
            pltpu.VMEM((tokens * key_count, width), f32),
            pltpu.VMEM((tokens * key_count, width), f32),
            pltpu.VMEM((tokens * heads, width), f32),
            pltpu.VMEM((heads, 3 * tokens, width), bf16),
            pltpu.VMEM((heads, 1, width), f32),
            pltpu.VMEM((ns, nh, 3 * tokens, width), bf16),
            pltpu.VMEM((ns, nh, 1, width), f32),
            pltpu.VMEM((ns * nh, tokens, width), bf16),
            pltpu.VMEM((ns, width, width), f32),
            pltpu.VMEM((ns, 2 * width, 2 * width), bf16),
            pltpu.VMEM((ns, 2 * width, width), f32),
            pltpu.VMEM((ns, 1, width), f32),
            pltpu.SemaphoreType.DMA((5,)),
            pltpu.SemaphoreType.DMA((4,)),
            pltpu.SemaphoreType.DMA((ns,)),
            pltpu.SemaphoreType.DMA((ns,)),
            pltpu.SemaphoreType.DMA((2,)),
        ],
        compiler_params=pltpu.CompilerParams(
            collective_id=0, has_side_effects=True, vmem_limit_bytes=60 * 1024 * 1024
        ),
    )(query_heads, key_heads, value_heads, gate_log, beta_rate)


def choose_device(query_heads, key_heads, value_heads, gate_log, beta_rate):
    ns, nh = lax.axis_size("seq"), lax.axis_size("head")
    tokens, heads, width = value_heads.shape
    fits = ns * nh == heads and tokens == 16 and nh * tokens == 128
    fits = fits and width == 128 and key_heads.shape[2] == 128
    run = fast_device if fits else per_device
    return run(query_heads, key_heads, value_heads, gate_log, beta_rate)


def solution(mesh):
    return jax.shard_map(
        choose_device,
        mesh=mesh,
        in_specs=(
            P(("seq", "head"), None, None),
            P(("seq", "head"), None, None),
            P(("seq", "head"), None, None),
            P(("seq", "head"), None),
            P(("seq", "head"), None),
        ),
        out_specs=(P(("seq", "head"), None), P("seq", "head", None, None)),
        check_vma=False,
    )
```

```python
import functools

import jax
import jax.numpy as jnp
from jax import lax
from jax.experimental import pallas as pl
from jax.experimental.pallas import tpu as pltpu
from jax.sharding import PartitionSpec as P

STRETCH = 64
MESH = pl.DeviceIdType.MESH


HIGHEST = lax.Precision.HIGHEST


def shifted(block, axis, distance):
    devices = range(lax.axis_size(axis))
    route = [(i - distance, i) for i in devices if i - distance in devices]
    return lax.ppermute(block, axis, route)


def normalize(tensor):
    tensor = tensor.astype(jnp.float32)
    return tensor / jnp.sqrt(jnp.sum(tensor * tensor, axis=-1, keepdims=True) + 1e-06)


def stretch_parts(queries, keys_in, values, gate_vals, beta_vals):
    span_len = gate_vals.shape[-1]
    cumulative = jnp.cumsum(gate_vals, axis=-1)
    row_ids = lax.broadcasted_iota(jnp.int32, (span_len, span_len), 0)
    columns = lax.broadcasted_iota(jnp.int32, (span_len, span_len), 1)
    strict = row_ids > columns
    inclusive = row_ids >= columns
    differ = cumulative[..., :, None] - cumulative[..., None, :]
    key_key = jnp.einsum("...rd,...sd->...rs", keys_in, keys_in, precision=HIGHEST)
    query_key = jnp.einsum("...rd,...sd->...rs", queries, keys_in, precision=HIGHEST)
    lower_triangle = jnp.where(
        strict, beta_vals[..., :, None] * jnp.exp(jnp.where(strict, differ, 0.0)) * key_key, 0.0
    )
    scores = jnp.where(inclusive, jnp.exp(jnp.where(inclusive, differ, 0.0)) * query_key, 0.0)
    identity = jnp.eye(span_len, dtype=jnp.float32)
    right_side = jnp.concatenate(
        [(beta_vals * jnp.exp(cumulative))[..., None] * keys_in, beta_vals[..., None] * values],
        axis=-1,
    )
    solved = jax.scipy.linalg.solve_triangular(
        identity + lower_triangle, right_side, lower=True, unit_diagonal=True
    )
    key_width = keys_in.shape[-1]
    last_cum = cumulative[..., -1:]
    query_dec = jnp.exp(cumulative)[..., None] * queries
    key_dec = jnp.exp(last_cum - cumulative)[..., None] * keys_in
    return (
        solved[..., :key_width],
        solved[..., key_width:],
        scores,
        query_dec,
        key_dec,
        jnp.exp(last_cum[..., 0]),
    )


def product(left_mat, right_mat):
    return jnp.einsum("...ij,...jk->...ik", left_mat, right_mat, precision=HIGHEST)


def compose(earlier, later):
    return (product(later[0], earlier[0]), product(later[0], earlier[1]) + later[1])


def slab_local(queries, keys_in, values, gate_vals, beta_vals):
    heads, length = gate_vals.shape
    blocks = length // STRETCH

    def split_rows(tensor):
        return tensor.reshape((heads, blocks, STRETCH) + tensor.shape[2:])

    write_keys, write_vals, scores, query_dec, key_dec, stretch_decay = stretch_parts(
        split_rows(queries),
        split_rows(keys_in),
        split_rows(values),
        split_rows(gate_vals),
        split_rows(beta_vals),
    )
    key_width = keys_in.shape[-1]
    identity = jnp.eye(key_width, dtype=jnp.float32)
    transit = stretch_decay[..., None, None] * identity - jnp.einsum(
        "hncd,hnce->hnde", key_dec, write_keys, precision=HIGHEST
    )
    inject = jnp.einsum("hncd,hnce->hnde", key_dec, write_vals, precision=HIGHEST)
    project = query_dec - jnp.einsum("hnrs,hnsd->hnrd", scores, write_keys, precision=HIGHEST)
    direct = jnp.einsum("hnrs,hnse->hnre", scores, write_vals, precision=HIGHEST)
    maps_all, states_all = lax.associative_scan(compose, (transit, inject), axis=1)
    reach_rest = product(project[:, 1:], maps_all[:, :-1])
    reach = jnp.concatenate([project[:, :1], reach_rest], axis=1).reshape(heads, length, key_width)
    out_rest = product(project[:, 1:], states_all[:, :-1]) + direct[:, 1:]
    local_out = jnp.concatenate([direct[:, :1], out_rest], axis=1).reshape(heads, length, -1)
    return (local_out, reach, maps_all[:, -1], states_all[:, -1])


def per_device(query_heads, key_heads, value_heads, gate_log, beta_rate):
    key_count = query_heads.shape[1]
    grouping = value_heads.shape[1] // key_count
    got_query, got_key, got_value, got_gate, got_beta = (
        lax.all_to_all(
            jnp.repeat(query_heads, grouping, axis=1),
            "head",
            split_axis=1,
            concat_axis=0,
            tiled=True,
        ),
        lax.all_to_all(
            jnp.repeat(key_heads, grouping, axis=1), "head", split_axis=1, concat_axis=0, tiled=True
        ),
        lax.all_to_all(value_heads, "head", split_axis=1, concat_axis=0, tiled=True),
        lax.all_to_all(gate_log, "head", split_axis=1, concat_axis=0, tiled=True),
        lax.all_to_all(beta_rate, "head", split_axis=1, concat_axis=0, tiled=True),
    )
    queries = jnp.swapaxes(normalize(got_query), 0, 1)
    keys_in = jnp.swapaxes(normalize(got_key), 0, 1)
    values = jnp.swapaxes(got_value.astype(jnp.float32), 0, 1)
    gate_vals = jnp.swapaxes(got_gate.astype(jnp.float32), 0, 1)
    beta_vals = jnp.swapaxes(got_beta.astype(jnp.float32), 0, 1)
    local_out, reach, slab_map, slab_state = slab_local(
        queries, keys_in, values, gate_vals, beta_vals
    )

    def advance(counter, carried):
        return shifted(product(slab_map, carried) + slab_state, "seq", 1)

    incoming = lax.fori_loop(0, lax.axis_size("seq") - 1, advance, jnp.zeros_like(slab_state))
    combined = local_out + product(reach, incoming)
    head_rows = jnp.swapaxes(combined, 0, 1).astype(jnp.bfloat16)
    flat_rows = head_rows.reshape(head_rows.shape[0], -1)
    head_output = lax.all_to_all(flat_rows, "head", split_axis=0, concat_axis=1, tiled=True)
    last_state = (product(slab_map, incoming) + slab_state)[None]
    return (head_output, last_state)


def split(matrix):
    high = matrix.astype(jnp.bfloat16)
    low = (matrix - high.astype(jnp.float32)).astype(jnp.bfloat16)
    return high, low


def dot(left, right):
    return jnp.dot(left, right, preferred_element_type=jnp.float32)


def wide(matrix):
    return jnp.concatenate(split(matrix), axis=1)


def tall(*matrices):
    row = jnp.concatenate([half for matrix in matrices for half in split(matrix)], axis=1)
    return jnp.concatenate([row, row], axis=0)


def fold(product):
    width = product.shape[1] // 2
    return product[:, :width] + product[:, width:]


def mul(left, right):
    return fold(dot(wide(left), tall(right)))


def fast_kernel(
    sizes,
    q_hbm,
    k_hbm,
    v_hbm,
    g_hbm,
    b_hbm,
    out_ref,
    states_ref,
    q_in,
    k_in,
    v_in,
    g_in,
    b_in,
    q_wide,
    k_wide,
    v_wide,
    send,
    gb_send,
    recv,
    swapped,
    gb_recv,
    out_buf,
    state_buf,
    step_maps,
    step_terms,
    step_decay,
    load_sem,
    send_sem,
    recv_sem,
    gb_sem,
    back_sem,
    swap_sem,
):
    ns, nh, tokens, heads, key_heads = sizes
    slab = nh * tokens
    width = 128
    s = lax.axis_index("seq")
    h = lax.axis_index("head")
    mine = h * ns + s

    loads = [
        pltpu.make_async_copy(source, target, load_sem.at[i])
        for i, (source, target) in enumerate(
            [(q_hbm, q_in), (k_hbm, k_in), (v_hbm, v_in), (g_hbm, g_in), (b_hbm, b_in)]
        )
    ]
    for load in loads:
        load.start()

    peers = []
    seq_peers = [s]
    for ds in range(1, ns):
        other, bit = s, 1
        while bit <= ds:
            if ds & bit:
                other = other + bit - 2 * bit * lax.rem(s // bit, 2)
            bit *= 2
        seq_peers.append(other)
    for ps in seq_peers:
        for dh in range(nh):
            peers.append((ps, lax.rem(h + dh, nh)))
    even = lax.rem(s, 2) == 0

    barrier = pltpu.get_barrier_semaphore()
    for ps, ph in peers[1:]:
        pl.semaphore_signal(barrier, inc=1, device_id=(ps, ph), device_id_type=MESH)

    for load in loads:
        load.wait()
    q_wide[...] = q_in[...].astype(jnp.float32).reshape(tokens * key_heads, width)
    k_wide[...] = k_in[...].astype(jnp.float32).reshape(tokens * key_heads, width)
    v_wide[...] = v_in[...].astype(jnp.float32).reshape(tokens * heads, width)
    for j in range(key_heads):
        queries = q_wide[pl.ds(j, tokens, stride=key_heads), :].astype(jnp.bfloat16)
        keys = k_wide[pl.ds(j, tokens, stride=key_heads), :].astype(jnp.bfloat16)
        send[2 * j, 0:tokens, :] = queries
        send[2 * j + 1, 0:tokens, :] = keys
    for j in range(heads):
        values = v_wide[pl.ds(j, tokens, stride=heads), :].astype(jnp.bfloat16)
        send[j, tokens : 2 * tokens, :] = values
    both = jnp.concatenate([g_in[...], b_in[...]], axis=0).astype(jnp.float32)
    place_row = lax.broadcasted_iota(jnp.int32, (2 * tokens, width), 0)
    place_col = lax.broadcasted_iota(jnp.int32, (2 * tokens, width), 1)
    place = (place_row == place_col).astype(jnp.bfloat16)
    turned = dot(both.T.astype(jnp.bfloat16), place)
    for j in range(heads):
        gb_send[j, :, :] = turned[j : j + 1, :]

    pl.semaphore_wait(barrier, ns * nh - 1)

    for i, (ps, ph) in enumerate(peers):
        j = ph * ns + ps
        if i == 0:
            pltpu.make_async_copy(send.at[j], recv.at[s, h], recv_sem.at[0]).start()
            pltpu.make_async_copy(gb_send.at[j], gb_recv.at[s, h], gb_sem.at[0]).start()
        else:
            for source, target, n, sem in ((gb_send, gb_recv, 1, gb_sem), (send, recv, 0, recv_sem)):
                pltpu.make_async_remote_copy(
                    src_ref=source.at[j],
                    dst_ref=target.at[s, h],
                    send_sem=send_sem.at[n],
                    recv_sem=sem.at[i // nh],
                    device_id=(ps, ph),
                    device_id_type=MESH,
                ).start()

    row_ids = lax.broadcasted_iota(jnp.int32, (slab, slab), 0)
    col_ids = lax.broadcasted_iota(jnp.int32, (slab, slab), 1)
    strict = row_ids > col_ids
    inclusive = row_ids >= col_ids
    eye = (row_ids == col_ids).astype(jnp.float32)
    lower_ones = inclusive.astype(jnp.bfloat16)
    all_ones = jnp.ones((slab, slab), jnp.bfloat16)
    token_at = row_ids % tokens
    expand = (
        lax.broadcasted_iota(jnp.int32, (slab, nh), 0) // tokens
        == lax.broadcasted_iota(jnp.int32, (slab, nh), 1)
    ).astype(jnp.bfloat16)

    for first in range(0, ns, 2):
        slabs = seq_peers[first : first + 2]
        count = len(slabs)
        for i, at in enumerate(slabs):
            pltpu.make_async_copy(gb_recv.at[at], gb_recv.at[at], gb_sem.at[first + i]).wait()
        cums, betas = [], []
        for at in slabs:
            rates = dot(expand, gb_recv[at, :, 0, :].astype(jnp.bfloat16))
            gates = jnp.where(col_ids == token_at, rates, 0.0).astype(jnp.bfloat16)
            writes = jnp.where(col_ids == token_at + tokens, rates, 0.0).astype(jnp.bfloat16)
            gate_cols = dot(gates, all_ones).astype(jnp.bfloat16)
            cums.append(dot(lower_ones, gate_cols))
            betas.append(dot(writes, all_ones))

        for i, at in enumerate(slabs):
            pltpu.make_async_copy(recv.at[at], recv.at[at], recv_sem.at[first + i]).wait()
            pltpu.make_async_remote_copy(
                src_ref=recv.at[at, :, 0:tokens, :],
                dst_ref=swapped.at[at],
                send_sem=send_sem.at[4],
                recv_sem=swap_sem.at[first // 2],
                device_id=(seq_peers[1], h),
                device_id_type=MESH,
            ).start()
        two = swapped.at[pl.ds(0, count)]
        pltpu.make_async_copy(two, two, swap_sem.at[first // 2]).wait()

        parts = []
        for n in range(count):
            own = recv[slabs[n], :, 0:tokens, :].reshape(slab, width)
            other = swapped[slabs[n]].reshape(slab, width)
            queries, keys = jnp.where(even, own, other), jnp.where(even, other, own)
            values = recv[slabs[n], :, tokens : 2 * tokens, :].reshape(slab, width)
            cum, beta = cums[n], betas[n]
            q32, k32 = queries.astype(jnp.float32), keys.astype(jnp.float32)
            q_norm = 1.0 / jnp.sqrt(jnp.sum(q32 * q32, axis=1, keepdims=True) + 1e-06)
            k_norm = 1.0 / jnp.sqrt(jnp.sum(k32 * k32, axis=1, keepdims=True) + 1e-06)
            columns = jnp.where(col_ids == 0, cum, jnp.where(col_ids == 1, k_norm, beta))
            rows = columns.T
            cum_row, k_norm_row, beta_row = rows[0:1, :], rows[1:2, :], rows[2:3, :]
            k_turned = k32.T.astype(jnp.bfloat16)
            decay = jnp.where(inclusive, jnp.exp(jnp.where(inclusive, cum - cum_row, 0.0)), 0.0)
            decay = decay * k_norm_row
            key_key = dot(keys, k_turned)
            query_key = dot(queries, k_turned)
            lower = jnp.where(strict, (beta * k_norm) * decay * key_key, 0.0)
            scores = q_norm * decay * query_key
            parts.append((queries, keys, values, cum, k_norm, q_norm, cum_row, k_norm_row, beta_row,
                          k_turned, lower, scores, q32))

        small = 32
        same = (row_ids // small) == (col_ids // small)
        lowers = [part[10] for part in parts]
        blocks = [jnp.where(same, lower, 0.0) for lower in lowers]
        inverses = [eye - block for block in blocks]
        powers = [mul(block, block) for block in blocks]
        reach = 2
        while reach < small:
            last = reach * 2 >= small
            for n in range(count):
                right = tall(powers[n])
                if last:
                    inverses[n] = inverses[n] + fold(dot(wide(inverses[n]), right))
                else:
                    left = jnp.concatenate([wide(inverses[n]), wide(powers[n])], axis=0)
                    both_products = fold(dot(left, right))
                    inverses[n] = inverses[n] + both_products[:slab]
                    powers[n] = both_products[slab:]
            reach *= 2
        size = small
        while size < slab:
            pair = ((row_ids // (2 * size)) == (col_ids // (2 * size))) & (
                (row_ids // size) != (col_ids // size)
            )
            inner = [mul(jnp.where(pair, lowers[n], 0.0), inverses[n]) for n in range(count)]
            inverses = [inverses[n] - mul(inverses[n], inner[n]) for n in range(count)]
            size *= 2

        for n in range(count):
            (queries, keys, values, cum, k_norm, q_norm, cum_row, k_norm_row, beta_row,
             k_turned, lower, scores, q32) = parts[n]
            solve = inverses[n] * beta_row
            write_vals = dot(wide(solve), jnp.concatenate([values, values], axis=0))
            final = cum[slab - 1 : slab, :]
            key_decay = jnp.exp(final - cum) * k_norm
            key_solve = solve * (jnp.exp(cum_row) * k_norm_row)
            write_keys = dot(wide(key_solve), jnp.concatenate([keys, keys], axis=0))
            scaled = jnp.concatenate([wide(key_decay * write_keys), wide(key_decay * write_vals)], axis=1)
            moved = dot(k_turned, scaled)
            read = dot(wide(scores), tall(write_keys, write_vals))
            project = (jnp.exp(cum) * q_norm) * q32 - fold(read[:, : 2 * width])
            at = slabs[n]
            step_maps[at, :slab, :] = wide(fold(moved[:, : 2 * width]))
            step_maps[at, slab:, :] = wide(project)
            step_terms[at, :slab, :] = fold(moved[:, 2 * width :])
            step_terms[at, slab:, :] = fold(read[:, 2 * width :])
            step_decay[at, :, :] = jnp.exp(final)

    columns = pl.ds(pl.multiple_of(mine * width, width), width)
    state = None
    for n in range(ns):
        if n == 0:
            state, output = step_terms[n, :slab, :], step_terms[n, slab:, :]
        else:
            products = fold(dot(step_maps[n], tall(state)))
            output = step_terms[n, slab:, :] + products[slab:]
            state = step_decay[n] * state + step_terms[n, :slab, :] - products[:slab]
        out_buf[n * nh : (n + 1) * nh] = output.astype(jnp.bfloat16).reshape(nh, tokens, width)
        state_buf[n] = state

        @pl.when(s == n)
        def _():
            pltpu.make_async_copy(state_buf.at[n], states_ref.at[0, s], back_sem.at[1]).start()

        @pl.when(s != n)
        def _():
            pltpu.make_async_remote_copy(
                src_ref=state_buf.at[n],
                dst_ref=states_ref.at[0, s],
                send_sem=send_sem.at[3],
                recv_sem=back_sem.at[1],
                device_id=(n, h),
                device_id_type=MESH,
            ).start()

        def give(ph):
            pltpu.make_async_remote_copy(
                src_ref=out_buf.at[n * nh + ph],
                dst_ref=out_ref.at[:, columns],
                send_sem=send_sem.at[2],
                recv_sem=back_sem.at[0],
                device_id=(n, ph),
                device_id_type=MESH,
            ).start()

        for dh in range(1, nh):
            give(lax.rem(h + dh, nh))

        @pl.when(s == n)
        def _():
            pltpu.make_async_copy(
                out_buf.at[n * nh + h], out_ref.at[:, columns], back_sem.at[0]
            ).start()

        @pl.when(s != n)
        def _():
            give(h)

    others = pl.ds(0, ns * nh - 1)
    pltpu.make_async_copy(send.at[others], send.at[others], send_sem.at[0]).wait()
    pltpu.make_async_copy(gb_send.at[others], gb_send.at[others], send_sem.at[1]).wait()
    pltpu.make_async_copy(out_buf.at[others], out_buf.at[others], send_sem.at[2]).wait()
    pltpu.make_async_copy(swapped, swapped, send_sem.at[4]).wait()
    rest = state_buf.at[pl.ds(0, ns - 1)]
    pltpu.make_async_copy(rest, rest, send_sem.at[3]).wait()
    pltpu.make_async_copy(out_ref, out_ref, back_sem.at[0]).wait()
    pltpu.make_async_copy(states_ref, states_ref, back_sem.at[1]).wait()


def fast_device(query_heads, key_heads, value_heads, gate_log, beta_rate):
    ns, nh = lax.axis_size("seq"), lax.axis_size("head")
    tokens, heads, width = value_heads.shape
    key_count = key_heads.shape[1]
    sizes = (ns, nh, tokens, heads, key_count)
    bf16, f32 = jnp.bfloat16, jnp.float32
    anywhere = pl.BlockSpec(memory_space=pl.ANY)
    return pl.pallas_call(
        functools.partial(fast_kernel, sizes),
        out_shape=(
            jax.ShapeDtypeStruct((tokens, heads * width), bf16),
            jax.ShapeDtypeStruct((1, ns, width, width), f32),
        ),
        in_specs=[anywhere] * 5,
        out_specs=(anywhere, anywhere),
        scratch_shapes=[
            pltpu.VMEM((tokens, key_count, width), bf16),
            pltpu.VMEM((tokens, key_count, width), bf16),
            pltpu.VMEM((tokens, heads, width), bf16),
            pltpu.VMEM((tokens, heads), bf16),
            pltpu.VMEM((tokens, heads), bf16),
            pltpu.VMEM((tokens * key_count, width), f32),
            pltpu.VMEM((tokens * key_count, width), f32),
            pltpu.VMEM((tokens * heads, width), f32),
            pltpu.VMEM((heads, 2 * tokens, width), bf16),
            pltpu.VMEM((heads, 1, width), f32),
            pltpu.VMEM((ns, nh, 2 * tokens, width), bf16),
            pltpu.VMEM((ns, nh, tokens, width), bf16),
            pltpu.VMEM((ns, nh, 1, width), f32),
            pltpu.VMEM((ns * nh, tokens, width), bf16),
            pltpu.VMEM((ns, width, width), f32),
            pltpu.VMEM((ns, 2 * width, 2 * width), bf16),
            pltpu.VMEM((ns, 2 * width, width), f32),
            pltpu.VMEM((ns, 1, width), f32),
            pltpu.SemaphoreType.DMA((5,)),
            pltpu.SemaphoreType.DMA((5,)),
            pltpu.SemaphoreType.DMA((ns,)),
            pltpu.SemaphoreType.DMA((ns,)),
            pltpu.SemaphoreType.DMA((2,)),
            pltpu.SemaphoreType.DMA((ns // 2,)),
        ],
        compiler_params=pltpu.CompilerParams(
            collective_id=0, has_side_effects=True, vmem_limit_bytes=60 * 1024 * 1024
        ),
    )(query_heads, key_heads, value_heads, gate_log, beta_rate)


def choose_device(query_heads, key_heads, value_heads, gate_log, beta_rate):
    ns, nh = lax.axis_size("seq"), lax.axis_size("head")
    tokens, heads, width = value_heads.shape
    fits = ns * nh == heads and tokens == 16 and nh * tokens == 128
    fits = fits and width == 128 and key_heads.shape[2] == 128
    fits = fits and heads == 2 * key_heads.shape[1] and ns in (2, 4, 8)
    run = fast_device if fits else per_device
    return run(query_heads, key_heads, value_heads, gate_log, beta_rate)


def solution(mesh):
    return jax.shard_map(
        choose_device,
        mesh=mesh,
        in_specs=(
            P(("seq", "head"), None, None),
            P(("seq", "head"), None, None),
            P(("seq", "head"), None, None),
            P(("seq", "head"), None),
            P(("seq", "head"), None),
        ),
        out_specs=(P(("seq", "head"), None), P("seq", "head", None, None)),
        check_vma=False,
    )
```

```python
import functools

import jax
import jax.numpy as jnp
from jax import lax
from jax.experimental import pallas as pl
from jax.experimental.pallas import tpu as pltpu
from jax.sharding import PartitionSpec as P

STRETCH = 64
MESH = pl.DeviceIdType.MESH


HIGHEST = lax.Precision.HIGHEST


def shifted(block, axis, distance):
    devices = range(lax.axis_size(axis))
    route = [(i - distance, i) for i in devices if i - distance in devices]
    return lax.ppermute(block, axis, route)


def normalize(tensor):
    tensor = tensor.astype(jnp.float32)
    return tensor / jnp.sqrt(jnp.sum(tensor * tensor, axis=-1, keepdims=True) + 1e-06)


def stretch_parts(queries, keys_in, values, gate_vals, beta_vals):
    span_len = gate_vals.shape[-1]
    cumulative = jnp.cumsum(gate_vals, axis=-1)
    row_ids = lax.broadcasted_iota(jnp.int32, (span_len, span_len), 0)
    columns = lax.broadcasted_iota(jnp.int32, (span_len, span_len), 1)
    strict = row_ids > columns
    inclusive = row_ids >= columns
    differ = cumulative[..., :, None] - cumulative[..., None, :]
    key_key = jnp.einsum("...rd,...sd->...rs", keys_in, keys_in, precision=HIGHEST)
    query_key = jnp.einsum("...rd,...sd->...rs", queries, keys_in, precision=HIGHEST)
    lower_triangle = jnp.where(
        strict, beta_vals[..., :, None] * jnp.exp(jnp.where(strict, differ, 0.0)) * key_key, 0.0
    )
    scores = jnp.where(inclusive, jnp.exp(jnp.where(inclusive, differ, 0.0)) * query_key, 0.0)
    identity = jnp.eye(span_len, dtype=jnp.float32)
    right_side = jnp.concatenate(
        [(beta_vals * jnp.exp(cumulative))[..., None] * keys_in, beta_vals[..., None] * values],
        axis=-1,
    )
    solved = jax.scipy.linalg.solve_triangular(
        identity + lower_triangle, right_side, lower=True, unit_diagonal=True
    )
    key_width = keys_in.shape[-1]
    last_cum = cumulative[..., -1:]
    query_dec = jnp.exp(cumulative)[..., None] * queries
    key_dec = jnp.exp(last_cum - cumulative)[..., None] * keys_in
    return (
        solved[..., :key_width],
        solved[..., key_width:],
        scores,
        query_dec,
        key_dec,
        jnp.exp(last_cum[..., 0]),
    )


def product(left_mat, right_mat):
    return jnp.einsum("...ij,...jk->...ik", left_mat, right_mat, precision=HIGHEST)


def compose(earlier, later):
    return (product(later[0], earlier[0]), product(later[0], earlier[1]) + later[1])


def slab_local(queries, keys_in, values, gate_vals, beta_vals):
    heads, length = gate_vals.shape
    blocks = length // STRETCH

    def split_rows(tensor):
        return tensor.reshape((heads, blocks, STRETCH) + tensor.shape[2:])

    write_keys, write_vals, scores, query_dec, key_dec, stretch_decay = stretch_parts(
        split_rows(queries),
        split_rows(keys_in),
        split_rows(values),
        split_rows(gate_vals),
        split_rows(beta_vals),
    )
    key_width = keys_in.shape[-1]
    identity = jnp.eye(key_width, dtype=jnp.float32)
    transit = stretch_decay[..., None, None] * identity - jnp.einsum(
        "hncd,hnce->hnde", key_dec, write_keys, precision=HIGHEST
    )
    inject = jnp.einsum("hncd,hnce->hnde", key_dec, write_vals, precision=HIGHEST)
    project = query_dec - jnp.einsum("hnrs,hnsd->hnrd", scores, write_keys, precision=HIGHEST)
    direct = jnp.einsum("hnrs,hnse->hnre", scores, write_vals, precision=HIGHEST)
    maps_all, states_all = lax.associative_scan(compose, (transit, inject), axis=1)
    reach_rest = product(project[:, 1:], maps_all[:, :-1])
    reach = jnp.concatenate([project[:, :1], reach_rest], axis=1).reshape(heads, length, key_width)
    out_rest = product(project[:, 1:], states_all[:, :-1]) + direct[:, 1:]
    local_out = jnp.concatenate([direct[:, :1], out_rest], axis=1).reshape(heads, length, -1)
    return (local_out, reach, maps_all[:, -1], states_all[:, -1])


def per_device(query_heads, key_heads, value_heads, gate_log, beta_rate):
    key_count = query_heads.shape[1]
    grouping = value_heads.shape[1] // key_count
    got_query, got_key, got_value, got_gate, got_beta = (
        lax.all_to_all(
            jnp.repeat(query_heads, grouping, axis=1),
            "head",
            split_axis=1,
            concat_axis=0,
            tiled=True,
        ),
        lax.all_to_all(
            jnp.repeat(key_heads, grouping, axis=1), "head", split_axis=1, concat_axis=0, tiled=True
        ),
        lax.all_to_all(value_heads, "head", split_axis=1, concat_axis=0, tiled=True),
        lax.all_to_all(gate_log, "head", split_axis=1, concat_axis=0, tiled=True),
        lax.all_to_all(beta_rate, "head", split_axis=1, concat_axis=0, tiled=True),
    )
    queries = jnp.swapaxes(normalize(got_query), 0, 1)
    keys_in = jnp.swapaxes(normalize(got_key), 0, 1)
    values = jnp.swapaxes(got_value.astype(jnp.float32), 0, 1)
    gate_vals = jnp.swapaxes(got_gate.astype(jnp.float32), 0, 1)
    beta_vals = jnp.swapaxes(got_beta.astype(jnp.float32), 0, 1)
    local_out, reach, slab_map, slab_state = slab_local(
        queries, keys_in, values, gate_vals, beta_vals
    )

    def advance(counter, carried):
        return shifted(product(slab_map, carried) + slab_state, "seq", 1)

    incoming = lax.fori_loop(0, lax.axis_size("seq") - 1, advance, jnp.zeros_like(slab_state))
    combined = local_out + product(reach, incoming)
    head_rows = jnp.swapaxes(combined, 0, 1).astype(jnp.bfloat16)
    flat_rows = head_rows.reshape(head_rows.shape[0], -1)
    head_output = lax.all_to_all(flat_rows, "head", split_axis=0, concat_axis=1, tiled=True)
    last_state = (product(slab_map, incoming) + slab_state)[None]
    return (head_output, last_state)


def split(matrix):
    high = matrix.astype(jnp.bfloat16)
    low = (matrix - high.astype(jnp.float32)).astype(jnp.bfloat16)
    return high, low


def dot(left, right):
    return jnp.dot(left, right, preferred_element_type=jnp.float32)


def wide(matrix):
    return jnp.concatenate(split(matrix), axis=1)


def tall(*matrices):
    row = jnp.concatenate([half for matrix in matrices for half in split(matrix)], axis=1)
    return jnp.concatenate([row, row], axis=0)


def fold(product):
    width = product.shape[1] // 2
    return product[:, :width] + product[:, width:]


def mul(left, right):
    return fold(dot(wide(left), tall(right)))


def fast_kernel(
    sizes,
    q_hbm,
    k_hbm,
    v_hbm,
    g_hbm,
    b_hbm,
    out_ref,
    states_ref,
    q_in,
    k_in,
    v_in,
    g_in,
    b_in,
    q_wide,
    k_wide,
    v_wide,
    send,
    recv,
    swapped,
    gb_all,
    out_buf,
    state_buf,
    step_maps,
    step_terms,
    step_decay,
    load_sem,
    send_sem,
    recv_sem,
    gb_sem,
    back_sem,
    swap_sem,
):
    ns, nh, tokens, heads, key_heads = sizes
    slab = nh * tokens
    width = 128
    s = lax.axis_index("seq")
    h = lax.axis_index("head")
    mine = h * ns + s

    loads = [
        pltpu.make_async_copy(source, target, load_sem.at[i])
        for i, (source, target) in enumerate(
            [(q_hbm, q_in), (k_hbm, k_in), (v_hbm, v_in), (g_hbm, g_in), (b_hbm, b_in)]
        )
    ]
    for load in loads:
        load.start()

    peers = []
    seq_peers = [s]
    for ds in range(1, ns):
        other, bit = s, 1
        while bit <= ds:
            if ds & bit:
                other = other + bit - 2 * bit * lax.rem(s // bit, 2)
            bit *= 2
        seq_peers.append(other)
    for ps in seq_peers:
        for dh in range(nh):
            peers.append((ps, lax.rem(h + dh, nh)))
    even = lax.rem(s, 2) == 0

    barrier = pltpu.get_barrier_semaphore()
    for ps, ph in peers[1:]:
        pl.semaphore_signal(barrier, inc=1, device_id=(ps, ph), device_id_type=MESH)

    for load in loads:
        load.wait()
    q_wide[...] = q_in[...].astype(jnp.float32).reshape(tokens * key_heads, width)
    k_wide[...] = k_in[...].astype(jnp.float32).reshape(tokens * key_heads, width)
    v_wide[...] = v_in[...].astype(jnp.float32).reshape(tokens * heads, width)
    for j in range(key_heads):
        queries = q_wide[pl.ds(j, tokens, stride=key_heads), :].astype(jnp.bfloat16)
        keys = k_wide[pl.ds(j, tokens, stride=key_heads), :].astype(jnp.bfloat16)
        send[2 * j, 0:tokens, :] = queries
        send[2 * j + 1, 0:tokens, :] = keys
    for j in range(heads):
        values = v_wide[pl.ds(j, tokens, stride=heads), :].astype(jnp.bfloat16)
        send[j, tokens : 2 * tokens, :] = values
    pad = jnp.zeros((tokens, width - 2 * heads), jnp.bfloat16)
    gb_all[s, h] = jnp.concatenate([g_in[...], b_in[...], pad], axis=1)

    pl.semaphore_wait(barrier, ns * nh - 1)

    for dh in range(1, nh):
        pltpu.make_async_remote_copy(
            src_ref=gb_all.at[s, h],
            dst_ref=gb_all.at[s, h],
            send_sem=send_sem.at[1],
            recv_sem=gb_sem.at[0],
            device_id=(s, lax.rem(h + dh, nh)),
            device_id_type=MESH,
        ).start()
    for i, (ps, ph) in enumerate(peers):
        j = ph * ns + ps
        if i == 0:
            pltpu.make_async_copy(send.at[j], recv.at[s, h], recv_sem.at[0]).start()
        else:
            pltpu.make_async_remote_copy(
                src_ref=send.at[j],
                dst_ref=recv.at[s, h],
                send_sem=send_sem.at[0],
                recv_sem=recv_sem.at[i // nh],
                device_id=(ps, ph),
                device_id_type=MESH,
            ).start()
    head_others = gb_all.at[0, pl.ds(0, nh - 1)]
    pltpu.make_async_copy(head_others, head_others, gb_sem.at[0]).wait()
    for ps in seq_peers[1:]:
        pltpu.make_async_remote_copy(
            src_ref=gb_all.at[s],
            dst_ref=gb_all.at[s],
            send_sem=send_sem.at[5],
            recv_sem=gb_sem.at[1],
            device_id=(ps, h),
            device_id_type=MESH,
        ).start()

    row_ids = lax.broadcasted_iota(jnp.int32, (slab, slab), 0)
    col_ids = lax.broadcasted_iota(jnp.int32, (slab, slab), 1)
    strict = row_ids > col_ids
    inclusive = row_ids >= col_ids
    eye = (row_ids == col_ids).astype(jnp.float32)
    lower_ones = inclusive.astype(jnp.bfloat16)
    pick_row = lax.broadcasted_iota(jnp.int32, (width, 2 * slab), 0)
    pick_col = lax.broadcasted_iota(jnp.int32, (width, 2 * slab), 1)
    pick = (pick_row == mine + heads * (pick_col // slab)).astype(jnp.bfloat16)

    seq_others = gb_all.at[pl.ds(0, ns - 1)]
    pltpu.make_async_copy(seq_others, seq_others, gb_sem.at[1]).wait()
    all_cums, all_betas = [], []
    for at in seq_peers:
        picked = dot(gb_all[at].reshape(slab, width), pick)
        all_cums.append(dot(lower_ones, picked[:, :slab].astype(jnp.bfloat16)))
        all_betas.append(picked[:, slab:])

    for first in range(0, ns, 2):
        slabs = seq_peers[first : first + 2]
        count = len(slabs)
        cums, betas = all_cums[first : first + 2], all_betas[first : first + 2]
        for i, at in enumerate(slabs):
            pltpu.make_async_copy(recv.at[at], recv.at[at], recv_sem.at[first + i]).wait()
            pltpu.make_async_remote_copy(
                src_ref=recv.at[at, :, 0:tokens, :],
                dst_ref=swapped.at[at],
                send_sem=send_sem.at[4],
                recv_sem=swap_sem.at[first // 2],
                device_id=(seq_peers[1], h),
                device_id_type=MESH,
            ).start()
        two = swapped.at[pl.ds(0, count)]
        pltpu.make_async_copy(two, two, swap_sem.at[first // 2]).wait()

        parts = []
        for n in range(count):
            own = recv[slabs[n], :, 0:tokens, :].reshape(slab, width)
            other = swapped[slabs[n]].reshape(slab, width)
            queries, keys = jnp.where(even, own, other), jnp.where(even, other, own)
            values = recv[slabs[n], :, tokens : 2 * tokens, :].reshape(slab, width)
            cum, beta = cums[n], betas[n]
            q32, k32 = queries.astype(jnp.float32), keys.astype(jnp.float32)
            q_norm = 1.0 / jnp.sqrt(jnp.sum(q32 * q32, axis=1, keepdims=True) + 1e-06)
            k_norm = 1.0 / jnp.sqrt(jnp.sum(k32 * k32, axis=1, keepdims=True) + 1e-06)
            columns = jnp.where(col_ids == 0, cum, jnp.where(col_ids == 1, k_norm, beta))
            rows = columns.T
            cum_row, k_norm_row, beta_row = rows[0:1, :], rows[1:2, :], rows[2:3, :]
            k_turned = k32.T.astype(jnp.bfloat16)
            decay = jnp.where(inclusive, jnp.exp(jnp.where(inclusive, cum - cum_row, 0.0)), 0.0)
            decay = decay * k_norm_row
            key_key = dot(keys, k_turned)
            query_key = dot(queries, k_turned)
            lower = jnp.where(strict, (beta * k_norm) * decay * key_key, 0.0)
            scores = q_norm * decay * query_key
            parts.append((queries, keys, values, cum, k_norm, q_norm, cum_row, k_norm_row, beta_row,
                          k_turned, lower, scores, q32))

        small = 32
        same = (row_ids // small) == (col_ids // small)
        lowers = [part[10] for part in parts]
        blocks = [jnp.where(same, lower, 0.0) for lower in lowers]
        inverses = [eye - block for block in blocks]
        powers = [mul(block, block) for block in blocks]
        reach = 2
        while reach < small:
            last = reach * 2 >= small
            for n in range(count):
                right = tall(powers[n])
                if last:
                    inverses[n] = inverses[n] + fold(dot(wide(inverses[n]), right))
                else:
                    left = jnp.concatenate([wide(inverses[n]), wide(powers[n])], axis=0)
                    both_products = fold(dot(left, right))
                    inverses[n] = inverses[n] + both_products[:slab]
                    powers[n] = both_products[slab:]
            reach *= 2
        size = small
        while size < slab:
            pair = ((row_ids // (2 * size)) == (col_ids // (2 * size))) & (
                (row_ids // size) != (col_ids // size)
            )
            inner = [mul(jnp.where(pair, lowers[n], 0.0), inverses[n]) for n in range(count)]
            inverses = [inverses[n] - mul(inverses[n], inner[n]) for n in range(count)]
            size *= 2

        for n in range(count):
            (queries, keys, values, cum, k_norm, q_norm, cum_row, k_norm_row, beta_row,
             k_turned, lower, scores, q32) = parts[n]
            solve = inverses[n] * beta_row
            write_vals = dot(wide(solve), jnp.concatenate([values, values], axis=0))
            final = cum[slab - 1 : slab, :]
            key_decay = jnp.exp(final - cum) * k_norm
            key_solve = solve * (jnp.exp(cum_row) * k_norm_row)
            write_keys = dot(wide(key_solve), jnp.concatenate([keys, keys], axis=0))
            scaled = jnp.concatenate([wide(key_decay * write_keys), wide(key_decay * write_vals)], axis=1)
            moved = dot(k_turned, scaled)
            read = dot(wide(scores), tall(write_keys, write_vals))
            project = (jnp.exp(cum) * q_norm) * q32 - fold(read[:, : 2 * width])
            at = slabs[n]
            step_maps[at, :slab, :] = wide(fold(moved[:, : 2 * width]))
            step_maps[at, slab:, :] = wide(project)
            step_terms[at, :slab, :] = fold(moved[:, 2 * width :])
            step_terms[at, slab:, :] = fold(read[:, 2 * width :])
            step_decay[at, :, :] = jnp.exp(final)

    columns = pl.ds(pl.multiple_of(mine * width, width), width)
    state = None
    for n in range(ns):
        if n == 0:
            state, output = step_terms[n, :slab, :], step_terms[n, slab:, :]
        else:
            products = fold(dot(step_maps[n], tall(state)))
            output = step_terms[n, slab:, :] + products[slab:]
            state = step_decay[n] * state + step_terms[n, :slab, :] - products[:slab]
        out_buf[n * nh : (n + 1) * nh] = output.astype(jnp.bfloat16).reshape(nh, tokens, width)
        state_buf[n] = state

        @pl.when(s == n)
        def _():
            pltpu.make_async_copy(state_buf.at[n], states_ref.at[0, s], back_sem.at[1]).start()

        @pl.when(s != n)
        def _():
            pltpu.make_async_remote_copy(
                src_ref=state_buf.at[n],
                dst_ref=states_ref.at[0, s],
                send_sem=send_sem.at[3],
                recv_sem=back_sem.at[1],
                device_id=(n, h),
                device_id_type=MESH,
            ).start()

        def give(ph):
            pltpu.make_async_remote_copy(
                src_ref=out_buf.at[n * nh + ph],
                dst_ref=out_ref.at[:, columns],
                send_sem=send_sem.at[2],
                recv_sem=back_sem.at[0],
                device_id=(n, ph),
                device_id_type=MESH,
            ).start()

        for dh in range(1, nh):
            give(lax.rem(h + dh, nh))

        @pl.when(s == n)
        def _():
            pltpu.make_async_copy(
                out_buf.at[n * nh + h], out_ref.at[:, columns], back_sem.at[0]
            ).start()

        @pl.when(s != n)
        def _():
            give(h)

    others = pl.ds(0, ns * nh - 1)
    pltpu.make_async_copy(send.at[others], send.at[others], send_sem.at[0]).wait()
    pltpu.make_async_copy(head_others, head_others, send_sem.at[1]).wait()
    pltpu.make_async_copy(seq_others, seq_others, send_sem.at[5]).wait()
    pltpu.make_async_copy(out_buf.at[others], out_buf.at[others], send_sem.at[2]).wait()
    pltpu.make_async_copy(swapped, swapped, send_sem.at[4]).wait()
    rest = state_buf.at[pl.ds(0, ns - 1)]
    pltpu.make_async_copy(rest, rest, send_sem.at[3]).wait()
    pltpu.make_async_copy(out_ref, out_ref, back_sem.at[0]).wait()
    pltpu.make_async_copy(states_ref, states_ref, back_sem.at[1]).wait()


def hand_over(rows_in, states_in, rows_out, states_out, sems):
    copies = [
        pltpu.make_async_copy(rows_in, rows_out, sems.at[0]),
        pltpu.make_async_copy(states_in, states_out, sems.at[1]),
    ]
    for copy in copies:
        copy.start()
    for copy in copies:
        copy.wait()


def fast_device(query_heads, key_heads, value_heads, gate_log, beta_rate):
    ns, nh = lax.axis_size("seq"), lax.axis_size("head")
    tokens, heads, width = value_heads.shape
    key_count = key_heads.shape[1]
    sizes = (ns, nh, tokens, heads, key_count)
    bf16, f32 = jnp.bfloat16, jnp.float32
    anywhere = pl.BlockSpec(memory_space=pl.ANY)
    rows, states = pl.pallas_call(
        functools.partial(fast_kernel, sizes),
        out_shape=(
            jax.ShapeDtypeStruct((tokens, heads * width), bf16),
            jax.ShapeDtypeStruct((1, ns, width, width), f32),
        ),
        in_specs=[anywhere] * 5,
        out_specs=(anywhere, anywhere),
        scratch_shapes=[
            pltpu.VMEM((tokens, key_count, width), bf16),
            pltpu.VMEM((tokens, key_count, width), bf16),
            pltpu.VMEM((tokens, heads, width), bf16),
            pltpu.VMEM((tokens, heads), bf16),
            pltpu.VMEM((tokens, heads), bf16),
            pltpu.VMEM((tokens * key_count, width), f32),
            pltpu.VMEM((tokens * key_count, width), f32),
            pltpu.VMEM((tokens * heads, width), f32),
            pltpu.VMEM((heads, 2 * tokens, width), bf16),
            pltpu.VMEM((ns, nh, 2 * tokens, width), bf16),
            pltpu.VMEM((ns, nh, tokens, width), bf16),
            pltpu.VMEM((ns, nh, tokens, width), bf16),
            pltpu.VMEM((ns * nh, tokens, width), bf16),
            pltpu.VMEM((ns, width, width), f32),
            pltpu.VMEM((ns, 2 * width, 2 * width), bf16),
            pltpu.VMEM((ns, 2 * width, width), f32),
            pltpu.VMEM((ns, 1, width), f32),
            pltpu.SemaphoreType.DMA((5,)),
            pltpu.SemaphoreType.DMA((6,)),
            pltpu.SemaphoreType.DMA((ns,)),
            pltpu.SemaphoreType.DMA((2,)),
            pltpu.SemaphoreType.DMA((2,)),
            pltpu.SemaphoreType.DMA((ns // 2,)),
        ],
        compiler_params=pltpu.CompilerParams(
            collective_id=0, has_side_effects=True, vmem_limit_bytes=60 * 1024 * 1024
        ),
    )(query_heads, key_heads, value_heads, gate_log, beta_rate)
    return pl.pallas_call(
        hand_over,
        out_shape=(
            jax.ShapeDtypeStruct(rows.shape, bf16),
            jax.ShapeDtypeStruct(states.shape, f32),
        ),
        in_specs=[anywhere] * 2,
        out_specs=(anywhere, anywhere),
        scratch_shapes=[pltpu.SemaphoreType.DMA((2,))],
        compiler_params=pltpu.CompilerParams(vmem_limit_bytes=60 * 1024 * 1024),
    )(rows, states)


def choose_device(query_heads, key_heads, value_heads, gate_log, beta_rate):
    ns, nh = lax.axis_size("seq"), lax.axis_size("head")
    tokens, heads, width = value_heads.shape
    fits = ns * nh == heads and tokens == 16 and nh * tokens == 128
    fits = fits and width == 128 and key_heads.shape[2] == 128
    fits = fits and heads == 2 * key_heads.shape[1] and ns in (2, 4, 8) and 2 * heads < width
    run = fast_device if fits else per_device
    return run(query_heads, key_heads, value_heads, gate_log, beta_rate)


def solution(mesh):
    return jax.shard_map(
        choose_device,
        mesh=mesh,
        in_specs=(
            P(("seq", "head"), None, None),
            P(("seq", "head"), None, None),
            P(("seq", "head"), None, None),
            P(("seq", "head"), None),
            P(("seq", "head"), None),
        ),
        out_specs=(P(("seq", "head"), None), P("seq", "head", None, None)),
        check_vma=False,
    )
```

```python
import functools

import jax
import jax.numpy as jnp
from jax import lax
from jax.experimental import pallas as pl
from jax.experimental.pallas import tpu as pltpu
from jax.sharding import PartitionSpec as P

STRETCH = 64
MESH = pl.DeviceIdType.MESH


HIGHEST = lax.Precision.HIGHEST


def shifted(block, axis, distance):
    devices = range(lax.axis_size(axis))
    route = [(i - distance, i) for i in devices if i - distance in devices]
    return lax.ppermute(block, axis, route)


def normalize(tensor):
    tensor = tensor.astype(jnp.float32)
    return tensor / jnp.sqrt(jnp.sum(tensor * tensor, axis=-1, keepdims=True) + 1e-06)


def stretch_parts(queries, keys_in, values, gate_vals, beta_vals):
    span_len = gate_vals.shape[-1]
    cumulative = jnp.cumsum(gate_vals, axis=-1)
    row_ids = lax.broadcasted_iota(jnp.int32, (span_len, span_len), 0)
    columns = lax.broadcasted_iota(jnp.int32, (span_len, span_len), 1)
    strict = row_ids > columns
    inclusive = row_ids >= columns
    differ = cumulative[..., :, None] - cumulative[..., None, :]
    key_key = jnp.einsum("...rd,...sd->...rs", keys_in, keys_in, precision=HIGHEST)
    query_key = jnp.einsum("...rd,...sd->...rs", queries, keys_in, precision=HIGHEST)
    lower_triangle = jnp.where(
        strict, beta_vals[..., :, None] * jnp.exp(jnp.where(strict, differ, 0.0)) * key_key, 0.0
    )
    scores = jnp.where(inclusive, jnp.exp(jnp.where(inclusive, differ, 0.0)) * query_key, 0.0)
    identity = jnp.eye(span_len, dtype=jnp.float32)
    right_side = jnp.concatenate(
        [(beta_vals * jnp.exp(cumulative))[..., None] * keys_in, beta_vals[..., None] * values],
        axis=-1,
    )
    solved = jax.scipy.linalg.solve_triangular(
        identity + lower_triangle, right_side, lower=True, unit_diagonal=True
    )
    key_width = keys_in.shape[-1]
    last_cum = cumulative[..., -1:]
    query_dec = jnp.exp(cumulative)[..., None] * queries
    key_dec = jnp.exp(last_cum - cumulative)[..., None] * keys_in
    return (
        solved[..., :key_width],
        solved[..., key_width:],
        scores,
        query_dec,
        key_dec,
        jnp.exp(last_cum[..., 0]),
    )


def product(left_mat, right_mat):
    return jnp.einsum("...ij,...jk->...ik", left_mat, right_mat, precision=HIGHEST)


def compose(earlier, later):
    return (product(later[0], earlier[0]), product(later[0], earlier[1]) + later[1])


def slab_local(queries, keys_in, values, gate_vals, beta_vals):
    heads, length = gate_vals.shape
    blocks = length // STRETCH

    def split_rows(tensor):
        return tensor.reshape((heads, blocks, STRETCH) + tensor.shape[2:])

    write_keys, write_vals, scores, query_dec, key_dec, stretch_decay = stretch_parts(
        split_rows(queries),
        split_rows(keys_in),
        split_rows(values),
        split_rows(gate_vals),
        split_rows(beta_vals),
    )
    key_width = keys_in.shape[-1]
    identity = jnp.eye(key_width, dtype=jnp.float32)
    transit = stretch_decay[..., None, None] * identity - jnp.einsum(
        "hncd,hnce->hnde", key_dec, write_keys, precision=HIGHEST
    )
    inject = jnp.einsum("hncd,hnce->hnde", key_dec, write_vals, precision=HIGHEST)
    project = query_dec - jnp.einsum("hnrs,hnsd->hnrd", scores, write_keys, precision=HIGHEST)
    direct = jnp.einsum("hnrs,hnse->hnre", scores, write_vals, precision=HIGHEST)
    maps_all, states_all = lax.associative_scan(compose, (transit, inject), axis=1)
    reach_rest = product(project[:, 1:], maps_all[:, :-1])
    reach = jnp.concatenate([project[:, :1], reach_rest], axis=1).reshape(heads, length, key_width)
    out_rest = product(project[:, 1:], states_all[:, :-1]) + direct[:, 1:]
    local_out = jnp.concatenate([direct[:, :1], out_rest], axis=1).reshape(heads, length, -1)
    return (local_out, reach, maps_all[:, -1], states_all[:, -1])


def per_device(query_heads, key_heads, value_heads, gate_log, beta_rate):
    key_count = query_heads.shape[1]
    grouping = value_heads.shape[1] // key_count
    got_query, got_key, got_value, got_gate, got_beta = (
        lax.all_to_all(
            jnp.repeat(query_heads, grouping, axis=1),
            "head",
            split_axis=1,
            concat_axis=0,
            tiled=True,
        ),
        lax.all_to_all(
            jnp.repeat(key_heads, grouping, axis=1), "head", split_axis=1, concat_axis=0, tiled=True
        ),
        lax.all_to_all(value_heads, "head", split_axis=1, concat_axis=0, tiled=True),
        lax.all_to_all(gate_log, "head", split_axis=1, concat_axis=0, tiled=True),
        lax.all_to_all(beta_rate, "head", split_axis=1, concat_axis=0, tiled=True),
    )
    queries = jnp.swapaxes(normalize(got_query), 0, 1)
    keys_in = jnp.swapaxes(normalize(got_key), 0, 1)
    values = jnp.swapaxes(got_value.astype(jnp.float32), 0, 1)
    gate_vals = jnp.swapaxes(got_gate.astype(jnp.float32), 0, 1)
    beta_vals = jnp.swapaxes(got_beta.astype(jnp.float32), 0, 1)
    local_out, reach, slab_map, slab_state = slab_local(
        queries, keys_in, values, gate_vals, beta_vals
    )

    def advance(counter, carried):
        return shifted(product(slab_map, carried) + slab_state, "seq", 1)

    incoming = lax.fori_loop(0, lax.axis_size("seq") - 1, advance, jnp.zeros_like(slab_state))
    combined = local_out + product(reach, incoming)
    head_rows = jnp.swapaxes(combined, 0, 1).astype(jnp.bfloat16)
    flat_rows = head_rows.reshape(head_rows.shape[0], -1)
    head_output = lax.all_to_all(flat_rows, "head", split_axis=0, concat_axis=1, tiled=True)
    last_state = (product(slab_map, incoming) + slab_state)[None]
    return (head_output, last_state)


def split(matrix):
    high = matrix.astype(jnp.bfloat16)
    low = (matrix - high.astype(jnp.float32)).astype(jnp.bfloat16)
    return high, low


def dot(left, right):
    return jnp.dot(left, right, preferred_element_type=jnp.float32)


def wide(matrix):
    return jnp.concatenate(split(matrix), axis=1)


def tall(*matrices):
    row = jnp.concatenate([half for matrix in matrices for half in split(matrix)], axis=1)
    return jnp.concatenate([row, row], axis=0)


def fold(product):
    width = product.shape[1] // 2
    return product[:, :width] + product[:, width:]


def mul(left, right):
    return fold(dot(wide(left), tall(right)))


def fast_kernel(
    sizes,
    q_hbm,
    k_hbm,
    v_hbm,
    g_hbm,
    b_hbm,
    out_ref,
    states_ref,
    q_in,
    k_in,
    v_in,
    g_in,
    b_in,
    q_wide,
    k_wide,
    v_wide,
    send,
    recv,
    swapped,
    out_buf,
    state_buf,
    step_maps,
    step_terms,
    step_decay,
    load_sem,
    send_sem,
    recv_sem,
    back_sem,
    swap_sem,
):
    ns, nh, tokens, heads, key_heads = sizes
    slab = nh * tokens
    width = 128
    s = lax.axis_index("seq")
    h = lax.axis_index("head")
    mine = h * ns + s

    loads = [
        pltpu.make_async_copy(source, target, load_sem.at[i])
        for i, (source, target) in enumerate(
            [(q_hbm, q_in), (k_hbm, k_in), (v_hbm, v_in), (g_hbm, g_in), (b_hbm, b_in)]
        )
    ]
    for load in loads:
        load.start()

    peers = []
    seq_peers = [s]
    for ds in range(1, ns):
        other, bit = s, 1
        while bit <= ds:
            if ds & bit:
                other = other + bit - 2 * bit * lax.rem(s // bit, 2)
            bit *= 2
        seq_peers.append(other)
    for ps in seq_peers:
        for dh in range(nh):
            peers.append((ps, lax.rem(h + dh, nh)))
    even = lax.rem(s, 2) == 0

    barrier = pltpu.get_barrier_semaphore()
    for ps, ph in peers[1:]:
        pl.semaphore_signal(barrier, inc=1, device_id=(ps, ph), device_id_type=MESH)

    for load in loads:
        load.wait()
    q_wide[...] = q_in[...].astype(jnp.float32).reshape(tokens * key_heads, width)
    k_wide[...] = k_in[...].astype(jnp.float32).reshape(tokens * key_heads, width)
    v_wide[...] = v_in[...].astype(jnp.float32).reshape(tokens * heads, width)
    for j in range(key_heads):
        queries = q_wide[pl.ds(j, tokens, stride=key_heads), :].astype(jnp.bfloat16)
        keys = k_wide[pl.ds(j, tokens, stride=key_heads), :].astype(jnp.bfloat16)
        send[2 * j, 0:tokens, :] = queries
        send[2 * j + 1, 0:tokens, :] = keys
    for j in range(heads):
        values = v_wide[pl.ds(j, tokens, stride=heads), :].astype(jnp.bfloat16)
        send[j, tokens : 2 * tokens, :] = values
    pad = jnp.zeros((tokens, width - 2 * heads), jnp.bfloat16)
    rates = jnp.concatenate([g_in[...], b_in[...], pad], axis=1)
    for j in range(heads):
        send[j, 2 * tokens : 3 * tokens, :] = rates

    pl.semaphore_wait(barrier, ns * nh - 1)

    for i, (ps, ph) in enumerate(peers):
        j = ph * ns + ps
        if i == 0:
            pltpu.make_async_copy(send.at[j], recv.at[s, h], recv_sem.at[0]).start()
        else:
            pltpu.make_async_remote_copy(
                src_ref=send.at[j],
                dst_ref=recv.at[s, h],
                send_sem=send_sem.at[0],
                recv_sem=recv_sem.at[i // nh],
                device_id=(ps, ph),
                device_id_type=MESH,
            ).start()
    row_ids = lax.broadcasted_iota(jnp.int32, (slab, slab), 0)
    col_ids = lax.broadcasted_iota(jnp.int32, (slab, slab), 1)
    strict = row_ids > col_ids
    inclusive = row_ids >= col_ids
    eye = (row_ids == col_ids).astype(jnp.float32)
    lower_ones = inclusive.astype(jnp.bfloat16)
    pick_row = lax.broadcasted_iota(jnp.int32, (width, 2 * slab), 0)
    pick_col = lax.broadcasted_iota(jnp.int32, (width, 2 * slab), 1)
    pick = (pick_row == mine + heads * (pick_col // slab)).astype(jnp.bfloat16)

    for first in range(0, ns, 2):
        slabs = seq_peers[first : first + 2]
        count = len(slabs)
        for i, at in enumerate(slabs):
            pltpu.make_async_copy(recv.at[at], recv.at[at], recv_sem.at[first + i]).wait()
            pltpu.make_async_remote_copy(
                src_ref=recv.at[at, :, 0:tokens, :],
                dst_ref=swapped.at[at],
                send_sem=send_sem.at[4],
                recv_sem=swap_sem.at[first // 2],
                device_id=(seq_peers[1], h),
                device_id_type=MESH,
            ).start()
        two = swapped.at[pl.ds(0, count)]
        pltpu.make_async_copy(two, two, swap_sem.at[first // 2]).wait()

        parts = []
        for n in range(count):
            own = recv[slabs[n], :, 0:tokens, :].reshape(slab, width)
            other = swapped[slabs[n]].reshape(slab, width)
            queries, keys = jnp.where(even, own, other), jnp.where(even, other, own)
            values = recv[slabs[n], :, tokens : 2 * tokens, :].reshape(slab, width)
            rates = recv[slabs[n], :, 2 * tokens : 3 * tokens, :].reshape(slab, width)
            picked = dot(rates, pick)
            cum, beta = dot(lower_ones, picked[:, :slab].astype(jnp.bfloat16)), picked[:, slab:]
            q32, k32 = queries.astype(jnp.float32), keys.astype(jnp.float32)
            q_norm = 1.0 / jnp.sqrt(jnp.sum(q32 * q32, axis=1, keepdims=True) + 1e-06)
            k_norm = 1.0 / jnp.sqrt(jnp.sum(k32 * k32, axis=1, keepdims=True) + 1e-06)
            columns = jnp.where(col_ids == 0, cum, jnp.where(col_ids == 1, k_norm, beta))
            rows = columns.T
            cum_row, k_norm_row, beta_row = rows[0:1, :], rows[1:2, :], rows[2:3, :]
            k_turned = k32.T.astype(jnp.bfloat16)
            decay = jnp.where(inclusive, jnp.exp(jnp.where(inclusive, cum - cum_row, 0.0)), 0.0)
            decay = decay * k_norm_row
            key_key = dot(keys, k_turned)
            query_key = dot(queries, k_turned)
            lower = jnp.where(strict, (beta * k_norm) * decay * key_key, 0.0)
            scores = q_norm * decay * query_key
            parts.append((queries, keys, values, cum, k_norm, q_norm, cum_row, k_norm_row, beta_row,
                          k_turned, lower, scores, q32))

        small = 32
        same = (row_ids // small) == (col_ids // small)
        lowers = [part[10] for part in parts]
        blocks = [jnp.where(same, lower, 0.0) for lower in lowers]
        inverses = [eye - block for block in blocks]
        powers = [mul(block, block) for block in blocks]
        reach = 2
        while reach < small:
            last = reach * 2 >= small
            for n in range(count):
                right = tall(powers[n])
                if last:
                    inverses[n] = inverses[n] + fold(dot(wide(inverses[n]), right))
                else:
                    left = jnp.concatenate([wide(inverses[n]), wide(powers[n])], axis=0)
                    both_products = fold(dot(left, right))
                    inverses[n] = inverses[n] + both_products[:slab]
                    powers[n] = both_products[slab:]
            reach *= 2
        size = small
        while size < slab:
            pair = ((row_ids // (2 * size)) == (col_ids // (2 * size))) & (
                (row_ids // size) != (col_ids // size)
            )
            inner = [mul(jnp.where(pair, lowers[n], 0.0), inverses[n]) for n in range(count)]
            inverses = [inverses[n] - mul(inverses[n], inner[n]) for n in range(count)]
            size *= 2

        for n in range(count):
            (queries, keys, values, cum, k_norm, q_norm, cum_row, k_norm_row, beta_row,
             k_turned, lower, scores, q32) = parts[n]
            solve = inverses[n] * beta_row
            write_vals = dot(wide(solve), jnp.concatenate([values, values], axis=0))
            final = cum[slab - 1 : slab, :]
            key_decay = jnp.exp(final - cum) * k_norm
            key_solve = solve * (jnp.exp(cum_row) * k_norm_row)
            write_keys = dot(wide(key_solve), jnp.concatenate([keys, keys], axis=0))
            scaled = jnp.concatenate([wide(key_decay * write_keys), wide(key_decay * write_vals)], axis=1)
            moved = dot(k_turned, scaled)
            read = dot(wide(scores), tall(write_keys, write_vals))
            project = (jnp.exp(cum) * q_norm) * q32 - fold(read[:, : 2 * width])
            at = slabs[n]
            step_maps[at, :slab, :] = wide(fold(moved[:, : 2 * width]))
            step_maps[at, slab:, :] = wide(project)
            step_terms[at, :slab, :] = fold(moved[:, 2 * width :])
            step_terms[at, slab:, :] = fold(read[:, 2 * width :])
            step_decay[at, :, :] = jnp.exp(final)

    columns = pl.ds(pl.multiple_of(mine * width, width), width)
    state = None
    for n in range(ns):
        if n == 0:
            state, output = step_terms[n, :slab, :], step_terms[n, slab:, :]
        else:
            products = fold(dot(step_maps[n], tall(state)))
            output = step_terms[n, slab:, :] + products[slab:]
            state = step_decay[n] * state + step_terms[n, :slab, :] - products[:slab]
        out_buf[n * nh : (n + 1) * nh] = output.astype(jnp.bfloat16).reshape(nh, tokens, width)
        state_buf[n] = state

        @pl.when(s == n)
        def _():
            pltpu.make_async_copy(state_buf.at[n], states_ref.at[0, s], back_sem.at[1]).start()

        @pl.when(s != n)
        def _():
            pltpu.make_async_remote_copy(
                src_ref=state_buf.at[n],
                dst_ref=states_ref.at[0, s],
                send_sem=send_sem.at[3],
                recv_sem=back_sem.at[1],
                device_id=(n, h),
                device_id_type=MESH,
            ).start()

        def give(ph):
            pltpu.make_async_remote_copy(
                src_ref=out_buf.at[n * nh + ph],
                dst_ref=out_ref.at[:, columns],
                send_sem=send_sem.at[2],
                recv_sem=back_sem.at[0],
                device_id=(n, ph),
                device_id_type=MESH,
            ).start()

        for dh in range(1, nh):
            give(lax.rem(h + dh, nh))

        @pl.when(s == n)
        def _():
            pltpu.make_async_copy(
                out_buf.at[n * nh + h], out_ref.at[:, columns], back_sem.at[0]
            ).start()

        @pl.when(s != n)
        def _():
            give(h)

    others = pl.ds(0, ns * nh - 1)
    pltpu.make_async_copy(send.at[others], send.at[others], send_sem.at[0]).wait()
    pltpu.make_async_copy(out_buf.at[others], out_buf.at[others], send_sem.at[2]).wait()
    pltpu.make_async_copy(swapped, swapped, send_sem.at[4]).wait()
    rest = state_buf.at[pl.ds(0, ns - 1)]
    pltpu.make_async_copy(rest, rest, send_sem.at[3]).wait()
    pltpu.make_async_copy(out_ref, out_ref, back_sem.at[0]).wait()
    pltpu.make_async_copy(states_ref, states_ref, back_sem.at[1]).wait()


def fast_device(query_heads, key_heads, value_heads, gate_log, beta_rate):
    ns, nh = lax.axis_size("seq"), lax.axis_size("head")
    tokens, heads, width = value_heads.shape
    key_count = key_heads.shape[1]
    sizes = (ns, nh, tokens, heads, key_count)
    bf16, f32 = jnp.bfloat16, jnp.float32
    anywhere = pl.BlockSpec(memory_space=pl.ANY)
    return pl.pallas_call(
        functools.partial(fast_kernel, sizes),
        out_shape=(
            pltpu.VMEM((tokens, heads * width), bf16),
            pltpu.VMEM((1, ns, width, width), f32),
        ),
        in_specs=[anywhere] * 5,
        out_specs=(pl.BlockSpec(memory_space=pltpu.VMEM),) * 2,
        scratch_shapes=[
            pltpu.VMEM((tokens, key_count, width), bf16),
            pltpu.VMEM((tokens, key_count, width), bf16),
            pltpu.VMEM((tokens, heads, width), bf16),
            pltpu.VMEM((tokens, heads), bf16),
            pltpu.VMEM((tokens, heads), bf16),
            pltpu.VMEM((tokens * key_count, width), f32),
            pltpu.VMEM((tokens * key_count, width), f32),
            pltpu.VMEM((tokens * heads, width), f32),
            pltpu.VMEM((heads, 3 * tokens, width), bf16),
            pltpu.VMEM((ns, nh, 3 * tokens, width), bf16),
            pltpu.VMEM((ns, nh, tokens, width), bf16),
            pltpu.VMEM((ns * nh, tokens, width), bf16),
            pltpu.VMEM((ns, width, width), f32),
            pltpu.VMEM((ns, 2 * width, 2 * width), bf16),
            pltpu.VMEM((ns, 2 * width, width), f32),
            pltpu.VMEM((ns, 1, width), f32),
            pltpu.SemaphoreType.DMA((5,)),
            pltpu.SemaphoreType.DMA((5,)),
            pltpu.SemaphoreType.DMA((ns,)),
            pltpu.SemaphoreType.DMA((2,)),
            pltpu.SemaphoreType.DMA((ns // 2,)),
        ],
        compiler_params=pltpu.CompilerParams(
            collective_id=0, has_side_effects=True, vmem_limit_bytes=60 * 1024 * 1024
        ),
    )(query_heads, key_heads, value_heads, gate_log, beta_rate)


def choose_device(query_heads, key_heads, value_heads, gate_log, beta_rate):
    ns, nh = lax.axis_size("seq"), lax.axis_size("head")
    tokens, heads, width = value_heads.shape
    fits = ns * nh == heads and tokens == 16 and nh * tokens == 128
    fits = fits and width == 128 and key_heads.shape[2] == 128
    fits = fits and heads == 2 * key_heads.shape[1] and ns in (2, 4, 8) and 2 * heads < width
    run = fast_device if fits else per_device
    return run(query_heads, key_heads, value_heads, gate_log, beta_rate)


def solution(mesh):
    return jax.shard_map(
        choose_device,
        mesh=mesh,
        in_specs=(
            P(("seq", "head"), None, None),
            P(("seq", "head"), None, None),
            P(("seq", "head"), None, None),
            P(("seq", "head"), None),
            P(("seq", "head"), None),
        ),
        out_specs=(P(("seq", "head"), None), P("seq", "head", None, None)),
        check_vma=False,
    )
```

```python
import functools

import jax
import jax.numpy as jnp
from jax import lax
from jax.experimental import pallas as pl
from jax.experimental.pallas import tpu as pltpu
from jax.sharding import PartitionSpec as P

STRETCH = 64
MESH = pl.DeviceIdType.MESH


HIGHEST = lax.Precision.HIGHEST


def shifted(block, axis, distance):
    devices = range(lax.axis_size(axis))
    route = [(i - distance, i) for i in devices if i - distance in devices]
    return lax.ppermute(block, axis, route)


def normalize(tensor):
    tensor = tensor.astype(jnp.float32)
    return tensor / jnp.sqrt(jnp.sum(tensor * tensor, axis=-1, keepdims=True) + 1e-06)


def stretch_parts(queries, keys_in, values, gate_vals, beta_vals):
    span_len = gate_vals.shape[-1]
    cumulative = jnp.cumsum(gate_vals, axis=-1)
    row_ids = lax.broadcasted_iota(jnp.int32, (span_len, span_len), 0)
    columns = lax.broadcasted_iota(jnp.int32, (span_len, span_len), 1)
    strict = row_ids > columns
    inclusive = row_ids >= columns
    differ = cumulative[..., :, None] - cumulative[..., None, :]
    key_key = jnp.einsum("...rd,...sd->...rs", keys_in, keys_in, precision=HIGHEST)
    query_key = jnp.einsum("...rd,...sd->...rs", queries, keys_in, precision=HIGHEST)
    lower_triangle = jnp.where(
        strict, beta_vals[..., :, None] * jnp.exp(jnp.where(strict, differ, 0.0)) * key_key, 0.0
    )
    scores = jnp.where(inclusive, jnp.exp(jnp.where(inclusive, differ, 0.0)) * query_key, 0.0)
    identity = jnp.eye(span_len, dtype=jnp.float32)
    right_side = jnp.concatenate(
        [(beta_vals * jnp.exp(cumulative))[..., None] * keys_in, beta_vals[..., None] * values],
        axis=-1,
    )
    solved = jax.scipy.linalg.solve_triangular(
        identity + lower_triangle, right_side, lower=True, unit_diagonal=True
    )
    key_width = keys_in.shape[-1]
    last_cum = cumulative[..., -1:]
    query_dec = jnp.exp(cumulative)[..., None] * queries
    key_dec = jnp.exp(last_cum - cumulative)[..., None] * keys_in
    return (
        solved[..., :key_width],
        solved[..., key_width:],
        scores,
        query_dec,
        key_dec,
        jnp.exp(last_cum[..., 0]),
    )


def product(left_mat, right_mat):
    return jnp.einsum("...ij,...jk->...ik", left_mat, right_mat, precision=HIGHEST)


def compose(earlier, later):
    return (product(later[0], earlier[0]), product(later[0], earlier[1]) + later[1])


def slab_local(queries, keys_in, values, gate_vals, beta_vals):
    heads, length = gate_vals.shape
    blocks = length // STRETCH

    def split_rows(tensor):
        return tensor.reshape((heads, blocks, STRETCH) + tensor.shape[2:])

    write_keys, write_vals, scores, query_dec, key_dec, stretch_decay = stretch_parts(
        split_rows(queries),
        split_rows(keys_in),
        split_rows(values),
        split_rows(gate_vals),
        split_rows(beta_vals),
    )
    key_width = keys_in.shape[-1]
    identity = jnp.eye(key_width, dtype=jnp.float32)
    transit = stretch_decay[..., None, None] * identity - jnp.einsum(
        "hncd,hnce->hnde", key_dec, write_keys, precision=HIGHEST
    )
    inject = jnp.einsum("hncd,hnce->hnde", key_dec, write_vals, precision=HIGHEST)
    project = query_dec - jnp.einsum("hnrs,hnsd->hnrd", scores, write_keys, precision=HIGHEST)
    direct = jnp.einsum("hnrs,hnse->hnre", scores, write_vals, precision=HIGHEST)
    maps_all, states_all = lax.associative_scan(compose, (transit, inject), axis=1)
    reach_rest = product(project[:, 1:], maps_all[:, :-1])
    reach = jnp.concatenate([project[:, :1], reach_rest], axis=1).reshape(heads, length, key_width)
    out_rest = product(project[:, 1:], states_all[:, :-1]) + direct[:, 1:]
    local_out = jnp.concatenate([direct[:, :1], out_rest], axis=1).reshape(heads, length, -1)
    return (local_out, reach, maps_all[:, -1], states_all[:, -1])


def per_device(query_heads, key_heads, value_heads, gate_log, beta_rate):
    key_count = query_heads.shape[1]
    grouping = value_heads.shape[1] // key_count
    got_query, got_key, got_value, got_gate, got_beta = (
        lax.all_to_all(
            jnp.repeat(query_heads, grouping, axis=1),
            "head",
            split_axis=1,
            concat_axis=0,
            tiled=True,
        ),
        lax.all_to_all(
            jnp.repeat(key_heads, grouping, axis=1), "head", split_axis=1, concat_axis=0, tiled=True
        ),
        lax.all_to_all(value_heads, "head", split_axis=1, concat_axis=0, tiled=True),
        lax.all_to_all(gate_log, "head", split_axis=1, concat_axis=0, tiled=True),
        lax.all_to_all(beta_rate, "head", split_axis=1, concat_axis=0, tiled=True),
    )
    queries = jnp.swapaxes(normalize(got_query), 0, 1)
    keys_in = jnp.swapaxes(normalize(got_key), 0, 1)
    values = jnp.swapaxes(got_value.astype(jnp.float32), 0, 1)
    gate_vals = jnp.swapaxes(got_gate.astype(jnp.float32), 0, 1)
    beta_vals = jnp.swapaxes(got_beta.astype(jnp.float32), 0, 1)
    local_out, reach, slab_map, slab_state = slab_local(
        queries, keys_in, values, gate_vals, beta_vals
    )

    def advance(counter, carried):
        return shifted(product(slab_map, carried) + slab_state, "seq", 1)

    incoming = lax.fori_loop(0, lax.axis_size("seq") - 1, advance, jnp.zeros_like(slab_state))
    combined = local_out + product(reach, incoming)
    head_rows = jnp.swapaxes(combined, 0, 1).astype(jnp.bfloat16)
    flat_rows = head_rows.reshape(head_rows.shape[0], -1)
    head_output = lax.all_to_all(flat_rows, "head", split_axis=0, concat_axis=1, tiled=True)
    last_state = (product(slab_map, incoming) + slab_state)[None]
    return (head_output, last_state)


def split(matrix):
    high = matrix.astype(jnp.bfloat16)
    low = (matrix - high.astype(jnp.float32)).astype(jnp.bfloat16)
    return high, low


def dot(left, right):
    return jnp.dot(left, right, preferred_element_type=jnp.float32)


def wide(matrix):
    return jnp.concatenate(split(matrix), axis=1)


def tall(*matrices):
    row = jnp.concatenate([half for matrix in matrices for half in split(matrix)], axis=1)
    return jnp.concatenate([row, row], axis=0)


def fold(product):
    width = product.shape[1] // 2
    return product[:, :width] + product[:, width:]


def mul(left, right):
    return fold(dot(wide(left), tall(right)))


def fast_kernel(
    sizes,
    q_hbm,
    k_hbm,
    v_hbm,
    g_hbm,
    b_hbm,
    out_ref,
    states_ref,
    q_in,
    k_in,
    v_in,
    g_in,
    b_in,
    q_wide,
    k_wide,
    v_wide,
    send,
    gb_send,
    recv,
    swapped,
    gb_recv,
    out_buf,
    state_buf,
    step_maps,
    step_terms,
    step_decay,
    load_sem,
    send_sem,
    recv_sem,
    gb_sem,
    back_sem,
    swap_sem,
):
    ns, nh, tokens, heads, key_heads = sizes
    slab = nh * tokens
    width = 128
    s = lax.axis_index("seq")
    h = lax.axis_index("head")
    mine = h * ns + s

    loads = [
        pltpu.make_async_copy(source, target, load_sem.at[i])
        for i, (source, target) in enumerate(
            [(q_hbm, q_in), (k_hbm, k_in), (v_hbm, v_in), (g_hbm, g_in), (b_hbm, b_in)]
        )
    ]
    for load in loads:
        load.start()

    peers = []
    seq_peers = [s]
    for ds in range(1, ns):
        other, bit = s, 1
        while bit <= ds:
            if ds & bit:
                other = other + bit - 2 * bit * lax.rem(s // bit, 2)
            bit *= 2
        seq_peers.append(other)
    for ps in seq_peers:
        for dh in range(nh):
            peers.append((ps, lax.rem(h + dh, nh)))
    even = lax.rem(s, 2) == 0

    barrier = pltpu.get_barrier_semaphore()
    for ps, ph in peers[1:]:
        pl.semaphore_signal(barrier, inc=1, device_id=(ps, ph), device_id_type=MESH)

    for load in loads:
        load.wait()
    q_wide[...] = q_in[...].astype(jnp.float32).reshape(tokens * key_heads, width)
    k_wide[...] = k_in[...].astype(jnp.float32).reshape(tokens * key_heads, width)
    v_wide[...] = v_in[...].astype(jnp.float32).reshape(tokens * heads, width)
    for j in range(key_heads):
        queries = q_wide[pl.ds(j, tokens, stride=key_heads), :].astype(jnp.bfloat16)
        keys = k_wide[pl.ds(j, tokens, stride=key_heads), :].astype(jnp.bfloat16)
        send[2 * j, 0:tokens, :] = queries
        send[2 * j + 1, 0:tokens, :] = keys
    for j in range(heads):
        values = v_wide[pl.ds(j, tokens, stride=heads), :].astype(jnp.bfloat16)
        send[j, tokens : 2 * tokens, :] = values
    both = jnp.concatenate([g_in[...], b_in[...]], axis=0).astype(jnp.float32)
    place_row = lax.broadcasted_iota(jnp.int32, (2 * tokens, width), 0)
    place_col = lax.broadcasted_iota(jnp.int32, (2 * tokens, width), 1)
    place = (place_row == place_col).astype(jnp.bfloat16)
    turned = dot(both.T.astype(jnp.bfloat16), place)
    for j in range(heads):
        gb_send[j, :, :] = turned[j : j + 1, :]

    pl.semaphore_wait(barrier, ns * nh - 1)

    for i, (ps, ph) in enumerate(peers):
        j = ph * ns + ps
        if i == 0:
            pltpu.make_async_copy(send.at[j], recv.at[s, h], recv_sem.at[0]).start()
            pltpu.make_async_copy(gb_send.at[j], gb_recv.at[s, h], gb_sem.at[0]).start()
        else:
            for source, target, n, sem in ((gb_send, gb_recv, 1, gb_sem), (send, recv, 0, recv_sem)):
                pltpu.make_async_remote_copy(
                    src_ref=source.at[j],
                    dst_ref=target.at[s, h],
                    send_sem=send_sem.at[n],
                    recv_sem=sem.at[i // nh],
                    device_id=(ps, ph),
                    device_id_type=MESH,
                ).start()

    row_ids = lax.broadcasted_iota(jnp.int32, (slab, slab), 0)
    col_ids = lax.broadcasted_iota(jnp.int32, (slab, slab), 1)
    strict = row_ids > col_ids
    inclusive = row_ids >= col_ids
    eye = (row_ids == col_ids).astype(jnp.float32)
    lower_ones = inclusive.astype(jnp.bfloat16)
    all_ones = jnp.ones((slab, slab), jnp.bfloat16)
    token_at = row_ids % tokens
    expand = (
        lax.broadcasted_iota(jnp.int32, (slab, nh), 0) // tokens
        == lax.broadcasted_iota(jnp.int32, (slab, nh), 1)
    ).astype(jnp.bfloat16)

    for first in range(0, ns, 2):
        slabs = seq_peers[first : first + 2]
        count = len(slabs)
        for i, at in enumerate(slabs):
            pltpu.make_async_copy(gb_recv.at[at], gb_recv.at[at], gb_sem.at[first + i]).wait()
        cums, betas = [], []
        for at in slabs:
            rates = dot(expand, gb_recv[at, :, 0, :].astype(jnp.bfloat16))
            gates = jnp.where(col_ids == token_at, rates, 0.0).astype(jnp.bfloat16)
            writes = jnp.where(col_ids == token_at + tokens, rates, 0.0).astype(jnp.bfloat16)
            gate_cols = dot(gates, all_ones).astype(jnp.bfloat16)
            cums.append(dot(lower_ones, gate_cols))
            betas.append(dot(writes, all_ones))

        for i, at in enumerate(slabs):
            pltpu.make_async_copy(recv.at[at], recv.at[at], recv_sem.at[first + i]).wait()
            pltpu.make_async_remote_copy(
                src_ref=recv.at[at, :, 0:tokens, :],
                dst_ref=swapped.at[at],
                send_sem=send_sem.at[4],
                recv_sem=swap_sem.at[first // 2],
                device_id=(seq_peers[1], h),
                device_id_type=MESH,
            ).start()
        two = swapped.at[pl.ds(0, count)]
        pltpu.make_async_copy(two, two, swap_sem.at[first // 2]).wait()

        parts = []
        for n in range(count):
            own = recv[slabs[n], :, 0:tokens, :].reshape(slab, width)
            other = swapped[slabs[n]].reshape(slab, width)
            queries, keys = jnp.where(even, own, other), jnp.where(even, other, own)
            values = recv[slabs[n], :, tokens : 2 * tokens, :].reshape(slab, width)
            cum, beta = cums[n], betas[n]
            q32, k32 = queries.astype(jnp.float32), keys.astype(jnp.float32)
            q_norm = 1.0 / jnp.sqrt(jnp.sum(q32 * q32, axis=1, keepdims=True) + 1e-06)
            k_norm = 1.0 / jnp.sqrt(jnp.sum(k32 * k32, axis=1, keepdims=True) + 1e-06)
            columns = jnp.where(col_ids == 0, cum, jnp.where(col_ids == 1, k_norm, beta))
            rows = columns.T
            cum_row, k_norm_row, beta_row = rows[0:1, :], rows[1:2, :], rows[2:3, :]
            k_turned = k32.T.astype(jnp.bfloat16)
            decay = jnp.where(inclusive, jnp.exp(jnp.where(inclusive, cum - cum_row, 0.0)), 0.0)
            decay = decay * k_norm_row
            key_key = dot(keys, k_turned)
            query_key = dot(queries, k_turned)
            lower = jnp.where(strict, (beta * k_norm) * decay * key_key, 0.0)
            scores = q_norm * decay * query_key
            parts.append((queries, keys, values, cum, k_norm, q_norm, cum_row, k_norm_row, beta_row,
                          k_turned, lower, scores, q32))

        small = 32
        same = (row_ids // small) == (col_ids // small)
        lowers = [part[10] for part in parts]
        blocks = [jnp.where(same, lower, 0.0) for lower in lowers]
        inverses = [eye - block for block in blocks]
        powers = [mul(block, block) for block in blocks]
        reach = 2
        while reach < small:
            last = reach * 2 >= small
            for n in range(count):
                right = tall(powers[n])
                if last:
                    inverses[n] = inverses[n] + fold(dot(wide(inverses[n]), right))
                else:
                    left = jnp.concatenate([wide(inverses[n]), wide(powers[n])], axis=0)
                    both_products = fold(dot(left, right))
                    inverses[n] = inverses[n] + both_products[:slab]
                    powers[n] = both_products[slab:]
            reach *= 2
        size = small
        while size < slab:
            pair = ((row_ids // (2 * size)) == (col_ids // (2 * size))) & (
                (row_ids // size) != (col_ids // size)
            )
            inner = [mul(jnp.where(pair, lowers[n], 0.0), inverses[n]) for n in range(count)]
            inverses = [inverses[n] - mul(inverses[n], inner[n]) for n in range(count)]
            size *= 2

        for n in range(count):
            (queries, keys, values, cum, k_norm, q_norm, cum_row, k_norm_row, beta_row,
             k_turned, lower, scores, q32) = parts[n]
            solve = inverses[n] * beta_row
            write_vals = dot(wide(solve), jnp.concatenate([values, values], axis=0))
            final = cum[slab - 1 : slab, :]
            key_decay = jnp.exp(final - cum) * k_norm
            key_solve = solve * (jnp.exp(cum_row) * k_norm_row)
            write_keys = dot(wide(key_solve), jnp.concatenate([keys, keys], axis=0))
            scaled = jnp.concatenate([wide(key_decay * write_keys), wide(key_decay * write_vals)], axis=1)
            moved = dot(k_turned, scaled)
            read = dot(wide(scores), tall(write_keys, write_vals))
            project = (jnp.exp(cum) * q_norm) * q32 - fold(read[:, : 2 * width])
            at = slabs[n]
            step_maps[at, :slab, :] = wide(fold(moved[:, : 2 * width]))
            step_maps[at, slab:, :] = wide(project)
            step_terms[at, :slab, :] = fold(moved[:, 2 * width :])
            step_terms[at, slab:, :] = fold(read[:, 2 * width :])
            step_decay[at, :, :] = jnp.exp(final)

    columns = pl.ds(pl.multiple_of(mine * width, width), width)
    state = None
    for n in range(ns):
        if n == 0:
            state, output = step_terms[n, :slab, :], step_terms[n, slab:, :]
        else:
            products = fold(dot(step_maps[n], tall(state)))
            output = step_terms[n, slab:, :] + products[slab:]
            state = step_decay[n] * state + step_terms[n, :slab, :] - products[:slab]
        out_buf[n * nh : (n + 1) * nh] = output.astype(jnp.bfloat16).reshape(nh, tokens, width)
        state_buf[n] = state

        @pl.when(s == n)
        def _():
            pltpu.make_async_copy(state_buf.at[n], states_ref.at[0, s], back_sem.at[1]).start()

        @pl.when(s != n)
        def _():
            pltpu.make_async_remote_copy(
                src_ref=state_buf.at[n],
                dst_ref=states_ref.at[0, s],
                send_sem=send_sem.at[3],
                recv_sem=back_sem.at[1],
                device_id=(n, h),
                device_id_type=MESH,
            ).start()

        def give(ph):
            pltpu.make_async_remote_copy(
                src_ref=out_buf.at[n * nh + ph],
                dst_ref=out_ref.at[:, columns],
                send_sem=send_sem.at[2],
                recv_sem=back_sem.at[0],
                device_id=(n, ph),
                device_id_type=MESH,
            ).start()

        for dh in range(1, nh):
            give(lax.rem(h + dh, nh))

        @pl.when(s == n)
        def _():
            pltpu.make_async_copy(
                out_buf.at[n * nh + h], out_ref.at[:, columns], back_sem.at[0]
            ).start()

        @pl.when(s != n)
        def _():
            give(h)

    others = pl.ds(0, ns * nh - 1)
    pltpu.make_async_copy(send.at[others], send.at[others], send_sem.at[0]).wait()
    pltpu.make_async_copy(gb_send.at[others], gb_send.at[others], send_sem.at[1]).wait()
    pltpu.make_async_copy(out_buf.at[others], out_buf.at[others], send_sem.at[2]).wait()
    pltpu.make_async_copy(swapped, swapped, send_sem.at[4]).wait()
    rest = state_buf.at[pl.ds(0, ns - 1)]
    pltpu.make_async_copy(rest, rest, send_sem.at[3]).wait()
    pltpu.make_async_copy(out_ref, out_ref, back_sem.at[0]).wait()
    pltpu.make_async_copy(states_ref, states_ref, back_sem.at[1]).wait()


def hand_over(rows_in, states_in, rows_out, states_out, sems):
    copies = [
        pltpu.make_async_copy(rows_in, rows_out, sems.at[0]),
        pltpu.make_async_copy(states_in, states_out, sems.at[1]),
    ]
    for copy in copies:
        copy.start()
    for copy in copies:
        copy.wait()


def fast_device(query_heads, key_heads, value_heads, gate_log, beta_rate):
    ns, nh = lax.axis_size("seq"), lax.axis_size("head")
    tokens, heads, width = value_heads.shape
    key_count = key_heads.shape[1]
    sizes = (ns, nh, tokens, heads, key_count)
    bf16, f32 = jnp.bfloat16, jnp.float32
    anywhere = pl.BlockSpec(memory_space=pl.ANY)
    vmem = pl.BlockSpec(memory_space=pltpu.VMEM)
    rows, states = pl.pallas_call(
        functools.partial(fast_kernel, sizes),
        out_shape=(
            pltpu.VMEM((tokens, heads * width), bf16),
            pltpu.VMEM((1, ns, width, width), f32),
        ),
        in_specs=[anywhere] * 5,
        out_specs=(vmem, vmem),
        scratch_shapes=[
            pltpu.VMEM((tokens, key_count, width), bf16),
            pltpu.VMEM((tokens, key_count, width), bf16),
            pltpu.VMEM((tokens, heads, width), bf16),
            pltpu.VMEM((tokens, heads), bf16),
            pltpu.VMEM((tokens, heads), bf16),
            pltpu.VMEM((tokens * key_count, width), f32),
            pltpu.VMEM((tokens * key_count, width), f32),
            pltpu.VMEM((tokens * heads, width), f32),
            pltpu.VMEM((heads, 2 * tokens, width), bf16),
            pltpu.VMEM((heads, 1, width), f32),
            pltpu.VMEM((ns, nh, 2 * tokens, width), bf16),
            pltpu.VMEM((ns, nh, tokens, width), bf16),
            pltpu.VMEM((ns, nh, 1, width), f32),
            pltpu.VMEM((ns * nh, tokens, width), bf16),
            pltpu.VMEM((ns, width, width), f32),
            pltpu.VMEM((ns, 2 * width, 2 * width), bf16),
            pltpu.VMEM((ns, 2 * width, width), f32),
            pltpu.VMEM((ns, 1, width), f32),
            pltpu.SemaphoreType.DMA((5,)),
            pltpu.SemaphoreType.DMA((5,)),
            pltpu.SemaphoreType.DMA((ns,)),
            pltpu.SemaphoreType.DMA((ns,)),
            pltpu.SemaphoreType.DMA((2,)),
            pltpu.SemaphoreType.DMA((ns // 2,)),
        ],
        compiler_params=pltpu.CompilerParams(
            collective_id=0, has_side_effects=True, vmem_limit_bytes=60 * 1024 * 1024
        ),
    )(query_heads, key_heads, value_heads, gate_log, beta_rate)
    return pl.pallas_call(
        hand_over,
        out_shape=(
            jax.ShapeDtypeStruct(rows.shape, bf16),
            jax.ShapeDtypeStruct(states.shape, f32),
        ),
        in_specs=[vmem] * 2,
        out_specs=(anywhere, anywhere),
        scratch_shapes=[pltpu.SemaphoreType.DMA((2,))],
    )(rows, states)


def choose_device(query_heads, key_heads, value_heads, gate_log, beta_rate):
    ns, nh = lax.axis_size("seq"), lax.axis_size("head")
    tokens, heads, width = value_heads.shape
    fits = ns * nh == heads and tokens == 16 and nh * tokens == 128
    fits = fits and width == 128 and key_heads.shape[2] == 128
    fits = fits and heads == 2 * key_heads.shape[1] and ns in (2, 4, 8)
    run = fast_device if fits else per_device
    return run(query_heads, key_heads, value_heads, gate_log, beta_rate)


def solution(mesh):
    return jax.shard_map(
        choose_device,
        mesh=mesh,
        in_specs=(
            P(("seq", "head"), None, None),
            P(("seq", "head"), None, None),
            P(("seq", "head"), None, None),
            P(("seq", "head"), None),
            P(("seq", "head"), None),
        ),
        out_specs=(P(("seq", "head"), None), P("seq", "head", None, None)),
        check_vma=False,
    )
```

```python
import functools

import jax
import jax.numpy as jnp
from jax import lax
from jax.experimental import pallas as pl
from jax.experimental.pallas import tpu as pltpu
from jax.sharding import PartitionSpec as P

STRETCH = 64
MESH = pl.DeviceIdType.MESH


HIGHEST = lax.Precision.HIGHEST


def shifted(block, axis, distance):
    devices = range(lax.axis_size(axis))
    route = [(i - distance, i) for i in devices if i - distance in devices]
    return lax.ppermute(block, axis, route)


def normalize(tensor):
    tensor = tensor.astype(jnp.float32)
    return tensor / jnp.sqrt(jnp.sum(tensor * tensor, axis=-1, keepdims=True) + 1e-06)


def stretch_parts(queries, keys_in, values, gate_vals, beta_vals):
    span_len = gate_vals.shape[-1]
    cumulative = jnp.cumsum(gate_vals, axis=-1)
    row_ids = lax.broadcasted_iota(jnp.int32, (span_len, span_len), 0)
    columns = lax.broadcasted_iota(jnp.int32, (span_len, span_len), 1)
    strict = row_ids > columns
    inclusive = row_ids >= columns
    differ = cumulative[..., :, None] - cumulative[..., None, :]
    key_key = jnp.einsum("...rd,...sd->...rs", keys_in, keys_in, precision=HIGHEST)
    query_key = jnp.einsum("...rd,...sd->...rs", queries, keys_in, precision=HIGHEST)
    lower_triangle = jnp.where(
        strict, beta_vals[..., :, None] * jnp.exp(jnp.where(strict, differ, 0.0)) * key_key, 0.0
    )
    scores = jnp.where(inclusive, jnp.exp(jnp.where(inclusive, differ, 0.0)) * query_key, 0.0)
    identity = jnp.eye(span_len, dtype=jnp.float32)
    right_side = jnp.concatenate(
        [(beta_vals * jnp.exp(cumulative))[..., None] * keys_in, beta_vals[..., None] * values],
        axis=-1,
    )
    solved = jax.scipy.linalg.solve_triangular(
        identity + lower_triangle, right_side, lower=True, unit_diagonal=True
    )
    key_width = keys_in.shape[-1]
    last_cum = cumulative[..., -1:]
    query_dec = jnp.exp(cumulative)[..., None] * queries
    key_dec = jnp.exp(last_cum - cumulative)[..., None] * keys_in
    return (
        solved[..., :key_width],
        solved[..., key_width:],
        scores,
        query_dec,
        key_dec,
        jnp.exp(last_cum[..., 0]),
    )


def product(left_mat, right_mat):
    return jnp.einsum("...ij,...jk->...ik", left_mat, right_mat, precision=HIGHEST)


def compose(earlier, later):
    return (product(later[0], earlier[0]), product(later[0], earlier[1]) + later[1])


def slab_local(queries, keys_in, values, gate_vals, beta_vals):
    heads, length = gate_vals.shape
    blocks = length // STRETCH

    def split_rows(tensor):
        return tensor.reshape((heads, blocks, STRETCH) + tensor.shape[2:])

    write_keys, write_vals, scores, query_dec, key_dec, stretch_decay = stretch_parts(
        split_rows(queries),
        split_rows(keys_in),
        split_rows(values),
        split_rows(gate_vals),
        split_rows(beta_vals),
    )
    key_width = keys_in.shape[-1]
    identity = jnp.eye(key_width, dtype=jnp.float32)
    transit = stretch_decay[..., None, None] * identity - jnp.einsum(
        "hncd,hnce->hnde", key_dec, write_keys, precision=HIGHEST
    )
    inject = jnp.einsum("hncd,hnce->hnde", key_dec, write_vals, precision=HIGHEST)
    project = query_dec - jnp.einsum("hnrs,hnsd->hnrd", scores, write_keys, precision=HIGHEST)
    direct = jnp.einsum("hnrs,hnse->hnre", scores, write_vals, precision=HIGHEST)
    maps_all, states_all = lax.associative_scan(compose, (transit, inject), axis=1)
    reach_rest = product(project[:, 1:], maps_all[:, :-1])
    reach = jnp.concatenate([project[:, :1], reach_rest], axis=1).reshape(heads, length, key_width)
    out_rest = product(project[:, 1:], states_all[:, :-1]) + direct[:, 1:]
    local_out = jnp.concatenate([direct[:, :1], out_rest], axis=1).reshape(heads, length, -1)
    return (local_out, reach, maps_all[:, -1], states_all[:, -1])


def per_device(query_heads, key_heads, value_heads, gate_log, beta_rate):
    key_count = query_heads.shape[1]
    grouping = value_heads.shape[1] // key_count
    got_query, got_key, got_value, got_gate, got_beta = (
        lax.all_to_all(
            jnp.repeat(query_heads, grouping, axis=1),
            "head",
            split_axis=1,
            concat_axis=0,
            tiled=True,
        ),
        lax.all_to_all(
            jnp.repeat(key_heads, grouping, axis=1), "head", split_axis=1, concat_axis=0, tiled=True
        ),
        lax.all_to_all(value_heads, "head", split_axis=1, concat_axis=0, tiled=True),
        lax.all_to_all(gate_log, "head", split_axis=1, concat_axis=0, tiled=True),
        lax.all_to_all(beta_rate, "head", split_axis=1, concat_axis=0, tiled=True),
    )
    queries = jnp.swapaxes(normalize(got_query), 0, 1)
    keys_in = jnp.swapaxes(normalize(got_key), 0, 1)
    values = jnp.swapaxes(got_value.astype(jnp.float32), 0, 1)
    gate_vals = jnp.swapaxes(got_gate.astype(jnp.float32), 0, 1)
    beta_vals = jnp.swapaxes(got_beta.astype(jnp.float32), 0, 1)
    local_out, reach, slab_map, slab_state = slab_local(
        queries, keys_in, values, gate_vals, beta_vals
    )

    def advance(counter, carried):
        return shifted(product(slab_map, carried) + slab_state, "seq", 1)

    incoming = lax.fori_loop(0, lax.axis_size("seq") - 1, advance, jnp.zeros_like(slab_state))
    combined = local_out + product(reach, incoming)
    head_rows = jnp.swapaxes(combined, 0, 1).astype(jnp.bfloat16)
    flat_rows = head_rows.reshape(head_rows.shape[0], -1)
    head_output = lax.all_to_all(flat_rows, "head", split_axis=0, concat_axis=1, tiled=True)
    last_state = (product(slab_map, incoming) + slab_state)[None]
    return (head_output, last_state)


def split(matrix):
    high = matrix.astype(jnp.bfloat16)
    low = (matrix - high.astype(jnp.float32)).astype(jnp.bfloat16)
    return high, low


def dot(left, right):
    return jnp.dot(left, right, preferred_element_type=jnp.float32)


def wide(matrix):
    return jnp.concatenate(split(matrix), axis=1)


def tall(*matrices):
    row = jnp.concatenate([half for matrix in matrices for half in split(matrix)], axis=1)
    return jnp.concatenate([row, row], axis=0)


def fold(product):
    width = product.shape[1] // 2
    return product[:, :width] + product[:, width:]


def mul(left, right):
    return fold(dot(wide(left), tall(right)))


def fast_kernel(
    sizes,
    q_hbm,
    k_hbm,
    v_hbm,
    g_hbm,
    b_hbm,
    out_ref,
    states_ref,
    q_in,
    k_in,
    v_in,
    g_in,
    b_in,
    q_wide,
    k_wide,
    v_wide,
    send,
    gb_send,
    recv,
    swapped,
    gb_recv,
    out_buf,
    state_buf,
    step_maps,
    step_terms,
    step_decay,
    load_sem,
    send_sem,
    recv_sem,
    gb_sem,
    back_sem,
    swap_sem,
):
    ns, nh, tokens, heads, key_heads = sizes
    slab = nh * tokens
    width = 128
    s = lax.axis_index("seq")
    h = lax.axis_index("head")
    mine = h * ns + s

    loads = [
        pltpu.make_async_copy(source, target, load_sem.at[i])
        for i, (source, target) in enumerate(
            [(q_hbm, q_in), (k_hbm, k_in), (v_hbm, v_in), (g_hbm, g_in), (b_hbm, b_in)]
        )
    ]
    for load in loads:
        load.start()

    peers = []
    seq_peers = [s]
    for ds in range(1, ns):
        other, bit = s, 1
        while bit <= ds:
            if ds & bit:
                other = other + bit - 2 * bit * lax.rem(s // bit, 2)
            bit *= 2
        seq_peers.append(other)
    for ps in seq_peers:
        for dh in range(nh):
            peers.append((ps, lax.rem(h + dh, nh)))
    even = lax.rem(s, 2) == 0

    barrier = pltpu.get_barrier_semaphore()
    for ps, ph in peers[1:]:
        pl.semaphore_signal(barrier, inc=1, device_id=(ps, ph), device_id_type=MESH)

    loads[0].wait()
    q_wide[...] = q_in[...].astype(jnp.float32).reshape(tokens * key_heads, width)
    loads[1].wait()
    k_wide[...] = k_in[...].astype(jnp.float32).reshape(tokens * key_heads, width)
    for j in range(key_heads):
        queries = q_wide[pl.ds(j, tokens, stride=key_heads), :].astype(jnp.bfloat16)
        keys = k_wide[pl.ds(j, tokens, stride=key_heads), :].astype(jnp.bfloat16)
        send[2 * j, 0:tokens, :] = queries
        send[2 * j + 1, 0:tokens, :] = keys
    loads[2].wait()
    v_wide[...] = v_in[...].astype(jnp.float32).reshape(tokens * heads, width)
    for j in range(heads):
        values = v_wide[pl.ds(j, tokens, stride=heads), :].astype(jnp.bfloat16)
        send[j, tokens : 2 * tokens, :] = values
    loads[3].wait()
    loads[4].wait()
    both = jnp.concatenate([g_in[...], b_in[...]], axis=0).astype(jnp.float32)
    place_row = lax.broadcasted_iota(jnp.int32, (2 * tokens, width), 0)
    place_col = lax.broadcasted_iota(jnp.int32, (2 * tokens, width), 1)
    place = (place_row == place_col).astype(jnp.bfloat16)
    turned = dot(both.T.astype(jnp.bfloat16), place)
    for j in range(heads):
        gb_send[j, :, :] = turned[j : j + 1, :]

    pl.semaphore_wait(barrier, ns * nh - 1)

    def remote(source, target, n, sem, i):
        ps, ph = peers[i]
        pltpu.make_async_remote_copy(
            src_ref=source.at[ph * ns + ps],
            dst_ref=target.at[s, h],
            send_sem=send_sem.at[n],
            recv_sem=sem.at[i // nh],
            device_id=(ps, ph),
            device_id_type=MESH,
        ).start()

    pltpu.make_async_copy(send.at[mine], recv.at[s, h], recv_sem.at[0]).start()
    pltpu.make_async_copy(gb_send.at[mine], gb_recv.at[s, h], gb_sem.at[0]).start()
    for i in range(1, ns * nh):
        for row in (2 * i - 1, 2 * i):
            if row < ns * nh:
                remote(gb_send, gb_recv, 1, gb_sem, row)
        remote(send, recv, 0, recv_sem, i)

    row_ids = lax.broadcasted_iota(jnp.int32, (slab, slab), 0)
    col_ids = lax.broadcasted_iota(jnp.int32, (slab, slab), 1)
    strict = row_ids > col_ids
    inclusive = row_ids >= col_ids
    eye = (row_ids == col_ids).astype(jnp.float32)
    lower_ones = inclusive.astype(jnp.bfloat16)
    all_ones = jnp.ones((slab, slab), jnp.bfloat16)
    token_at = row_ids % tokens
    expand = (
        lax.broadcasted_iota(jnp.int32, (slab, nh), 0) // tokens
        == lax.broadcasted_iota(jnp.int32, (slab, nh), 1)
    ).astype(jnp.bfloat16)

    for i, at in enumerate(seq_peers):
        pltpu.make_async_copy(gb_recv.at[at], gb_recv.at[at], gb_sem.at[i]).wait()
    all_cums, all_betas = [], []
    for at in seq_peers:
        rates = dot(expand, gb_recv[at, :, 0, :].astype(jnp.bfloat16))
        gates = jnp.where(col_ids == token_at, rates, 0.0).astype(jnp.bfloat16)
        writes = jnp.where(col_ids == token_at + tokens, rates, 0.0).astype(jnp.bfloat16)
        gate_cols = dot(gates, all_ones).astype(jnp.bfloat16)
        all_cums.append(dot(lower_ones, gate_cols))
        all_betas.append(dot(writes, all_ones))

    for first in range(0, ns, 2):
        slabs = seq_peers[first : first + 2]
        count = len(slabs)
        cums, betas = all_cums[first : first + 2], all_betas[first : first + 2]
        for i, at in enumerate(slabs):
            pltpu.make_async_copy(recv.at[at], recv.at[at], recv_sem.at[first + i]).wait()
            pltpu.make_async_remote_copy(
                src_ref=recv.at[at, :, 0:tokens, :],
                dst_ref=swapped.at[at],
                send_sem=send_sem.at[4],
                recv_sem=swap_sem.at[first // 2],
                device_id=(seq_peers[1], h),
                device_id_type=MESH,
            ).start()
        two = swapped.at[pl.ds(0, count)]
        pltpu.make_async_copy(two, two, swap_sem.at[first // 2]).wait()

        parts = []
        for n in range(count):
            own = recv[slabs[n], :, 0:tokens, :].reshape(slab, width)
            other = swapped[slabs[n]].reshape(slab, width)
            queries, keys = jnp.where(even, own, other), jnp.where(even, other, own)
            values = recv[slabs[n], :, tokens : 2 * tokens, :].reshape(slab, width)
            cum, beta = cums[n], betas[n]
            q32, k32 = queries.astype(jnp.float32), keys.astype(jnp.float32)
            q_norm = 1.0 / jnp.sqrt(jnp.sum(q32 * q32, axis=1, keepdims=True) + 1e-06)
            k_norm = 1.0 / jnp.sqrt(jnp.sum(k32 * k32, axis=1, keepdims=True) + 1e-06)
            columns = jnp.where(col_ids == 0, cum, jnp.where(col_ids == 1, k_norm, beta))
            rows = columns.T
            cum_row, k_norm_row, beta_row = rows[0:1, :], rows[1:2, :], rows[2:3, :]
            k_turned = k32.T.astype(jnp.bfloat16)
            decay = jnp.where(inclusive, jnp.exp(jnp.where(inclusive, cum - cum_row, 0.0)), 0.0)
            decay = decay * k_norm_row
            key_key = dot(keys, k_turned)
            query_key = dot(queries, k_turned)
            lower = jnp.where(strict, (beta * k_norm) * decay * key_key, 0.0)
            scores = q_norm * decay * query_key
            parts.append((queries, keys, values, cum, k_norm, q_norm, cum_row, k_norm_row, beta_row,
                          k_turned, lower, scores, q32))

        small = 32
        same = (row_ids // small) == (col_ids // small)
        lowers = [part[10] for part in parts]
        blocks = [jnp.where(same, lower, 0.0) for lower in lowers]
        inverses = [eye - block for block in blocks]
        powers = [mul(block, block) for block in blocks]
        reach = 2
        while reach < small:
            last = reach * 2 >= small
            for n in range(count):
                right = tall(powers[n])
                if last:
                    inverses[n] = inverses[n] + fold(dot(wide(inverses[n]), right))
                else:
                    left = jnp.concatenate([wide(inverses[n]), wide(powers[n])], axis=0)
                    both_products = fold(dot(left, right))
                    inverses[n] = inverses[n] + both_products[:slab]
                    powers[n] = both_products[slab:]
            reach *= 2
        steps = [mul(inverses[n], jnp.where(same, 0.0, lowers[n])) for n in range(count)]
        squares = [mul(steps[n], steps[n]) for n in range(count)]
        inverses = [inverses[n] - mul(steps[n], inverses[n]) for n in range(count)]
        inverses = [inverses[n] + mul(squares[n], inverses[n]) for n in range(count)]

        for n in range(count):
            (queries, keys, values, cum, k_norm, q_norm, cum_row, k_norm_row, beta_row,
             k_turned, lower, scores, q32) = parts[n]
            solve = inverses[n] * beta_row
            write_vals = dot(wide(solve), jnp.concatenate([values, values], axis=0))
            final = cum[slab - 1 : slab, :]
            key_decay = jnp.exp(final - cum) * k_norm
            key_solve = solve * (jnp.exp(cum_row) * k_norm_row)
            write_keys = dot(wide(key_solve), jnp.concatenate([keys, keys], axis=0))
            scaled = jnp.concatenate([wide(key_decay * write_keys), wide(key_decay * write_vals)], axis=1)
            moved = dot(k_turned, scaled)
            read = dot(wide(scores), tall(write_keys, write_vals))
            project = (jnp.exp(cum) * q_norm) * q32 - fold(read[:, : 2 * width])
            at = slabs[n]
            step_maps[at, :slab, :] = wide(fold(moved[:, : 2 * width]))
            step_maps[at, slab:, :] = wide(project)
            step_terms[at, :slab, :] = fold(moved[:, 2 * width :])
            step_terms[at, slab:, :] = fold(read[:, 2 * width :])
            step_decay[at, :, :] = jnp.exp(final)

    columns = pl.ds(pl.multiple_of(mine * width, width), width)
    state = None
    for n in range(ns):
        if n == 0:
            state, output = step_terms[n, :slab, :], step_terms[n, slab:, :]
        else:
            products = fold(dot(step_maps[n], tall(state)))
            output = step_terms[n, slab:, :] + products[slab:]
            state = step_decay[n] * state + step_terms[n, :slab, :] - products[:slab]
        out_buf[n * nh : (n + 1) * nh] = output.astype(jnp.bfloat16).reshape(nh, tokens, width)
        state_buf[n] = state

        @pl.when(s == n)
        def _():
            pltpu.make_async_copy(state_buf.at[n], states_ref.at[0, s], back_sem.at[1]).start()

        @pl.when(s != n)
        def _():
            pltpu.make_async_remote_copy(
                src_ref=state_buf.at[n],
                dst_ref=states_ref.at[0, s],
                send_sem=send_sem.at[3],
                recv_sem=back_sem.at[1],
                device_id=(n, h),
                device_id_type=MESH,
            ).start()

        def give(ph):
            pltpu.make_async_remote_copy(
                src_ref=out_buf.at[n * nh + ph],
                dst_ref=out_ref.at[:, columns],
                send_sem=send_sem.at[2],
                recv_sem=back_sem.at[0],
                device_id=(n, ph),
                device_id_type=MESH,
            ).start()

        for dh in range(1, nh):
            give(lax.rem(h + dh, nh))

        @pl.when(s == n)
        def _():
            pltpu.make_async_copy(
                out_buf.at[n * nh + h], out_ref.at[:, columns], back_sem.at[0]
            ).start()

        @pl.when(s != n)
        def _():
            give(h)

    others = pl.ds(0, ns * nh - 1)
    pltpu.make_async_copy(send.at[others], send.at[others], send_sem.at[0]).wait()
    pltpu.make_async_copy(gb_send.at[others], gb_send.at[others], send_sem.at[1]).wait()
    pltpu.make_async_copy(out_buf.at[others], out_buf.at[others], send_sem.at[2]).wait()
    pltpu.make_async_copy(swapped, swapped, send_sem.at[4]).wait()
    rest = state_buf.at[pl.ds(0, ns - 1)]
    pltpu.make_async_copy(rest, rest, send_sem.at[3]).wait()
    pltpu.make_async_copy(out_ref, out_ref, back_sem.at[0]).wait()
    pltpu.make_async_copy(states_ref, states_ref, back_sem.at[1]).wait()


def fast_device(query_heads, key_heads, value_heads, gate_log, beta_rate):
    ns, nh = lax.axis_size("seq"), lax.axis_size("head")
    tokens, heads, width = value_heads.shape
    key_count = key_heads.shape[1]
    sizes = (ns, nh, tokens, heads, key_count)
    bf16, f32 = jnp.bfloat16, jnp.float32
    anywhere = pl.BlockSpec(memory_space=pl.ANY)
    vmem = pl.BlockSpec(memory_space=pltpu.VMEM)
    return pl.pallas_call(
        functools.partial(fast_kernel, sizes),
        out_shape=(
            pltpu.VMEM((tokens, heads * width), bf16),
            pltpu.VMEM((1, ns, width, width), f32),
        ),
        in_specs=[anywhere] * 5,
        out_specs=(vmem, vmem),
        scratch_shapes=[
            pltpu.VMEM((tokens, key_count, width), bf16),
            pltpu.VMEM((tokens, key_count, width), bf16),
            pltpu.VMEM((tokens, heads, width), bf16),
            pltpu.VMEM((tokens, heads), bf16),
            pltpu.VMEM((tokens, heads), bf16),
            pltpu.VMEM((tokens * key_count, width), f32),
            pltpu.VMEM((tokens * key_count, width), f32),
            pltpu.VMEM((tokens * heads, width), f32),
            pltpu.VMEM((heads, 2 * tokens, width), bf16),
            pltpu.VMEM((heads, 1, width), f32),
            pltpu.VMEM((ns, nh, 2 * tokens, width), bf16),
            pltpu.VMEM((ns, nh, tokens, width), bf16),
            pltpu.VMEM((ns, nh, 1, width), f32),
            pltpu.VMEM((ns * nh, tokens, width), bf16),
            pltpu.VMEM((ns, width, width), f32),
            pltpu.VMEM((ns, 2 * width, 2 * width), bf16),
            pltpu.VMEM((ns, 2 * width, width), f32),
            pltpu.VMEM((ns, 1, width), f32),
            pltpu.SemaphoreType.DMA((5,)),
            pltpu.SemaphoreType.DMA((5,)),
            pltpu.SemaphoreType.DMA((ns,)),
            pltpu.SemaphoreType.DMA((ns,)),
            pltpu.SemaphoreType.DMA((2,)),
            pltpu.SemaphoreType.DMA((ns // 2,)),
        ],
        compiler_params=pltpu.CompilerParams(
            collective_id=0, has_side_effects=True, vmem_limit_bytes=60 * 1024 * 1024
        ),
    )(query_heads, key_heads, value_heads, gate_log, beta_rate)


def choose_device(query_heads, key_heads, value_heads, gate_log, beta_rate):
    ns, nh = lax.axis_size("seq"), lax.axis_size("head")
    tokens, heads, width = value_heads.shape
    fits = ns * nh == heads and tokens == 16 and nh * tokens == 128
    fits = fits and width == 128 and key_heads.shape[2] == 128
    fits = fits and heads == 2 * key_heads.shape[1] and ns in (2, 4, 8)
    run = fast_device if fits else per_device
    return run(query_heads, key_heads, value_heads, gate_log, beta_rate)


def solution(mesh):
    return jax.shard_map(
        choose_device,
        mesh=mesh,
        in_specs=(
            P(("seq", "head"), None, None),
            P(("seq", "head"), None, None),
            P(("seq", "head"), None, None),
            P(("seq", "head"), None),
            P(("seq", "head"), None),
        ),
        out_specs=(P(("seq", "head"), None), P("seq", "head", None, None)),
        check_vma=False,
    )
```

```python
import functools

import jax
import jax.numpy as jnp
from jax import lax
from jax.experimental import pallas as pl
from jax.experimental.pallas import tpu as pltpu
from jax.sharding import PartitionSpec as P

STRETCH = 64
MESH = pl.DeviceIdType.MESH


HIGHEST = lax.Precision.HIGHEST


def shifted(block, axis, distance):
    devices = range(lax.axis_size(axis))
    route = [(i - distance, i) for i in devices if i - distance in devices]
    return lax.ppermute(block, axis, route)


def normalize(tensor):
    tensor = tensor.astype(jnp.float32)
    return tensor / jnp.sqrt(jnp.sum(tensor * tensor, axis=-1, keepdims=True) + 1e-06)


def stretch_parts(queries, keys_in, values, gate_vals, beta_vals):
    span_len = gate_vals.shape[-1]
    cumulative = jnp.cumsum(gate_vals, axis=-1)
    row_ids = lax.broadcasted_iota(jnp.int32, (span_len, span_len), 0)
    columns = lax.broadcasted_iota(jnp.int32, (span_len, span_len), 1)
    strict = row_ids > columns
    inclusive = row_ids >= columns
    differ = cumulative[..., :, None] - cumulative[..., None, :]
    key_key = jnp.einsum("...rd,...sd->...rs", keys_in, keys_in, precision=HIGHEST)
    query_key = jnp.einsum("...rd,...sd->...rs", queries, keys_in, precision=HIGHEST)
    lower_triangle = jnp.where(
        strict, beta_vals[..., :, None] * jnp.exp(jnp.where(strict, differ, 0.0)) * key_key, 0.0
    )
    scores = jnp.where(inclusive, jnp.exp(jnp.where(inclusive, differ, 0.0)) * query_key, 0.0)
    identity = jnp.eye(span_len, dtype=jnp.float32)
    right_side = jnp.concatenate(
        [(beta_vals * jnp.exp(cumulative))[..., None] * keys_in, beta_vals[..., None] * values],
        axis=-1,
    )
    solved = jax.scipy.linalg.solve_triangular(
        identity + lower_triangle, right_side, lower=True, unit_diagonal=True
    )
    key_width = keys_in.shape[-1]
    last_cum = cumulative[..., -1:]
    query_dec = jnp.exp(cumulative)[..., None] * queries
    key_dec = jnp.exp(last_cum - cumulative)[..., None] * keys_in
    return (
        solved[..., :key_width],
        solved[..., key_width:],
        scores,
        query_dec,
        key_dec,
        jnp.exp(last_cum[..., 0]),
    )


def product(left_mat, right_mat):
    return jnp.einsum("...ij,...jk->...ik", left_mat, right_mat, precision=HIGHEST)


def compose(earlier, later):
    return (product(later[0], earlier[0]), product(later[0], earlier[1]) + later[1])


def slab_local(queries, keys_in, values, gate_vals, beta_vals):
    heads, length = gate_vals.shape
    blocks = length // STRETCH

    def split_rows(tensor):
        return tensor.reshape((heads, blocks, STRETCH) + tensor.shape[2:])

    write_keys, write_vals, scores, query_dec, key_dec, stretch_decay = stretch_parts(
        split_rows(queries),
        split_rows(keys_in),
        split_rows(values),
        split_rows(gate_vals),
        split_rows(beta_vals),
    )
    key_width = keys_in.shape[-1]
    identity = jnp.eye(key_width, dtype=jnp.float32)
    transit = stretch_decay[..., None, None] * identity - jnp.einsum(
        "hncd,hnce->hnde", key_dec, write_keys, precision=HIGHEST
    )
    inject = jnp.einsum("hncd,hnce->hnde", key_dec, write_vals, precision=HIGHEST)
    project = query_dec - jnp.einsum("hnrs,hnsd->hnrd", scores, write_keys, precision=HIGHEST)
    direct = jnp.einsum("hnrs,hnse->hnre", scores, write_vals, precision=HIGHEST)
    maps_all, states_all = lax.associative_scan(compose, (transit, inject), axis=1)
    reach_rest = product(project[:, 1:], maps_all[:, :-1])
    reach = jnp.concatenate([project[:, :1], reach_rest], axis=1).reshape(heads, length, key_width)
    out_rest = product(project[:, 1:], states_all[:, :-1]) + direct[:, 1:]
    local_out = jnp.concatenate([direct[:, :1], out_rest], axis=1).reshape(heads, length, -1)
    return (local_out, reach, maps_all[:, -1], states_all[:, -1])


def per_device(query_heads, key_heads, value_heads, gate_log, beta_rate):
    key_count = query_heads.shape[1]
    grouping = value_heads.shape[1] // key_count
    got_query, got_key, got_value, got_gate, got_beta = (
        lax.all_to_all(
            jnp.repeat(query_heads, grouping, axis=1),
            "head",
            split_axis=1,
            concat_axis=0,
            tiled=True,
        ),
        lax.all_to_all(
            jnp.repeat(key_heads, grouping, axis=1), "head", split_axis=1, concat_axis=0, tiled=True
        ),
        lax.all_to_all(value_heads, "head", split_axis=1, concat_axis=0, tiled=True),
        lax.all_to_all(gate_log, "head", split_axis=1, concat_axis=0, tiled=True),
        lax.all_to_all(beta_rate, "head", split_axis=1, concat_axis=0, tiled=True),
    )
    queries = jnp.swapaxes(normalize(got_query), 0, 1)
    keys_in = jnp.swapaxes(normalize(got_key), 0, 1)
    values = jnp.swapaxes(got_value.astype(jnp.float32), 0, 1)
    gate_vals = jnp.swapaxes(got_gate.astype(jnp.float32), 0, 1)
    beta_vals = jnp.swapaxes(got_beta.astype(jnp.float32), 0, 1)
    local_out, reach, slab_map, slab_state = slab_local(
        queries, keys_in, values, gate_vals, beta_vals
    )

    def advance(counter, carried):
        return shifted(product(slab_map, carried) + slab_state, "seq", 1)

    incoming = lax.fori_loop(0, lax.axis_size("seq") - 1, advance, jnp.zeros_like(slab_state))
    combined = local_out + product(reach, incoming)
    head_rows = jnp.swapaxes(combined, 0, 1).astype(jnp.bfloat16)
    flat_rows = head_rows.reshape(head_rows.shape[0], -1)
    head_output = lax.all_to_all(flat_rows, "head", split_axis=0, concat_axis=1, tiled=True)
    last_state = (product(slab_map, incoming) + slab_state)[None]
    return (head_output, last_state)


def split(matrix):
    high = matrix.astype(jnp.bfloat16)
    low = (matrix - high.astype(jnp.float32)).astype(jnp.bfloat16)
    return high, low


def dot(left, right):
    return jnp.dot(left, right, preferred_element_type=jnp.float32)


def wide(matrix):
    return jnp.concatenate(split(matrix), axis=1)


def tall(*matrices):
    row = jnp.concatenate([half for matrix in matrices for half in split(matrix)], axis=1)
    return jnp.concatenate([row, row], axis=0)


def fold(product):
    width = product.shape[1] // 2
    return product[:, :width] + product[:, width:]


def mul(left, right):
    return fold(dot(wide(left), tall(right)))


def fast_kernel(
    sizes,
    q_hbm,
    k_hbm,
    v_hbm,
    g_hbm,
    b_hbm,
    out_ref,
    states_ref,
    q_in,
    k_in,
    v_in,
    g_in,
    b_in,
    q_wide,
    k_wide,
    v_wide,
    send,
    gb_send,
    recv,
    swapped,
    gb_recv,
    out_buf,
    state_buf,
    step_maps,
    step_terms,
    step_decay,
    load_sem,
    send_sem,
    recv_sem,
    gb_sem,
    back_sem,
    swap_sem,
):
    ns, nh, tokens, heads, key_heads = sizes
    slab = nh * tokens
    width = 128
    s = lax.axis_index("seq")
    h = lax.axis_index("head")
    mine = h * ns + s

    loads = [
        pltpu.make_async_copy(source, target, load_sem.at[i])
        for i, (source, target) in enumerate(
            [(q_hbm, q_in), (k_hbm, k_in), (v_hbm, v_in), (g_hbm, g_in), (b_hbm, b_in)]
        )
    ]
    for load in loads:
        load.start()

    peers = []
    seq_peers = [s]
    for ds in range(1, ns):
        other, bit = s, 1
        while bit <= ds:
            if ds & bit:
                other = other + bit - 2 * bit * lax.rem(s // bit, 2)
            bit *= 2
        seq_peers.append(other)
    for ps in seq_peers:
        for dh in range(nh):
            peers.append((ps, lax.rem(h + dh, nh)))
    even = lax.rem(s, 2) == 0

    barrier = pltpu.get_barrier_semaphore()
    for ps, ph in peers[1:]:
        pl.semaphore_signal(barrier, inc=1, device_id=(ps, ph), device_id_type=MESH)

    loads[0].wait()
    q_wide[...] = q_in[...].astype(jnp.float32).reshape(tokens * key_heads, width)
    loads[1].wait()
    k_wide[...] = k_in[...].astype(jnp.float32).reshape(tokens * key_heads, width)
    for j in range(key_heads):
        queries = q_wide[pl.ds(j, tokens, stride=key_heads), :].astype(jnp.bfloat16)
        keys = k_wide[pl.ds(j, tokens, stride=key_heads), :].astype(jnp.bfloat16)
        send[2 * j, 0:tokens, :] = queries
        send[2 * j + 1, 0:tokens, :] = keys
    loads[2].wait()
    v_wide[...] = v_in[...].astype(jnp.float32).reshape(tokens * heads, width)
    for j in range(heads):
        values = v_wide[pl.ds(j, tokens, stride=heads), :].astype(jnp.bfloat16)
        send[j, tokens : 2 * tokens, :] = values
    loads[3].wait()
    loads[4].wait()
    both = jnp.concatenate([g_in[...], b_in[...]], axis=0).astype(jnp.float32)
    place_row = lax.broadcasted_iota(jnp.int32, (2 * tokens, width), 0)
    place_col = lax.broadcasted_iota(jnp.int32, (2 * tokens, width), 1)
    place = (place_row == place_col).astype(jnp.bfloat16)
    turned = dot(both.T.astype(jnp.bfloat16), place)
    for j in range(heads):
        gb_send[j, :, :] = turned[j : j + 1, :]

    pl.semaphore_wait(barrier, ns * nh - 1)

    for i, (ps, ph) in enumerate(peers):
        j = ph * ns + ps
        if i == 0:
            pltpu.make_async_copy(send.at[j], recv.at[s, h], recv_sem.at[0]).start()
            pltpu.make_async_copy(gb_send.at[j], gb_recv.at[s, h], gb_sem.at[0]).start()
        else:
            for source, target, n, sem in ((gb_send, gb_recv, 1, gb_sem), (send, recv, 0, recv_sem)):
                pltpu.make_async_remote_copy(
                    src_ref=source.at[j],
                    dst_ref=target.at[s, h],
                    send_sem=send_sem.at[n],
                    recv_sem=sem.at[i // nh],
                    device_id=(ps, ph),
                    device_id_type=MESH,
                ).start()

    row_ids = lax.broadcasted_iota(jnp.int32, (slab, slab), 0)
    col_ids = lax.broadcasted_iota(jnp.int32, (slab, slab), 1)
    strict = row_ids > col_ids
    inclusive = row_ids >= col_ids
    eye = (row_ids == col_ids).astype(jnp.float32)
    lower_ones = inclusive.astype(jnp.bfloat16)
    all_ones = jnp.ones((slab, slab), jnp.bfloat16)
    token_at = row_ids % tokens
    expand = (
        lax.broadcasted_iota(jnp.int32, (slab, nh), 0) // tokens
        == lax.broadcasted_iota(jnp.int32, (slab, nh), 1)
    ).astype(jnp.bfloat16)

    for first in range(0, ns, 2):
        slabs = seq_peers[first : first + 2]
        count = len(slabs)
        for i, at in enumerate(slabs):
            pltpu.make_async_copy(gb_recv.at[at], gb_recv.at[at], gb_sem.at[first + i]).wait()
        cums, betas = [], []
        for at in slabs:
            rates = dot(expand, gb_recv[at, :, 0, :].astype(jnp.bfloat16))
            gates = jnp.where(col_ids == token_at, rates, 0.0).astype(jnp.bfloat16)
            writes = jnp.where(col_ids == token_at + tokens, rates, 0.0).astype(jnp.bfloat16)
            gate_cols = dot(gates, all_ones).astype(jnp.bfloat16)
            cums.append(dot(lower_ones, gate_cols))
            betas.append(dot(writes, all_ones))

        for i, at in enumerate(slabs):
            pltpu.make_async_copy(recv.at[at], recv.at[at], recv_sem.at[first + i]).wait()
            pltpu.make_async_remote_copy(
                src_ref=recv.at[at, :, 0:tokens, :],
                dst_ref=swapped.at[at],
                send_sem=send_sem.at[4],
                recv_sem=swap_sem.at[first // 2],
                device_id=(seq_peers[1], h),
                device_id_type=MESH,
            ).start()
        two = swapped.at[pl.ds(0, count)]
        pltpu.make_async_copy(two, two, swap_sem.at[first // 2]).wait()

        parts = []
        for n in range(count):
            own = recv[slabs[n], :, 0:tokens, :].reshape(slab, width)
            other = swapped[slabs[n]].reshape(slab, width)
            queries, keys = jnp.where(even, own, other), jnp.where(even, other, own)
            values = recv[slabs[n], :, tokens : 2 * tokens, :].reshape(slab, width)
            cum, beta = cums[n], betas[n]
            q32, k32 = queries.astype(jnp.float32), keys.astype(jnp.float32)
            q_norm = 1.0 / jnp.sqrt(jnp.sum(q32 * q32, axis=1, keepdims=True) + 1e-06)
            k_norm = 1.0 / jnp.sqrt(jnp.sum(k32 * k32, axis=1, keepdims=True) + 1e-06)
            columns = jnp.where(col_ids == 0, cum, jnp.where(col_ids == 1, k_norm, beta))
            rows = columns.T
            cum_row, k_norm_row, beta_row = rows[0:1, :], rows[1:2, :], rows[2:3, :]
            k_turned = k32.T.astype(jnp.bfloat16)
            decay = jnp.where(inclusive, jnp.exp(jnp.where(inclusive, cum - cum_row, 0.0)), 0.0)
            decay = decay * k_norm_row
            key_key = dot(keys, k_turned)
            query_key = dot(queries, k_turned)
            lower = jnp.where(strict, (beta * k_norm) * decay * key_key, 0.0)
            scores = q_norm * decay * query_key
            parts.append((queries, keys, values, cum, k_norm, q_norm, cum_row, k_norm_row, beta_row,
                          k_turned, lower, scores, q32))

        small = 32
        same = (row_ids // small) == (col_ids // small)
        lowers = [part[10] for part in parts]
        blocks = [jnp.where(same, lower, 0.0) for lower in lowers]
        inverses = [eye - block for block in blocks]
        powers = [mul(block, block) for block in blocks]
        reach = 2
        while reach < small:
            last = reach * 2 >= small
            for n in range(count):
                right = tall(powers[n])
                if last:
                    inverses[n] = inverses[n] + fold(dot(wide(inverses[n]), right))
                else:
                    left = jnp.concatenate([wide(inverses[n]), wide(powers[n])], axis=0)
                    both_products = fold(dot(left, right))
                    inverses[n] = inverses[n] + both_products[:slab]
                    powers[n] = both_products[slab:]
            reach *= 2
        steps = [mul(inverses[n], jnp.where(same, 0.0, lowers[n])) for n in range(count)]
        squares = [mul(steps[n], steps[n]) for n in range(count)]
        inverses = [inverses[n] - mul(steps[n], inverses[n]) for n in range(count)]
        inverses = [inverses[n] + mul(squares[n], inverses[n]) for n in range(count)]

        for n in range(count):
            (queries, keys, values, cum, k_norm, q_norm, cum_row, k_norm_row, beta_row,
             k_turned, lower, scores, q32) = parts[n]
            solve = inverses[n] * beta_row
            write_vals = dot(wide(solve), jnp.concatenate([values, values], axis=0))
            final = cum[slab - 1 : slab, :]
            key_decay = jnp.exp(final - cum) * k_norm
            key_solve = solve * (jnp.exp(cum_row) * k_norm_row)
            write_keys = dot(wide(key_solve), jnp.concatenate([keys, keys], axis=0))
            scaled = jnp.concatenate([wide(key_decay * write_keys), wide(key_decay * write_vals)], axis=1)
            moved = dot(k_turned, scaled)
            read = dot(wide(scores), tall(write_keys, write_vals))
            project = (jnp.exp(cum) * q_norm) * q32 - fold(read[:, : 2 * width])
            at = slabs[n]
            step_maps[at, :slab, :] = wide(fold(moved[:, : 2 * width]))
            step_maps[at, slab:, :] = wide(project)
            step_terms[at, :slab, :] = fold(moved[:, 2 * width :])
            step_terms[at, slab:, :] = fold(read[:, 2 * width :])
            step_decay[at, :, :] = jnp.exp(final)

    columns = pl.ds(pl.multiple_of(mine * width, width), width)
    state = None
    for n in range(ns):
        if n == 0:
            state, output = step_terms[n, :slab, :], step_terms[n, slab:, :]
        else:
            products = fold(dot(step_maps[n], tall(state)))
            output = step_terms[n, slab:, :] + products[slab:]
            state = step_decay[n] * state + step_terms[n, :slab, :] - products[:slab]
        out_buf[n * nh : (n + 1) * nh] = output.astype(jnp.bfloat16).reshape(nh, tokens, width)
        state_buf[n] = state

        @pl.when(s == n)
        def _():
            pltpu.make_async_copy(state_buf.at[n], states_ref.at[0, s], back_sem.at[1]).start()

        @pl.when(s != n)
        def _():
            pltpu.make_async_remote_copy(
                src_ref=state_buf.at[n],
                dst_ref=states_ref.at[0, s],
                send_sem=send_sem.at[3],
                recv_sem=back_sem.at[1],
                device_id=(n, h),
                device_id_type=MESH,
            ).start()

        def give(ph):
            pltpu.make_async_remote_copy(
                src_ref=out_buf.at[n * nh + ph],
                dst_ref=out_ref.at[:, columns],
                send_sem=send_sem.at[2],
                recv_sem=back_sem.at[0],
                device_id=(n, ph),
                device_id_type=MESH,
            ).start()

        for dh in range(1, nh):
            give(lax.rem(h + dh, nh))

        @pl.when(s == n)
        def _():
            pltpu.make_async_copy(
                out_buf.at[n * nh + h], out_ref.at[:, columns], back_sem.at[0]
            ).start()

        @pl.when(s != n)
        def _():
            give(h)

    others = pl.ds(0, ns * nh - 1)
    pltpu.make_async_copy(send.at[others], send.at[others], send_sem.at[0]).wait()
    pltpu.make_async_copy(gb_send.at[others], gb_send.at[others], send_sem.at[1]).wait()
    pltpu.make_async_copy(out_buf.at[others], out_buf.at[others], send_sem.at[2]).wait()
    pltpu.make_async_copy(swapped, swapped, send_sem.at[4]).wait()
    rest = state_buf.at[pl.ds(0, ns - 1)]
    pltpu.make_async_copy(rest, rest, send_sem.at[3]).wait()
    pltpu.make_async_copy(out_ref, out_ref, back_sem.at[0]).wait()
    pltpu.make_async_copy(states_ref, states_ref, back_sem.at[1]).wait()


def fast_device(query_heads, key_heads, value_heads, gate_log, beta_rate):
    ns, nh = lax.axis_size("seq"), lax.axis_size("head")
    tokens, heads, width = value_heads.shape
    key_count = key_heads.shape[1]
    sizes = (ns, nh, tokens, heads, key_count)
    bf16, f32 = jnp.bfloat16, jnp.float32
    anywhere = pl.BlockSpec(memory_space=pl.ANY)
    vmem = pl.BlockSpec(memory_space=pltpu.VMEM)
    return pl.pallas_call(
        functools.partial(fast_kernel, sizes),
        out_shape=(
            pltpu.VMEM((tokens, heads * width), bf16),
            pltpu.VMEM((1, ns, width, width), f32),
        ),
        in_specs=[anywhere] * 5,
        out_specs=(vmem, vmem),
        scratch_shapes=[
            pltpu.VMEM((tokens, key_count, width), bf16),
            pltpu.VMEM((tokens, key_count, width), bf16),
            pltpu.VMEM((tokens, heads, width), bf16),
            pltpu.VMEM((tokens, heads), bf16),
            pltpu.VMEM((tokens, heads), bf16),
            pltpu.VMEM((tokens * key_count, width), f32),
            pltpu.VMEM((tokens * key_count, width), f32),
            pltpu.VMEM((tokens * heads, width), f32),
            pltpu.VMEM((heads, 2 * tokens, width), bf16),
            pltpu.VMEM((heads, 1, width), f32),
            pltpu.VMEM((ns, nh, 2 * tokens, width), bf16),
            pltpu.VMEM((ns, nh, tokens, width), bf16),
            pltpu.VMEM((ns, nh, 1, width), f32),
            pltpu.VMEM((ns * nh, tokens, width), bf16),
            pltpu.VMEM((ns, width, width), f32),
            pltpu.VMEM((ns, 2 * width, 2 * width), bf16),
            pltpu.VMEM((ns, 2 * width, width), f32),
            pltpu.VMEM((ns, 1, width), f32),
            pltpu.SemaphoreType.DMA((5,)),
            pltpu.SemaphoreType.DMA((5,)),
            pltpu.SemaphoreType.DMA((ns,)),
            pltpu.SemaphoreType.DMA((ns,)),
            pltpu.SemaphoreType.DMA((2,)),
            pltpu.SemaphoreType.DMA((ns // 2,)),
        ],
        compiler_params=pltpu.CompilerParams(
            collective_id=0, has_side_effects=True, vmem_limit_bytes=60 * 1024 * 1024
        ),
    )(query_heads, key_heads, value_heads, gate_log, beta_rate)


def choose_device(query_heads, key_heads, value_heads, gate_log, beta_rate):
    ns, nh = lax.axis_size("seq"), lax.axis_size("head")
    tokens, heads, width = value_heads.shape
    fits = ns * nh == heads and tokens == 16 and nh * tokens == 128
    fits = fits and width == 128 and key_heads.shape[2] == 128
    fits = fits and heads == 2 * key_heads.shape[1] and ns in (2, 4, 8)
    run = fast_device if fits else per_device
    return run(query_heads, key_heads, value_heads, gate_log, beta_rate)


def solution(mesh):
    return jax.shard_map(
        choose_device,
        mesh=mesh,
        in_specs=(
            P(("seq", "head"), None, None),
            P(("seq", "head"), None, None),
            P(("seq", "head"), None, None),
            P(("seq", "head"), None),
            P(("seq", "head"), None),
        ),
        out_specs=(P(("seq", "head"), None), P("seq", "head", None, None)),
        check_vma=False,
    )
```

```python
import functools

import jax
import jax.numpy as jnp
from jax import lax
from jax.experimental import pallas as pl
from jax.experimental.pallas import tpu as pltpu
from jax.sharding import PartitionSpec as P

STRETCH = 64
MESH = pl.DeviceIdType.MESH


HIGHEST = lax.Precision.HIGHEST


def shifted(block, axis, distance):
    devices = range(lax.axis_size(axis))
    route = [(i - distance, i) for i in devices if i - distance in devices]
    return lax.ppermute(block, axis, route)


def normalize(tensor):
    tensor = tensor.astype(jnp.float32)
    return tensor / jnp.sqrt(jnp.sum(tensor * tensor, axis=-1, keepdims=True) + 1e-06)


def stretch_parts(queries, keys_in, values, gate_vals, beta_vals):
    span_len = gate_vals.shape[-1]
    cumulative = jnp.cumsum(gate_vals, axis=-1)
    row_ids = lax.broadcasted_iota(jnp.int32, (span_len, span_len), 0)
    columns = lax.broadcasted_iota(jnp.int32, (span_len, span_len), 1)
    strict = row_ids > columns
    inclusive = row_ids >= columns
    differ = cumulative[..., :, None] - cumulative[..., None, :]
    key_key = jnp.einsum("...rd,...sd->...rs", keys_in, keys_in, precision=HIGHEST)
    query_key = jnp.einsum("...rd,...sd->...rs", queries, keys_in, precision=HIGHEST)
    lower_triangle = jnp.where(
        strict, beta_vals[..., :, None] * jnp.exp(jnp.where(strict, differ, 0.0)) * key_key, 0.0
    )
    scores = jnp.where(inclusive, jnp.exp(jnp.where(inclusive, differ, 0.0)) * query_key, 0.0)
    identity = jnp.eye(span_len, dtype=jnp.float32)
    right_side = jnp.concatenate(
        [(beta_vals * jnp.exp(cumulative))[..., None] * keys_in, beta_vals[..., None] * values],
        axis=-1,
    )
    solved = jax.scipy.linalg.solve_triangular(
        identity + lower_triangle, right_side, lower=True, unit_diagonal=True
    )
    key_width = keys_in.shape[-1]
    last_cum = cumulative[..., -1:]
    query_dec = jnp.exp(cumulative)[..., None] * queries
    key_dec = jnp.exp(last_cum - cumulative)[..., None] * keys_in
    return (
        solved[..., :key_width],
        solved[..., key_width:],
        scores,
        query_dec,
        key_dec,
        jnp.exp(last_cum[..., 0]),
    )


def product(left_mat, right_mat):
    return jnp.einsum("...ij,...jk->...ik", left_mat, right_mat, precision=HIGHEST)


def compose(earlier, later):
    return (product(later[0], earlier[0]), product(later[0], earlier[1]) + later[1])


def slab_local(queries, keys_in, values, gate_vals, beta_vals):
    heads, length = gate_vals.shape
    blocks = length // STRETCH

    def split_rows(tensor):
        return tensor.reshape((heads, blocks, STRETCH) + tensor.shape[2:])

    write_keys, write_vals, scores, query_dec, key_dec, stretch_decay = stretch_parts(
        split_rows(queries),
        split_rows(keys_in),
        split_rows(values),
        split_rows(gate_vals),
        split_rows(beta_vals),
    )
    key_width = keys_in.shape[-1]
    identity = jnp.eye(key_width, dtype=jnp.float32)
    transit = stretch_decay[..., None, None] * identity - jnp.einsum(
        "hncd,hnce->hnde", key_dec, write_keys, precision=HIGHEST
    )
    inject = jnp.einsum("hncd,hnce->hnde", key_dec, write_vals, precision=HIGHEST)
    project = query_dec - jnp.einsum("hnrs,hnsd->hnrd", scores, write_keys, precision=HIGHEST)
    direct = jnp.einsum("hnrs,hnse->hnre", scores, write_vals, precision=HIGHEST)
    maps_all, states_all = lax.associative_scan(compose, (transit, inject), axis=1)
    reach_rest = product(project[:, 1:], maps_all[:, :-1])
    reach = jnp.concatenate([project[:, :1], reach_rest], axis=1).reshape(heads, length, key_width)
    out_rest = product(project[:, 1:], states_all[:, :-1]) + direct[:, 1:]
    local_out = jnp.concatenate([direct[:, :1], out_rest], axis=1).reshape(heads, length, -1)
    return (local_out, reach, maps_all[:, -1], states_all[:, -1])


def per_device(query_heads, key_heads, value_heads, gate_log, beta_rate):
    key_count = query_heads.shape[1]
    grouping = value_heads.shape[1] // key_count
    got_query, got_key, got_value, got_gate, got_beta = (
        lax.all_to_all(
            jnp.repeat(query_heads, grouping, axis=1),
            "head",
            split_axis=1,
            concat_axis=0,
            tiled=True,
        ),
        lax.all_to_all(
            jnp.repeat(key_heads, grouping, axis=1), "head", split_axis=1, concat_axis=0, tiled=True
        ),
        lax.all_to_all(value_heads, "head", split_axis=1, concat_axis=0, tiled=True),
        lax.all_to_all(gate_log, "head", split_axis=1, concat_axis=0, tiled=True),
        lax.all_to_all(beta_rate, "head", split_axis=1, concat_axis=0, tiled=True),
    )
    queries = jnp.swapaxes(normalize(got_query), 0, 1)
    keys_in = jnp.swapaxes(normalize(got_key), 0, 1)
    values = jnp.swapaxes(got_value.astype(jnp.float32), 0, 1)
    gate_vals = jnp.swapaxes(got_gate.astype(jnp.float32), 0, 1)
    beta_vals = jnp.swapaxes(got_beta.astype(jnp.float32), 0, 1)
    local_out, reach, slab_map, slab_state = slab_local(
        queries, keys_in, values, gate_vals, beta_vals
    )

    def advance(counter, carried):
        return shifted(product(slab_map, carried) + slab_state, "seq", 1)

    incoming = lax.fori_loop(0, lax.axis_size("seq") - 1, advance, jnp.zeros_like(slab_state))
    combined = local_out + product(reach, incoming)
    head_rows = jnp.swapaxes(combined, 0, 1).astype(jnp.bfloat16)
    flat_rows = head_rows.reshape(head_rows.shape[0], -1)
    head_output = lax.all_to_all(flat_rows, "head", split_axis=0, concat_axis=1, tiled=True)
    last_state = (product(slab_map, incoming) + slab_state)[None]
    return (head_output, last_state)


def split(matrix):
    high = matrix.astype(jnp.bfloat16)
    low = (matrix - high.astype(jnp.float32)).astype(jnp.bfloat16)
    return high, low


def dot(left, right):
    return jnp.dot(left, right, preferred_element_type=jnp.float32)


def wide(matrix):
    return jnp.concatenate(split(matrix), axis=1)


def tall(*matrices):
    row = jnp.concatenate([half for matrix in matrices for half in split(matrix)], axis=1)
    return jnp.concatenate([row, row], axis=0)


def fold(product):
    width = product.shape[1] // 2
    return product[:, :width] + product[:, width:]


def mul(left, right):
    return fold(dot(wide(left), tall(right)))


def fast_kernel(
    sizes,
    q_hbm,
    k_hbm,
    v_hbm,
    g_hbm,
    b_hbm,
    out_ref,
    states_ref,
    q_in,
    k_in,
    v_in,
    g_in,
    b_in,
    q_wide,
    k_wide,
    v_wide,
    send,
    gb_send,
    recv,
    swapped,
    gb_recv,
    out_buf,
    state_buf,
    step_maps,
    step_terms,
    step_decay,
    load_sem,
    send_sem,
    recv_sem,
    gb_sem,
    back_sem,
    swap_sem,
):
    ns, nh, tokens, heads, key_heads = sizes
    slab = nh * tokens
    width = 128
    s = lax.axis_index("seq")
    h = lax.axis_index("head")
    mine = h * ns + s

    loads = [
        pltpu.make_async_copy(source, target, load_sem.at[i])
        for i, (source, target) in enumerate(
            [(q_hbm, q_in), (k_hbm, k_in), (v_hbm, v_in), (g_hbm, g_in), (b_hbm, b_in)]
        )
    ]
    for load in loads:
        load.start()

    peers = []
    seq_peers = [s]
    for ds in range(1, ns):
        other, bit = s, 1
        while bit <= ds:
            if ds & bit:
                other = other + bit - 2 * bit * lax.rem(s // bit, 2)
            bit *= 2
        seq_peers.append(other)
    for ps in seq_peers:
        for dh in range(nh):
            peers.append((ps, lax.rem(h + dh, nh)))
    even = lax.rem(s, 2) == 0

    barrier = pltpu.get_barrier_semaphore()
    for ps, ph in peers[1:]:
        pl.semaphore_signal(barrier, inc=1, device_id=(ps, ph), device_id_type=MESH)

    loads[0].wait()
    q_wide[...] = q_in[...].astype(jnp.float32).reshape(tokens * key_heads, width)
    loads[1].wait()
    k_wide[...] = k_in[...].astype(jnp.float32).reshape(tokens * key_heads, width)
    for j in range(key_heads):
        queries = q_wide[pl.ds(j, tokens, stride=key_heads), :].astype(jnp.bfloat16)
        keys = k_wide[pl.ds(j, tokens, stride=key_heads), :].astype(jnp.bfloat16)
        send[2 * j, 0:tokens, :] = queries
        send[2 * j + 1, 0:tokens, :] = keys
    loads[2].wait()
    v_wide[...] = v_in[...].astype(jnp.float32).reshape(tokens * heads, width)
    for j in range(heads):
        values = v_wide[pl.ds(j, tokens, stride=heads), :].astype(jnp.bfloat16)
        send[j, tokens : 2 * tokens, :] = values
    loads[3].wait()
    loads[4].wait()
    both = jnp.concatenate([g_in[...], b_in[...]], axis=0).astype(jnp.float32)
    place_row = lax.broadcasted_iota(jnp.int32, (2 * tokens, width), 0)
    place_col = lax.broadcasted_iota(jnp.int32, (2 * tokens, width), 1)
    place = (place_row == place_col).astype(jnp.bfloat16)
    turned = dot(both.T.astype(jnp.bfloat16), place)
    for j in range(heads):
        gb_send[j, :, :] = turned[j : j + 1, :]

    pl.semaphore_wait(barrier, ns * nh - 1)

    for i, (ps, ph) in enumerate(peers):
        j = ph * ns + ps
        if i == 0:
            pltpu.make_async_copy(send.at[j], recv.at[s, h], recv_sem.at[0]).start()
            pltpu.make_async_copy(gb_send.at[j], gb_recv.at[s, h], gb_sem.at[0]).start()
        else:
            for source, target, n, sem in ((gb_send, gb_recv, 1, gb_sem), (send, recv, 0, recv_sem)):
                pltpu.make_async_remote_copy(
                    src_ref=source.at[j],
                    dst_ref=target.at[s, h],
                    send_sem=send_sem.at[n],
                    recv_sem=sem.at[i // nh],
                    device_id=(ps, ph),
                    device_id_type=MESH,
                ).start()

    row_ids = lax.broadcasted_iota(jnp.int32, (slab, slab), 0)
    col_ids = lax.broadcasted_iota(jnp.int32, (slab, slab), 1)
    strict = row_ids > col_ids
    inclusive = row_ids >= col_ids
    eye = (row_ids == col_ids).astype(jnp.float32)
    lower_ones = inclusive.astype(jnp.bfloat16)
    all_ones = jnp.ones((slab, slab), jnp.bfloat16)
    token_at = row_ids % tokens
    expand = (
        lax.broadcasted_iota(jnp.int32, (slab, nh), 0) // tokens
        == lax.broadcasted_iota(jnp.int32, (slab, nh), 1)
    ).astype(jnp.bfloat16)

    for first in range(0, ns, 2):
        slabs = seq_peers[first : first + 2]
        count = len(slabs)
        for i, at in enumerate(slabs):
            pltpu.make_async_copy(gb_recv.at[at], gb_recv.at[at], gb_sem.at[first + i]).wait()
        cums, betas = [], []
        for at in slabs:
            rates = dot(expand, gb_recv[at, :, 0, :].astype(jnp.bfloat16))
            gates = jnp.where(col_ids == token_at, rates, 0.0).astype(jnp.bfloat16)
            writes = jnp.where(col_ids == token_at + tokens, rates, 0.0).astype(jnp.bfloat16)
            gate_cols = dot(gates, all_ones).astype(jnp.bfloat16)
            cums.append(dot(lower_ones, gate_cols))
            betas.append(dot(writes, all_ones))

        for i, at in enumerate(slabs):
            pltpu.make_async_copy(recv.at[at], recv.at[at], recv_sem.at[first + i]).wait()
            pltpu.make_async_remote_copy(
                src_ref=recv.at[at, :, 0:tokens, :],
                dst_ref=swapped.at[at],
                send_sem=send_sem.at[4],
                recv_sem=swap_sem.at[first // 2],
                device_id=(seq_peers[1], h),
                device_id_type=MESH,
            ).start()
        two = swapped.at[pl.ds(0, count)]
        pltpu.make_async_copy(two, two, swap_sem.at[first // 2]).wait()

        parts = []
        for n in range(count):
            own = recv[slabs[n], :, 0:tokens, :].reshape(slab, width)
            other = swapped[slabs[n]].reshape(slab, width)
            queries, keys = jnp.where(even, own, other), jnp.where(even, other, own)
            values = recv[slabs[n], :, tokens : 2 * tokens, :].reshape(slab, width)
            cum, beta = cums[n], betas[n]
            q32, k32 = queries.astype(jnp.float32), keys.astype(jnp.float32)
            q_norm = 1.0 / jnp.sqrt(jnp.sum(q32 * q32, axis=1, keepdims=True) + 1e-06)
            k_norm = 1.0 / jnp.sqrt(jnp.sum(k32 * k32, axis=1, keepdims=True) + 1e-06)
            columns = jnp.where(col_ids == 0, cum, jnp.where(col_ids == 1, k_norm, beta))
            rows = columns.T
            cum_row, k_norm_row, beta_row = rows[0:1, :], rows[1:2, :], rows[2:3, :]
            k_turned = k32.T.astype(jnp.bfloat16)
            decay = jnp.where(inclusive, jnp.exp(jnp.where(inclusive, cum - cum_row, 0.0)), 0.0)
            decay = decay * k_norm_row
            key_key = dot(keys, k_turned)
            query_key = dot(queries, k_turned)
            lower = jnp.where(strict, (beta * k_norm) * decay * key_key, 0.0)
            scores = q_norm * decay * query_key
            parts.append((queries, keys, values, cum, k_norm, q_norm, cum_row, k_norm_row, beta_row,
                          k_turned, lower, scores, q32))

        small = 32
        same = (row_ids // small) == (col_ids // small)
        lowers = [part[10] for part in parts]
        blocks = [jnp.where(same, lower, 0.0) for lower in lowers]
        inverses = [eye - block for block in blocks]
        powers = [mul(block, block) for block in blocks]
        reach = 2
        while reach < small:
            last = reach * 2 >= small
            for n in range(count):
                right = tall(powers[n])
                if last:
                    inverses[n] = inverses[n] + fold(dot(wide(inverses[n]), right))
                else:
                    left = jnp.concatenate([wide(inverses[n]), wide(powers[n])], axis=0)
                    both_products = fold(dot(left, right))
                    inverses[n] = inverses[n] + both_products[:slab]
                    powers[n] = both_products[slab:]
            reach *= 2
        steps = [mul(inverses[n], jnp.where(same, 0.0, lowers[n])) for n in range(count)]
        squares = [mul(steps[n], steps[n]) for n in range(count)]
        inverses = [inverses[n] - mul(steps[n], inverses[n]) for n in range(count)]
        inverses = [inverses[n] + mul(squares[n], inverses[n]) for n in range(count)]

        for n in range(count):
            (queries, keys, values, cum, k_norm, q_norm, cum_row, k_norm_row, beta_row,
             k_turned, lower, scores, q32) = parts[n]
            solve = inverses[n] * beta_row
            write_vals = dot(wide(solve), jnp.concatenate([values, values], axis=0))
            final = cum[slab - 1 : slab, :]
            key_decay = jnp.exp(final - cum) * k_norm
            key_solve = solve * (jnp.exp(cum_row) * k_norm_row)
            write_keys = dot(wide(key_solve), jnp.concatenate([keys, keys], axis=0))
            scaled = jnp.concatenate([wide(key_decay * write_keys), wide(key_decay * write_vals)], axis=1)
            moved = dot(k_turned, scaled)
            read = dot(wide(scores), tall(write_keys, write_vals))
            project = (jnp.exp(cum) * q_norm) * q32 - fold(read[:, : 2 * width])
            at = slabs[n]
            step_maps[at, :slab, :] = wide(fold(moved[:, : 2 * width]))
            step_maps[at, slab:, :] = wide(project)
            step_terms[at, :slab, :] = fold(moved[:, 2 * width :])
            step_terms[at, slab:, :] = fold(read[:, 2 * width :])
            step_decay[at, :, :] = jnp.exp(final)

    columns = pl.ds(pl.multiple_of(mine * width, width), width)
    state = None
    for n in range(ns):
        if n == 0:
            state, output = step_terms[n, :slab, :], step_terms[n, slab:, :]
        else:
            products = fold(dot(step_maps[n], tall(state)))
            output = step_terms[n, slab:, :] + products[slab:]
            state = step_decay[n] * state + step_terms[n, :slab, :] - products[:slab]
        out_buf[n * nh : (n + 1) * nh] = output.astype(jnp.bfloat16).reshape(nh, tokens, width)
        state_buf[n] = state

        def give(ph):
            pltpu.make_async_remote_copy(
                src_ref=out_buf.at[n * nh + ph],
                dst_ref=out_ref.at[:, columns],
                send_sem=send_sem.at[2],
                recv_sem=back_sem.at[0],
                device_id=(n, ph),
                device_id_type=MESH,
            ).start()

        for dh in range(1, nh):
            give(lax.rem(h + dh, nh))

        @pl.when(s == n)
        def _():
            pltpu.make_async_copy(
                out_buf.at[n * nh + h], out_ref.at[:, columns], back_sem.at[0]
            ).start()

        @pl.when(s != n)
        def _():
            give(h)

        @pl.when(s == n)
        def _():
            pltpu.make_async_copy(state_buf.at[n], states_ref.at[0, s], back_sem.at[1]).start()

        @pl.when(s != n)
        def _():
            pltpu.make_async_remote_copy(
                src_ref=state_buf.at[n],
                dst_ref=states_ref.at[0, s],
                send_sem=send_sem.at[3],
                recv_sem=back_sem.at[1],
                device_id=(n, h),
                device_id_type=MESH,
            ).start()

    others = pl.ds(0, ns * nh - 1)
    pltpu.make_async_copy(send.at[others], send.at[others], send_sem.at[0]).wait()
    pltpu.make_async_copy(gb_send.at[others], gb_send.at[others], send_sem.at[1]).wait()
    pltpu.make_async_copy(out_buf.at[others], out_buf.at[others], send_sem.at[2]).wait()
    pltpu.make_async_copy(swapped, swapped, send_sem.at[4]).wait()
    rest = state_buf.at[pl.ds(0, ns - 1)]
    pltpu.make_async_copy(rest, rest, send_sem.at[3]).wait()
    pltpu.make_async_copy(out_ref, out_ref, back_sem.at[0]).wait()
    pltpu.make_async_copy(states_ref, states_ref, back_sem.at[1]).wait()


def fast_device(query_heads, key_heads, value_heads, gate_log, beta_rate):
    ns, nh = lax.axis_size("seq"), lax.axis_size("head")
    tokens, heads, width = value_heads.shape
    key_count = key_heads.shape[1]
    sizes = (ns, nh, tokens, heads, key_count)
    bf16, f32 = jnp.bfloat16, jnp.float32
    anywhere = pl.BlockSpec(memory_space=pl.ANY)
    vmem = pl.BlockSpec(memory_space=pltpu.VMEM)
    return pl.pallas_call(
        functools.partial(fast_kernel, sizes),
        out_shape=(
            pltpu.VMEM((tokens, heads * width), bf16),
            pltpu.VMEM((1, ns, width, width), f32),
        ),
        in_specs=[anywhere] * 5,
        out_specs=(vmem, vmem),
        scratch_shapes=[
            pltpu.VMEM((tokens, key_count, width), bf16),
            pltpu.VMEM((tokens, key_count, width), bf16),
            pltpu.VMEM((tokens, heads, width), bf16),
            pltpu.VMEM((tokens, heads), bf16),
            pltpu.VMEM((tokens, heads), bf16),
            pltpu.VMEM((tokens * key_count, width), f32),
            pltpu.VMEM((tokens * key_count, width), f32),
            pltpu.VMEM((tokens * heads, width), f32),
            pltpu.VMEM((heads, 2 * tokens, width), bf16),
            pltpu.VMEM((heads, 1, width), f32),
            pltpu.VMEM((ns, nh, 2 * tokens, width), bf16),
            pltpu.VMEM((ns, nh, tokens, width), bf16),
            pltpu.VMEM((ns, nh, 1, width), f32),
            pltpu.VMEM((ns * nh, tokens, width), bf16),
            pltpu.VMEM((ns, width, width), f32),
            pltpu.VMEM((ns, 2 * width, 2 * width), bf16),
            pltpu.VMEM((ns, 2 * width, width), f32),
            pltpu.VMEM((ns, 1, width), f32),
            pltpu.SemaphoreType.DMA((5,)),
            pltpu.SemaphoreType.DMA((5,)),
            pltpu.SemaphoreType.DMA((ns,)),
            pltpu.SemaphoreType.DMA((ns,)),
            pltpu.SemaphoreType.DMA((2,)),
            pltpu.SemaphoreType.DMA((ns // 2,)),
        ],
        compiler_params=pltpu.CompilerParams(
            collective_id=0, has_side_effects=True, vmem_limit_bytes=60 * 1024 * 1024
        ),
    )(query_heads, key_heads, value_heads, gate_log, beta_rate)


def choose_device(query_heads, key_heads, value_heads, gate_log, beta_rate):
    ns, nh = lax.axis_size("seq"), lax.axis_size("head")
    tokens, heads, width = value_heads.shape
    fits = ns * nh == heads and tokens == 16 and nh * tokens == 128
    fits = fits and width == 128 and key_heads.shape[2] == 128
    fits = fits and heads == 2 * key_heads.shape[1] and ns in (2, 4, 8)
    run = fast_device if fits else per_device
    return run(query_heads, key_heads, value_heads, gate_log, beta_rate)


def solution(mesh):
    return jax.shard_map(
        choose_device,
        mesh=mesh,
        in_specs=(
            P(("seq", "head"), None, None),
            P(("seq", "head"), None, None),
            P(("seq", "head"), None, None),
            P(("seq", "head"), None),
            P(("seq", "head"), None),
        ),
        out_specs=(P(("seq", "head"), None), P("seq", "head", None, None)),
        check_vma=False,
    )
```
